32 devices in a mesh: region: 16 (over z, x, core), slab: 2 (over y).
Axes of the slice: x: 2, y: 2, z: 4, core: 2. Of those that a mesh axis runs over, the one named last changes fastest.
Arguments:
- features: bfloat16 [8192, 96], P(('region', 'slab')), may hold values from -6 to 6
- neighbours: int32 [8192, 27], P(('region', 'slab')), may hold values from 0 to 2304, as said below
- down_map: int32 [2048, 8], P(('region', 'slab')), may hold values from 0 to 256, as said below
- w_conv: bfloat16 [2592, 96], replicated, may hold values from -0.125 to 0.125
- w_down: bfloat16 [768, 128], replicated, may hold values from -0.21875 to 0.21875
- coarse_grad: bfloat16 [2048, 128], P(('region', 'slab')), may hold values from -6 to 6
Outputs:
- coarse: bfloat16 [2048, 128], P(('region', 'slab'))
- grad_input: float32 [8192, 96], P(('region', 'slab'))
- conv_weight_grad: float32 [2592, 96], replicated
- down_weight_grad: float32 [768, 128], replicated
The draws below stay inside these ranges and needn't reach their ends.
Inputs may be any that keep to these rules, and one draw needn't show every extreme that they name: `neighbours`: device d is the device at region index d // (slab axis size) and slab index d mod (slab axis size). Each device's live voxels are its first slots; dead slots list 9 * 256 everywhere and are named by no one. An entry k * 256 + j names slot j of the device whose region index differs by k // 3 - 1 and slab index by k mod 3 - 1; that device exists. A live voxel names itself at offset 13 (k = 4), and otherwise a live voxel or 2304. When k is not 4, j is below 64, the naming voxel lies in its device's first 64 slots, and some voxel names slot 63 of another device in every draw. 9 * 256 means no source. `down_map`: every live voxel of a device is named exactly once, by a coarse voxel slot of that device, by its slot on the device; all other entries are 256.
All inputs are finite; a program needn't handle non-finite values.
Results may differ from the reference program's by a relative error of at most 0.005.
Values may be sent and summed in bfloat16 or wider, within the bound.
No kernel may reach another device: no remote copies, remote signals or barrier semaphores. Data moves between devices by JAX's collectives and lax.ppermute only.
A program may use at most 64 MiB of HBM per device.

```python
import jax
import jax.numpy as jnp
from jax import lax

C = 96
C_OUT = 128
OFFS = 27
DOWN_OFFS = 8
V_DEV = 256
RIM = 64
VC_DEV = 64
NV = 8192
NC = 2048
N_REGION = 16
N_SLAB = 2
DEVICES = 32


def live_counts(key):
    cube = jax.random.randint(jax.random.fold_in(key, 7), (DEVICES,), 0, 65)
    counts = RIM + (V_DEV - RIM) * cube * cube * cube // (64 * 64 * 64)
    fullest = jax.random.randint(jax.random.fold_in(key, 8), (), 0, DEVICES)
    return jnp.where(jnp.arange(DEVICES) == fullest, V_DEV, counts).astype(jnp.int32)


def draw_neighbours(key, part):
    counts = live_counts(key)
    voxel = jnp.arange(NV, dtype=jnp.int32)[:, None]
    device = voxel // V_DEV
    local_idx = voxel % V_DEV
    region = device // N_SLAB
    slab = device % N_SLAB
    offset = jnp.arange(OFFS, dtype=jnp.int32)[None, :]
    step_region = offset // 9 - 1
    step_slab = offset // 3 % 3 - 1
    device_live = counts[device]
    live = local_idx < device_live
    present = jax.random.randint(jax.random.fold_in(key, 11), (NV, OFFS), 0, 5) < 2
    centre = offset == OFFS // 2
    target_region = region + step_region
    target_slab = slab + step_slab
    inside = (target_region >= 0) & (target_region < N_REGION) & (target_slab >= 0) & (target_slab < N_SLAB)
    moving = (step_region != 0) | (step_slab != 0)
    outward_draw = jax.random.randint(jax.random.fold_in(key, 12), (NV, OFFS), 0, 4) == 0
    outward = (local_idx < RIM) & inside & moving & outward_draw
    nearby = jax.random.randint(jax.random.fold_in(key, 13), (NV, OFFS), 0, 1 << 20) % device_live
    remote_slot = jax.random.randint(jax.random.fold_in(key, 14), (NV, OFFS), 0, RIM)
    remote = (target_region * N_SLAB + target_slab) * V_DEV + remote_slot
    value = jnp.where(outward, remote, device * V_DEV + nearby)
    value = jnp.where(centre, voxel, value)
    value = jnp.where(live & (present | centre), value, NV)
    upward = region + 1 < N_REGION
    forced_offset = jnp.where(upward, 21, 3)
    forced_region = jnp.where(upward, region + 1, region - 1)
    forced_target = (forced_region * N_SLAB + slab) * V_DEV + RIM - 1
    value = jnp.where((local_idx == 0) & (offset == forced_offset), forced_target, value)
    target_dev = value // V_DEV
    code = (target_dev // N_SLAB - region + 1) * 3 + (target_dev % N_SLAB - slab + 1)
    encoded = jnp.where(value >= NV, 9 * V_DEV, code * V_DEV + value % V_DEV)
    return encoded.astype(jnp.int32)


def draw_down_map(key, part):
    counts = live_counts(key)
    base = jax.random.fold_in(key, 21)

    def device_map(device):
        order = jax.random.permutation(jax.random.fold_in(base, device), DOWN_OFFS * VC_DEV)
        source = jnp.argsort(order).astype(jnp.int32)
        return jnp.where(source < counts[device], source, V_DEV)
    maps = jax.vmap(device_map)(jnp.arange(DEVICES, dtype=jnp.int32))
    return maps.reshape(NC, DOWN_OFFS).astype(jnp.int32)


def steps_of(own_key, dims, pieces, low, high):
    def one(axis_at, parts):
        steps = jax.random.uniform(jax.random.fold_in(jax.random.fold_in(own_key, 6), axis_at), (parts,), jnp.float32, low / len(pieces), high / len(pieces))
        return jnp.repeat(jnp.exp(steps), dims[axis_at] // parts).reshape((-1,) + (1,) * (len(dims) - axis_at - 1))

    factor_of = one(*pieces[0])
    for cut in pieces[1:]:
        factor_of = factor_of * one(*cut)
    return factor_of


def normal_values(own_key, shape, scale, reach, cuts=(), kind=jnp.bfloat16):
    values = scale * jax.random.normal(own_key, shape, jnp.float32)
    if cuts:
        values = values * steps_of(own_key, shape, cuts, -0.22, 0.18)
    return jnp.clip(values, -reach, reach).astype(kind)


def setup_inputs(seed: int = 0) -> dict:
    keys = jax.random.split(jax.random.key(seed), 7)
    return {
        "features": normal_values(keys[0], (NV, C), 1.0, 6.0, ((0, 32),)),
        "neighbours": draw_neighbours(jax.random.fold_in(keys[6], 71), 0),
        "down_map": draw_down_map(jax.random.fold_in(keys[6], 71), 0),
        "w_conv": normal_values(keys[3], (OFFS * C, C), (OFFS * C) ** -0.5, 0.125),
        "w_down": normal_values(keys[4], (DOWN_OFFS * C, C_OUT), (DOWN_OFFS * C) ** -0.5, 0.21875),
        "coarse_grad": normal_values(keys[5], (NC, C_OUT), 1.0, 6.0, ((0, 32),)),
    }


def reference(features, neighbours, down_map, w_conv, w_down, coarse_grad):
    total, channels = features.shape
    offsets = neighbours.shape[1]
    taps = down_map.shape[1]
    device = (jnp.arange(total, dtype=jnp.int32) // V_DEV)[:, None]
    code = neighbours // V_DEV
    target = device + (code // 3 - 1) * N_SLAB + (code % 3 - 1)
    source = jnp.where(neighbours >= 9 * V_DEV, total, target * V_DEV + neighbours % V_DEV).astype(jnp.int32)
    coarse_dev = (jnp.arange(down_map.shape[0], dtype=jnp.int32) // VC_DEV)[:, None]
    fine = jnp.where(down_map >= V_DEV, total, coarse_dev * V_DEV + down_map).astype(jnp.int32)
    zero_row = jnp.zeros((1, channels), features.dtype)
    table = jnp.concatenate([features, zero_row], axis=0)
    pos_blocks = source.reshape(-1, V_DEV, offsets)

    def conv_block(block_pos):
        rows = table[block_pos].reshape(block_pos.shape[0], offsets * channels)
        return jnp.dot(rows, w_conv, preferred_element_type=jnp.float32)

    conv_out = lax.map(conv_block, pos_blocks).reshape(total, channels)
    hidden = (features.astype(jnp.float32) + jax.nn.silu(conv_out)).astype(jnp.bfloat16)
    hidden_pad = jnp.concatenate([hidden, jnp.zeros((1, channels), hidden.dtype)], axis=0)
    down_blocks = fine.reshape(-1, VC_DEV, taps)
    cotangent_blocks = coarse_grad.reshape(-1, VC_DEV, coarse_grad.shape[1])

    def down_block(carry, inputs):
        hidden_grad, weight_grad = carry
        block_map, block_grad = inputs
        rows = hidden_pad[block_map].reshape(block_map.shape[0], taps * channels)
        result = jnp.dot(rows, w_down, preferred_element_type=jnp.float32).astype(jnp.bfloat16)
        weight_grad = weight_grad + jnp.dot(rows.T, block_grad, preferred_element_type=jnp.float32)
        spread = jnp.dot(block_grad, w_down.T, preferred_element_type=jnp.float32).reshape(-1, channels)
        hidden_grad = hidden_grad.at[block_map.reshape(-1)].add(spread)
        return (hidden_grad, weight_grad), result

    start = (jnp.zeros((total + 1, channels), jnp.float32), jnp.zeros(w_down.shape, jnp.float32))
    (hidden_grad, down_weight_grad), coarse = lax.scan(down_block, start, (down_blocks, cotangent_blocks))
    coarse = coarse.reshape(-1, w_down.shape[1])
    hidden_grad = hidden_grad[:total]
    sigmoid_y = jax.nn.sigmoid(conv_out)
    conv_grad = (hidden_grad * sigmoid_y * (1.0 + conv_out * (1.0 - sigmoid_y))).astype(jnp.bfloat16)
    grad_blocks = conv_grad.reshape(-1, V_DEV, channels)

    def back_block(carry, inputs):
        table_grad, weight_grad = carry
        block_pos, block_grad = inputs
        rows = table[block_pos].reshape(block_pos.shape[0], offsets * channels)
        weight_grad = weight_grad + jnp.dot(rows.T, block_grad, preferred_element_type=jnp.float32)
        spread = jnp.dot(block_grad, w_conv.T, preferred_element_type=jnp.float32).reshape(-1, channels)
        table_grad = table_grad.at[block_pos.reshape(-1)].add(spread)
        return (table_grad, weight_grad), None

    start = (jnp.zeros((total + 1, channels), jnp.float32), jnp.zeros(w_conv.shape, jnp.float32))
    (table_grad, conv_weight_grad), unused = lax.scan(back_block, start, (pos_blocks, grad_blocks))
    grad_input = hidden_grad + table_grad[:total]
    return coarse, grad_input, conv_weight_grad, down_weight_grad
```

```python
import functools

import jax
import jax.numpy as jnp
from jax import lax
from jax.experimental import pallas as pl
from jax.experimental.pallas import tpu as pltpu
from jax.sharding import PartitionSpec as P

AXES = ("region", "slab")
RIM = 64
LANES = 128
F32 = jnp.float32
BF16 = jnp.bfloat16
NN = (((1,), (0,)), ((), ()))
NT = (((1,), (1,)), ((), ()))


def mm(a, b, dims=NN):
    return lax.dot_general(a, b, dims, preferred_element_type=F32)


def halo_sections(slabs):
    if slabs == 2:
        return ((-1, 0), (1, 0), (-1, 1), (0, 1), (1, 1))
    return tuple((dr, ds) for dr in (-1, 0, 1) for ds in (-1, 0, 1) if (dr, ds) != (0, 0))


def halo_pairs(section, regions, slabs):
    dr, ds = section
    pairs = []
    for region in range(regions):
        for slab in range(slabs):
            other = region + dr
            across = (slab + ds) % 2 if slabs == 2 else slab + ds
            if 0 <= other < regions and 0 <= across < slabs:
                pairs.append((other * slabs + across, region * slabs + slab))
    return pairs


def table_rows(neighbours, voxels, slabs):
    code = neighbours // voxels
    slot = neighbours - code * voxels
    row = code // 3
    if slabs == 2:
        section = jnp.where(code - row * 3 != 1, 2 + row, row // 2)
    else:
        section = code - (code > 4)
    rows = jnp.where(code == 4, slot, voxels + section * RIM + slot)
    return jnp.where(code > 8, -1, rows)


def local_kernel(
    offsets, taps, sections, f_ref, rows_ref, down_ref, w_ref, wd_ref, cgrad_ref, *refs
):
    halo_refs = refs[:sections]
    coarse_ref, base_ref, back_ref, conv_w_ref, down_w_ref, rt, drt, drt_far, hot, far, w_pad = refs[sections:]
    voxels, channels = f_ref.shape
    coarse_count = down_ref.shape[0]
    rim_rows = sections * RIM
    feats = f_ref[...]
    feats_t = feats.astype(F32).T
    table_t = feats_t.astype(BF16)
    halo_t = jnp.concatenate([h[...] for h in halo_refs], axis=0).astype(F32).T.astype(BF16)
    near_iota = lax.broadcasted_iota(jnp.int32, (voxels, voxels), 0)
    far_iota = lax.broadcasted_iota(jnp.int32, (rim_rows, LANES), 0) + voxels

    for o in range(offsets):
        row = rows_ref[o : o + 1, :]
        near = jnp.where(near_iota == row, 1.0, 0.0).astype(BF16)
        away = jnp.where(far_iota == row[:, :LANES], 1.0, 0.0).astype(BF16)
        hot[:, o * voxels : (o + 1) * voxels] = near
        far[:, o * LANES : (o + 1) * LANES] = away
        own = mm(table_t, near)
        first = own[:, :LANES] + mm(halo_t, away)
        rt[o * channels : (o + 1) * channels, :LANES] = first.astype(BF16)
        rt[o * channels : (o + 1) * channels, LANES:] = own[:, LANES:].astype(BF16)

    w_t = w_ref[...].astype(F32).T.astype(BF16)
    out_t = mm(w_t, rt[...])
    sig = 1.0 / (1.0 + jnp.exp(-out_t))
    hidden_t = feats_t + out_t * sig
    hidden = hidden_t.T.astype(BF16)
    hidden_tb = hidden_t.astype(BF16)

    cgrad = cgrad_ref[...]
    cgrad_t = cgrad.astype(F32).T.astype(BF16)
    lane_iota = lax.broadcasted_iota(jnp.int32, (coarse_count, voxels), 1)
    coarse = jnp.zeros(cgrad.shape, F32)
    hgrad_t = jnp.zeros((channels, voxels), F32)
    for t in range(taps):
        pick = jnp.where(lane_iota == down_ref[:, t : t + 1], 1.0, 0.0).astype(BF16)
        wd = wd_ref[t * channels : (t + 1) * channels, :]
        coarse += mm(mm(pick, hidden).astype(BF16), wd)
        picked_t = mm(hidden_tb, pick, NT).astype(BF16)
        down_w_ref[t * channels : (t + 1) * channels, :] = mm(picked_t, cgrad).astype(BF16)
        hgrad_t += mm(wd, mm(cgrad_t, pick).astype(BF16))
    coarse_ref[...] = coarse.astype(BF16)

    grad_t = (hgrad_t * sig * (1.0 + out_t * (1.0 - sig))).astype(F32)
    grad = grad_t.T.astype(BF16)
    grad_t = grad_t.astype(BF16)
    conv_w_ref[:, :channels] = mm(rt[...], grad).astype(BF16)
    conv_w_ref[:, channels:] = jnp.zeros((rt.shape[0], LANES - channels), BF16)
    w_pad[:, :channels] = w_ref[...]
    w_pad[:, channels:] = jnp.zeros((rt.shape[0], LANES - channels), BF16)
    grad_pad = jnp.concatenate([grad_t, jnp.zeros((LANES - channels, voxels), BF16)], axis=0)
    for o in range(offsets):
        spread = mm(w_pad[o * channels : (o + 1) * channels, :], grad_pad).astype(BF16)
        drt[:, o * voxels : (o + 1) * voxels] = spread
        drt_far[:, o * LANES : (o + 1) * LANES] = spread[:, :LANES]
    own_t = hgrad_t + mm(drt[...], hot[...], NT)
    back_t = mm(drt_far[...], far[...], NT)
    base_ref[...] = own_t.T
    back_ref[...] = back_t.T.astype(BF16)


def on_device(features, neighbours, down_map, w_conv, w_down, coarse_grad):
    regions, slabs = lax.axis_size("region"), lax.axis_size("slab")
    devices = regions * slabs
    voxels, channels = features.shape
    offsets, taps = neighbours.shape[1], down_map.shape[1]
    wide = w_down.shape[1]
    sections = halo_sections(slabs)
    pairs = [halo_pairs(s, regions, slabs) for s in sections]
    rim = features[:RIM]
    halos = [lax.ppermute(rim, AXES, p) for p in pairs]
    rows = table_rows(neighbours, voxels, slabs).T

    count = len(sections)
    coarse, base, back, conv_w, down_w = pl.pallas_call(
        functools.partial(local_kernel, offsets, taps, count),
        out_shape=(
            jax.ShapeDtypeStruct(coarse_grad.shape, BF16),
            jax.ShapeDtypeStruct((voxels, channels), F32),
            jax.ShapeDtypeStruct((count * RIM, channels), BF16),
            jax.ShapeDtypeStruct((offsets * channels, LANES), BF16),
            jax.ShapeDtypeStruct((taps * channels, wide), BF16),
        ),
        scratch_shapes=[
            pltpu.VMEM((offsets * channels, voxels), BF16),
            pltpu.VMEM((channels, offsets * voxels), BF16),
            pltpu.VMEM((channels, offsets * LANES), BF16),
            pltpu.VMEM((voxels, offsets * voxels), BF16),
            pltpu.VMEM((count * RIM, offsets * LANES), BF16),
            pltpu.VMEM((offsets * channels, LANES), BF16),
        ],
        compiler_params=pltpu.CompilerParams(vmem_limit_bytes=40 * 2**20),
        name="local",
    )(features, rows, down_map, w_conv, w_down, coarse_grad, *halos)

    returned = [
        lax.ppermute(back[i * RIM : (i + 1) * RIM], AXES, [(b, a) for a, b in p])
        for i, p in enumerate(pairs)
    ]

    conv_rows, down_rows = offsets * channels, taps * channels
    piece = -(-(conv_rows + down_rows) // (16 * devices)) * 16
    slack = jnp.zeros((piece * devices - conv_rows - down_rows, LANES), BF16)
    payload = jnp.concatenate([conv_w, down_w, slack], axis=0).reshape(devices, piece, LANES)
    parts = lax.all_to_all(payload, AXES, 0, 0)
    total = jnp.sum(parts.astype(F32), axis=0).astype(BF16)
    full = lax.all_gather(total, AXES, axis=0, tiled=True)
    conv_wgrad = full[:conv_rows, :channels].astype(F32)
    down_wgrad = full[conv_rows : conv_rows + down_rows].astype(F32)

    incoming = sum(r.astype(F32) for r in returned)
    grad_input = base.at[:RIM].add(incoming)
    return coarse, grad_input, conv_wgrad, down_wgrad


def solution(mesh):
    split = P(("region", "slab"), None)
    return jax.shard_map(
        on_device,
        mesh=mesh,
        in_specs=(split, split, split, P(), P(), split),
        out_specs=(split, split, P(), P()),
        check_vma=False,
    )
```

```python
import functools

import jax
import jax.numpy as jnp
from jax import lax
from jax.experimental import pallas as pl
from jax.experimental.pallas import tpu as pltpu
from jax.sharding import Mesh, PartitionSpec as P

SPLIT = ("chips", "core", "slab")
RING = ("chips", "core")
PEERS = ("chips", "slab")
RIM = 64
LANES = 128
TILE = 16
F32 = jnp.float32
BF16 = jnp.bfloat16
NN = (((1,), (0,)), ((), ()))
NT = (((1,), (1,)), ((), ()))
VMEM_BYTES = 40 * 2**20


def mm(a, b, dims=NN):
    return lax.dot_general(a, b, dims, preferred_element_type=F32)


def table_lanes(neighbours, voxels, slabs):
    code = neighbours // voxels
    slot = neighbours - code * voxels
    row = code // 3
    col = code - row * 3
    if slabs == 2:
        rims = 2
        place = jnp.where(col == 1, 0, 1)
        beside = 0
    else:
        rims = 3
        place = col
        beside = col // 2
    rim = jnp.where(row == 1, 2 * rims + beside, (row // 2) * rims + place)
    lane = jnp.where(code == 4, slot, voxels + rim * RIM + slot)
    return jnp.where(code > 8, -1, lane)


def payload_tiles(channels, conv_columns, taps):
    tiles = []
    for column in range(0, conv_columns, LANES):
        for row in range(0, channels, TILE):
            tiles.append((0, row, column, min(LANES, conv_columns - column)))
    for row in range(0, taps * channels, TILE):
        tiles.append((1, row, 0, LANES))
    return tiles


def local_kernel(slabs, core_ref, f_ref, near_ref, down_ref, w_ref, wd_ref, cgrad_ref, *refs):
    halo_refs = refs[:3] if slabs == 2 else refs[:4]
    coarse_ref, base_ref, low_ref, high_ref, side_ref, keep_ref, send_ref = refs[
        len(halo_refs) : len(halo_refs) + 7
    ]
    rt, drt, drt_far, hot, far, w_back, conv_w, down_w = refs[len(halo_refs) + 7 :]
    channels, voxels = f_ref.shape
    offsets = near_ref.shape[0]
    taps, coarse_count = down_ref.shape
    group = low_ref.shape[1]
    rim_lanes = 2 * group + side_ref.shape[1]
    far_rows = far.shape[0]

    table_t = f_ref[...]
    halo = [h[...] for h in halo_refs]
    if far_rows > rim_lanes:
        halo.append(jnp.zeros((channels, far_rows - rim_lanes), BF16))
    halo_t = jnp.concatenate(halo, axis=1)
    lanes = table_lanes(near_ref[...], voxels, slabs)
    near_iota = lax.broadcasted_iota(jnp.int32, (voxels, voxels), 0)
    far_iota = lax.broadcasted_iota(jnp.int32, (far_rows, LANES), 0) + voxels

    for o in range(offsets):
        lane = lanes[o : o + 1, :]
        near = jnp.where(near_iota == lane, 1.0, 0.0).astype(BF16)
        away = jnp.where(far_iota == lane[:, :LANES], 1.0, 0.0).astype(BF16)
        hot[:, o * voxels : (o + 1) * voxels] = near
        far[:, o * LANES : (o + 1) * LANES] = away
        own = mm(table_t, near)
        first = own[:, :LANES] + mm(halo_t, away)
        rt[o * channels : (o + 1) * channels, :LANES] = first.astype(BF16)
        rt[o * channels : (o + 1) * channels, LANES:] = own[:, LANES:].astype(BF16)

    out_t = mm(w_ref[...], rt[...])
    sig = 1.0 / (1.0 + jnp.exp(-out_t))
    hidden_t = (table_t.astype(F32) + out_t * sig).astype(BF16)

    cgrad = cgrad_ref[...]
    cgrad_t = cgrad.astype(F32).T.astype(BF16)
    down = down_ref[...].astype(F32).T
    lane_iota = lax.broadcasted_iota(jnp.int32, (coarse_count, voxels), 1).astype(F32)
    coarse = jnp.zeros(cgrad.shape, F32)
    hgrad_t = jnp.zeros((channels, voxels), F32)
    for t in range(taps):
        pick = jnp.where(lane_iota == down[:, t : t + 1], 1.0, 0.0).astype(BF16)
        wd = wd_ref[t * channels : (t + 1) * channels, :]
        coarse += mm(mm(pick, hidden_t, NT).astype(BF16), wd)
        picked_t = mm(hidden_t, pick, NT).astype(BF16)
        down_w[t * channels : (t + 1) * channels, :] = mm(picked_t, cgrad).astype(BF16)
        hgrad_t += mm(wd, mm(cgrad_t, pick).astype(BF16))
    coarse_ref[...] = coarse.astype(BF16)

    grad_t = (hgrad_t * sig * (1.0 + out_t * (1.0 - sig))).astype(BF16)
    conv_columns = offsets * channels
    conv_w[:, :conv_columns] = mm(grad_t, rt[...], NT).astype(BF16)
    if conv_w.shape[1] > conv_columns:
        slack = conv_w.shape[1] - conv_columns
        conv_w[:, conv_columns:] = jnp.zeros((channels, slack), BF16)

    w_back[:, :channels] = w_ref[...].astype(F32).T.astype(BF16)
    w_back[:, channels:] = jnp.zeros((conv_columns, LANES - channels), BF16)
    grad_pad = jnp.concatenate([grad_t, jnp.zeros((LANES - channels, voxels), BF16)], axis=0)
    for o in range(offsets):
        spread = mm(w_back[o * channels : (o + 1) * channels, :], grad_pad).astype(BF16)
        drt[:, o * voxels : (o + 1) * voxels] = spread
        drt_far[:, o * LANES : (o + 1) * LANES] = spread[:, :LANES]
    base_ref[...] = hgrad_t + mm(drt[...], hot[...], NT)
    back_t = mm(drt_far[...], far[...], NT).astype(BF16)
    low_ref[...] = back_t[:, :group]
    high_ref[...] = back_t[:, group : 2 * group]
    side_ref[...] = back_t[:, 2 * group : rim_lanes]

    tiles = payload_tiles(channels, conv_columns, taps)
    half = keep_ref.shape[0]
    for core in range(2):

        @pl.when(core_ref[0] == core)
        def _(core=core):
            for i in range(2 * half):
                ref = keep_ref if i // half == core else send_ref
                if i < len(tiles):
                    kind, row, column, _ = tiles[i]
                    source = down_w if kind else conv_w
                    ref[i % half] = source[row : row + TILE, column : column + LANES]
                else:
                    ref[i % half] = jnp.zeros((TILE, LANES), BF16)


def unpack_kernel(taps, core_ref, mine_ref, other_ref, conv_ref, down_ref):
    channels, conv_columns = conv_ref.shape
    half = mine_ref.shape[0]
    for core in range(2):

        @pl.when(core_ref[0] == core)
        def _(core=core):
            for i, tile in enumerate(payload_tiles(channels, conv_columns, taps)):
                kind, row, column, columns = tile
                source = mine_ref if i // half == core else other_ref
                value = source[i % half].astype(F32)
                target = down_ref if kind else conv_ref
                target[row : row + TILE, column : column + columns] = value[:, :columns]


def shifts(count, step):
    return [(i, i + step) for i in range(count) if 0 <= i + step < count]


def on_device(features, neighbours, down_map, w_conv, w_down, coarse_grad):
    regions = lax.axis_size("chips") * lax.axis_size("core")
    slabs = lax.axis_size("slab")
    peers = lax.axis_size("chips") * slabs
    voxels, channels = features.shape
    offsets, taps = neighbours.shape[1], down_map.shape[1]
    conv_columns = offsets * channels
    core = lax.axis_index("core").astype(jnp.int32).reshape(1)
    swap = [(0, 1), (1, 0)]
    up, down = shifts(regions, 1), shifts(regions, -1)

    features_t = features.T
    rim = features_t[:, :RIM]
    if slabs == 2:
        side = [lax.ppermute(rim, "slab", swap)]
        row = [rim, side[0]]
    else:
        side = [
            lax.ppermute(rim, "slab", shifts(slabs, 1)),
            lax.ppermute(rim, "slab", shifts(slabs, -1)),
        ]
        row = [side[0], rim, side[1]]
    row = jnp.concatenate(row, axis=1)
    halos = [lax.ppermute(row, RING, up), lax.ppermute(row, RING, down), *side]

    tiles = len(payload_tiles(channels, conv_columns, taps))
    piece = -(-tiles // (2 * peers))
    half = piece * peers
    group, beside = row.shape[1], len(side) * RIM
    far_rows = -(-(2 * group + beside) // LANES) * LANES
    smem = pl.BlockSpec(memory_space=pltpu.SMEM)
    vmem = pl.BlockSpec(memory_space=pltpu.VMEM)
    coarse, base, low, high, own_side, keep, send = pl.pallas_call(
        functools.partial(local_kernel, slabs),
        out_shape=(
            jax.ShapeDtypeStruct(coarse_grad.shape, BF16),
            jax.ShapeDtypeStruct((channels, voxels), F32),
            jax.ShapeDtypeStruct((channels, group), BF16),
            jax.ShapeDtypeStruct((channels, group), BF16),
            jax.ShapeDtypeStruct((channels, beside), BF16),
            jax.ShapeDtypeStruct((half, TILE, LANES), BF16),
            jax.ShapeDtypeStruct((half, TILE, LANES), BF16),
        ),
        in_specs=[smem] + [vmem] * (6 + len(halos)),
        scratch_shapes=[
            pltpu.VMEM((conv_columns, voxels), BF16),
            pltpu.VMEM((channels, offsets * voxels), BF16),
            pltpu.VMEM((channels, offsets * LANES), BF16),
            pltpu.VMEM((voxels, offsets * voxels), BF16),
            pltpu.VMEM((far_rows, offsets * LANES), BF16),
            pltpu.VMEM((conv_columns, LANES), BF16),
            pltpu.VMEM((channels, -(-conv_columns // LANES) * LANES), BF16),
            pltpu.VMEM((taps * channels, LANES), BF16),
        ],
        compiler_params=pltpu.CompilerParams(vmem_limit_bytes=VMEM_BYTES),
        name="local",
    )(core, features_t, neighbours.T, down_map.T, w_conv.T, w_down, coarse_grad, *halos)

    got = lax.ppermute(send, "core", swap)
    pair = (keep.astype(F32) + got.astype(F32)).astype(BF16)
    parts = lax.all_to_all(pair.reshape(peers, piece, TILE, LANES), PEERS, 0, 0)
    total = jnp.sum(parts.astype(F32), axis=0).astype(BF16)
    spread = jnp.broadcast_to(total[None], parts.shape)
    mine = lax.all_to_all(spread, PEERS, 0, 0).reshape(half, TILE, LANES)
    other = lax.ppermute(mine, "core", swap)
    conv_wgrad_t, down_wgrad = pl.pallas_call(
        functools.partial(unpack_kernel, taps),
        out_shape=(
            jax.ShapeDtypeStruct((channels, conv_columns), F32),
            jax.ShapeDtypeStruct((taps * channels, LANES), F32),
        ),
        in_specs=[smem, vmem, vmem],
        compiler_params=pltpu.CompilerParams(vmem_limit_bytes=VMEM_BYTES),
        name="unpack",
    )(core, mine, other)

    row_grad = lax.ppermute(low, RING, down).astype(F32) + lax.ppermute(high, RING, up).astype(F32)
    columns = [row_grad[:, i : i + RIM] for i in range(0, group, RIM)]
    own = [own_side[:, i : i + RIM].astype(F32) for i in range(0, beside, RIM)]
    if slabs == 2:
        incoming = columns[0] + lax.ppermute((columns[1] + own[0]).astype(BF16), "slab", swap)
    else:
        incoming = columns[1]
        incoming += lax.ppermute((columns[0] + own[0]).astype(BF16), "slab", shifts(slabs, -1))
        incoming += lax.ppermute((columns[2] + own[1]).astype(BF16), "slab", shifts(slabs, 1))
    grad_input_t = base.at[:, :RIM].add(incoming)
    return coarse, grad_input_t.T, conv_wgrad_t.T, down_wgrad


def solution(mesh):
    regions, slabs = mesh.shape["region"], mesh.shape["slab"]
    fine = Mesh(mesh.devices.reshape(regions // 2, 2, slabs), SPLIT)
    split = P(SPLIT, None)
    return jax.shard_map(
        on_device,
        mesh=fine,
        in_specs=(split, split, split, P(), P(), split),
        out_specs=(split, split, P(), P()),
        check_vma=False,
    )
```

```python
import functools

import jax
import jax.numpy as jnp
from jax import lax
from jax.experimental import pallas as pl
from jax.experimental.pallas import tpu as pltpu
from jax.sharding import Mesh, PartitionSpec as P

SPLIT = ("far", "near", "core", "slab")
RING = ("far", "near", "core")
AROUND = ("near", "slab")
RIM = 64
LANES = 128
TILE = 16
F32 = jnp.float32
BF16 = jnp.bfloat16
NN = (((1,), (0,)), ((), ()))
NT = (((1,), (1,)), ((), ()))
VMEM_BYTES = 20 * 2**20


def mm(a, b, dims=NN):
    return lax.dot_general(a, b, dims, preferred_element_type=F32)


def table_lanes(neighbours, voxels, slabs):
    code = neighbours // voxels
    slot = neighbours - code * voxels
    row = code // 3
    col = code - row * 3
    if slabs == 2:
        rims = 2
        place = jnp.where(col == 1, 0, 1)
        beside = 0
    else:
        rims = 3
        place = col
        beside = col // 2
    rim = jnp.where(row == 1, 2 * rims + beside, (row // 2) * rims + place)
    lane = jnp.where(code == 4, slot, voxels + rim * RIM + slot)
    return jnp.where(code > 8, -1, lane)


def payload_tiles(channels, conv_columns, taps):
    tiles = []
    for column in range(0, conv_columns, LANES):
        for row in range(0, channels, TILE):
            tiles.append((0, row, column, min(LANES, conv_columns - column)))
    for row in range(0, taps * channels, TILE):
        tiles.append((1, row, 0, LANES))
    return tiles


def padded_halo(halo_refs):
    halo = [h[...] for h in halo_refs]
    width = sum(h.shape[1] for h in halo)
    slack = -width % LANES
    if slack:
        halo.append(jnp.zeros((halo[0].shape[0], slack), BF16))
    return jnp.concatenate(halo, axis=1)


def prepare_kernel(slabs, f_ref, near_ref, down_ref, cgrad_ref, w_ref, wd_ref, *refs):
    first_ref, rest_ref, pick_ref, hgrad_ref, w_out, wd_out = refs
    channels, voxels = f_ref.shape
    offsets = near_ref.shape[0]
    taps, coarse_count = down_ref.shape
    w_out[...] = w_ref[...]
    wd_out[...] = wd_ref[...]
    cgrad_t = cgrad_ref[...].astype(F32).T.astype(BF16)
    down = down_ref[...].astype(F32).T
    lane_iota = lax.broadcasted_iota(jnp.int32, (coarse_count, voxels), 1).astype(F32)
    hgrad_t = jnp.zeros((channels, voxels), F32)
    for t in range(taps):
        pick = jnp.where(lane_iota == down[:, t : t + 1], 1.0, 0.0).astype(BF16)
        pick_ref[t] = pick
        wd = wd_ref[t * channels : (t + 1) * channels, :]
        hgrad_t += mm(wd, mm(cgrad_t, pick).astype(BF16))
    hgrad_ref[...] = hgrad_t
    table_t = f_ref[...]
    lanes = table_lanes(near_ref[...], voxels, slabs)
    near_iota = lax.broadcasted_iota(jnp.int32, (voxels, voxels), 0)
    for o in range(offsets):
        near = jnp.where(near_iota == lanes[o : o + 1, :], 1.0, 0.0).astype(BF16)
        own = mm(table_t, near).astype(BF16)
        first_ref[o * channels : (o + 1) * channels, :] = own[:, :LANES]
        rest_ref[o * channels : (o + 1) * channels, :] = own[:, LANES:]


def forward_kernel(slabs, core_ref, f_ref, near_ref, cgrad_ref, *refs):
    first_ref, rest_ref, pick_ref, hgrad_ref, w_ref, wd_ref = refs[:6]
    halo_refs, refs = (refs[6:9], refs[9:]) if slabs == 2 else (refs[6:10], refs[10:])
    coarse_ref, grad_ref, keep_ref, send_ref, rt, conv_w, down_w = refs
    channels, voxels = f_ref.shape
    offsets = near_ref.shape[0]
    taps = pick_ref.shape[0]
    conv_columns = offsets * channels
    halo_t = padded_halo(halo_refs)
    lanes = table_lanes(near_ref[:, :LANES], voxels, slabs)
    far_iota = lax.broadcasted_iota(jnp.int32, (halo_t.shape[1], LANES), 0) + voxels
    for o in range(offsets):
        rows = slice(o * channels, (o + 1) * channels)
        away = jnp.where(far_iota == lanes[o : o + 1, :], 1.0, 0.0).astype(BF16)
        first = first_ref[rows, :].astype(F32) + mm(halo_t, away)
        rt[rows, :LANES] = first.astype(BF16)
        rt[rows, LANES:] = rest_ref[rows, :]

    out_t = mm(w_ref[...], rt[...])
    sig = 1.0 / (1.0 + jnp.exp(-out_t))
    hidden_t = (f_ref[...].astype(F32) + out_t * sig).astype(BF16)
    grad_t = (hgrad_ref[...] * sig * (1.0 + out_t * (1.0 - sig))).astype(BF16)
    grad_ref[...] = grad_t
    conv_w[:, :conv_columns] = mm(grad_t, rt[...], NT).astype(BF16)
    if conv_w.shape[1] > conv_columns:
        slack = conv_w.shape[1] - conv_columns
        conv_w[:, conv_columns:] = jnp.zeros((channels, slack), BF16)

    cgrad = cgrad_ref[...]
    coarse = jnp.zeros(cgrad.shape, F32)
    for t in range(taps):
        rows = slice(t * channels, (t + 1) * channels)
        pick = pick_ref[t]
        coarse += mm(mm(pick, hidden_t, NT).astype(BF16), wd_ref[rows, :])
        picked_t = mm(hidden_t, pick, NT).astype(BF16)
        down_w[rows, :] = mm(picked_t, cgrad).astype(BF16)
    coarse_ref[...] = coarse.astype(BF16)

    tiles = payload_tiles(channels, conv_columns, taps)
    half = keep_ref.shape[0]
    for core in range(2):

        @pl.when(core_ref[0] == core)
        def _(core=core):
            for i in range(2 * half):
                ref = keep_ref if i // half == core else send_ref
                if i < len(tiles):
                    kind, row, column, _ = tiles[i]
                    source = down_w if kind else conv_w
                    ref[i % half] = source[row : row + TILE, column : column + LANES]
                else:
                    ref[i % half] = jnp.zeros((TILE, LANES), BF16)


def backward_kernel(slabs, near_ref, hgrad_ref, grad_ref, w_ref, *refs):
    base_ref, low_ref, high_ref, side_ref, drt, drt_far, hot, far, w_back = refs
    channels, voxels = hgrad_ref.shape
    offsets = near_ref.shape[0]
    group = low_ref.shape[1]
    lanes = table_lanes(near_ref[...], voxels, slabs)
    near_iota = lax.broadcasted_iota(jnp.int32, (voxels, voxels), 0)
    far_iota = lax.broadcasted_iota(jnp.int32, (far.shape[0], LANES), 0) + voxels
    w_back[:, :channels] = w_ref[...].astype(F32).T.astype(BF16)
    w_back[:, channels:] = jnp.zeros((offsets * channels, LANES - channels), BF16)
    slack = jnp.zeros((LANES - channels, voxels), BF16)
    grad_pad = jnp.concatenate([grad_ref[...], slack], axis=0)
    for o in range(offsets):
        lane = lanes[o : o + 1, :]
        near = jnp.where(near_iota == lane, 1.0, 0.0).astype(BF16)
        away = jnp.where(far_iota == lane[:, :LANES], 1.0, 0.0).astype(BF16)
        hot[:, o * voxels : (o + 1) * voxels] = near
        far[:, o * LANES : (o + 1) * LANES] = away
        spread = mm(w_back[o * channels : (o + 1) * channels, :], grad_pad).astype(BF16)
        drt[:, o * voxels : (o + 1) * voxels] = spread
        drt_far[:, o * LANES : (o + 1) * LANES] = spread[:, :LANES]
    base_ref[...] = hgrad_ref[...] + mm(drt[...], hot[...], NT)
    back_t = mm(drt_far[...], far[...], NT).astype(BF16)
    low_ref[...] = back_t[:, :group]
    high_ref[...] = back_t[:, group : 2 * group]
    side_ref[...] = back_t[:, 2 * group : 2 * group + side_ref.shape[1]]


def final_kernel(taps, core_ref, mine_ref, other_ref, base_ref, *refs):
    conv_ref, down_ref, grad_ref = refs[-3:]
    channels, conv_columns = conv_ref.shape
    half = mine_ref.shape[0]
    total = refs[0][...].astype(F32)
    for ref in refs[1:-3]:
        total += ref[...].astype(F32)
    grad_ref[:, RIM:] = base_ref[:, RIM:]
    grad_ref[:, :RIM] = base_ref[:, :RIM] + total
    for core in range(2):

        @pl.when(core_ref[0] == core)
        def _(core=core):
            for i, tile in enumerate(payload_tiles(channels, conv_columns, taps)):
                kind, row, column, columns = tile
                source = mine_ref if i // half == core else other_ref
                value = source[i % half].astype(F32)
                target = down_ref if kind else conv_ref
                target[row : row + TILE, column : column + columns] = value[:, :columns]


def shifts(count, step):
    return [(i, i + step) for i in range(count) if 0 <= i + step < count]


def on_device(features, neighbours, down_map, w_conv, w_down, coarse_grad):
    regions = lax.axis_size("far") * lax.axis_size("near") * lax.axis_size("core")
    slabs = lax.axis_size("slab")
    around, along = lax.axis_size("near") * slabs, lax.axis_size("far")
    voxels, channels = features.shape
    offsets, taps = neighbours.shape[1], down_map.shape[1]
    conv_columns = offsets * channels
    core = lax.axis_index("core").astype(jnp.int32).reshape(1)
    swap = [(0, 1), (1, 0)]
    up, down = shifts(regions, 1), shifts(regions, -1)

    features_t, neighbours_t, w_conv_t = features.T, neighbours.T, w_conv.T
    rim = features_t[:, :RIM]
    if slabs == 2:
        side = [lax.ppermute(rim, "slab", swap)]
        row = [rim, side[0]]
    else:
        side = [
            lax.ppermute(rim, "slab", shifts(slabs, 1)),
            lax.ppermute(rim, "slab", shifts(slabs, -1)),
        ]
        row = [side[0], rim, side[1]]
    row = jnp.concatenate(row, axis=1)
    halos = [lax.ppermute(row, RING, up), lax.ppermute(row, RING, down), *side]

    tiles = len(payload_tiles(channels, conv_columns, taps))
    piece = -(-tiles // (2 * around * along))
    half = piece * around * along
    group, beside = row.shape[1], len(side) * RIM
    far_rows = -(-(2 * group + beside) // LANES) * LANES
    smem = pl.BlockSpec(memory_space=pltpu.SMEM)
    vmem = pl.BlockSpec(memory_space=pltpu.VMEM)
    params = pltpu.CompilerParams(vmem_limit_bytes=VMEM_BYTES)
    own = pl.pallas_call(
        functools.partial(prepare_kernel, slabs),
        out_shape=(
            jax.ShapeDtypeStruct((conv_columns, LANES), BF16),
            jax.ShapeDtypeStruct((conv_columns, voxels - LANES), BF16),
            jax.ShapeDtypeStruct((taps, down_map.shape[0], voxels), BF16),
            jax.ShapeDtypeStruct((channels, voxels), F32),
            jax.ShapeDtypeStruct((channels, conv_columns), BF16),
            jax.ShapeDtypeStruct(w_down.shape, BF16),
        ),
        compiler_params=params,
        cost_estimate=pl.CostEstimate(flops=2 * 10**9, bytes_accessed=10**7, transcendentals=0),
        name="prepare",
    )(features_t, neighbours_t, down_map.T, coarse_grad, w_conv_t, w_down)
    hgrad, w_near = own[3], own[4]
    coarse, grad, keep, send = pl.pallas_call(
        functools.partial(forward_kernel, slabs),
        out_shape=(
            jax.ShapeDtypeStruct(coarse_grad.shape, BF16),
            jax.ShapeDtypeStruct((channels, voxels), BF16),
            jax.ShapeDtypeStruct((half, TILE, LANES), BF16),
            jax.ShapeDtypeStruct((half, TILE, LANES), BF16),
        ),
        in_specs=[smem] + [vmem] * (9 + len(halos)),
        scratch_shapes=[
            pltpu.VMEM((conv_columns, voxels), BF16),
            pltpu.VMEM((channels, -(-conv_columns // LANES) * LANES), BF16),
            pltpu.VMEM((taps * channels, LANES), BF16),
        ],
        compiler_params=params,
        name="forward",
    )(core, features_t, neighbours_t, coarse_grad, *own, *halos)
    got = lax.ppermute(send, "core", swap)
    pair = (keep.astype(F32) + got.astype(F32)).astype(BF16)
    pair, grad = lax.optimization_barrier((pair, grad))

    base, low, high, own_side = pl.pallas_call(
        functools.partial(backward_kernel, slabs),
        out_shape=(
            jax.ShapeDtypeStruct((channels, voxels), F32),
            jax.ShapeDtypeStruct((channels, group), BF16),
            jax.ShapeDtypeStruct((channels, group), BF16),
            jax.ShapeDtypeStruct((channels, beside), BF16),
        ),
        scratch_shapes=[
            pltpu.VMEM((channels, offsets * voxels), BF16),
            pltpu.VMEM((channels, offsets * LANES), BF16),
            pltpu.VMEM((voxels, offsets * voxels), BF16),
            pltpu.VMEM((far_rows, offsets * LANES), BF16),
            pltpu.VMEM((conv_columns, LANES), BF16),
        ],
        compiler_params=params,
        cost_estimate=pl.CostEstimate(flops=3 * 10**9, bytes_accessed=10**7, transcendentals=0),
        name="backward",
    )(neighbours_t, hgrad, grad, w_near)

    parts = lax.all_to_all(pair.reshape(around, along * piece, TILE, LANES), AROUND, 0, 0)
    parts, low, high, own_side, base = lax.optimization_barrier((parts, low, high, own_side, base))
    square = jnp.sum(parts.astype(F32), axis=0).astype(BF16)
    parts = lax.all_to_all(square.reshape(along, piece, TILE, LANES), "far", 0, 0)
    low, high = lax.ppermute(low, RING, down), lax.ppermute(high, RING, up)
    parts, low, high = lax.optimization_barrier((parts, low, high))
    total = jnp.sum(parts.astype(F32), axis=0).astype(BF16)
    total = jnp.broadcast_to(total[None], parts.shape)
    square = lax.all_to_all(total, "far", 0, 0).reshape(1, along * piece, TILE, LANES)
    row_grad = low.astype(F32) + high.astype(F32)
    columns = [row_grad[:, i : i + RIM] for i in range(0, group, RIM)]
    own = [own_side[:, i : i + RIM].astype(F32) for i in range(0, beside, RIM)]
    if slabs == 2:
        crossing = [(columns[1] + own[0]).astype(BF16)]
        crossing = [lax.ppermute(crossing[0], "slab", swap)]
        here = columns[0]
    else:
        crossing = [(columns[0] + own[0]).astype(BF16), (columns[2] + own[1]).astype(BF16)]
        crossing[0] = lax.ppermute(crossing[0], "slab", shifts(slabs, -1))
        crossing[1] = lax.ppermute(crossing[1], "slab", shifts(slabs, 1))
        here = columns[1]
    square = jnp.broadcast_to(square, (around,) + square.shape[1:])
    mine = lax.all_to_all(square, AROUND, 0, 0).reshape(half, TILE, LANES)
    mine, crossing, here = lax.optimization_barrier((mine, crossing, here))
    other = lax.ppermute(mine, "core", swap)
    conv_wgrad_t, down_wgrad, grad_input_t = pl.pallas_call(
        functools.partial(final_kernel, taps),
        out_shape=(
            jax.ShapeDtypeStruct((channels, conv_columns), F32),
            jax.ShapeDtypeStruct((taps * channels, LANES), F32),
            jax.ShapeDtypeStruct((channels, voxels), F32),
        ),
        in_specs=[smem] + [vmem] * (4 + len(crossing)),
        compiler_params=params,
        name="final",
    )(core, mine, other, base, here, *crossing)
    return coarse, grad_input_t.T, conv_wgrad_t.T, down_wgrad


def solution(mesh):
    regions, slabs = mesh.shape["region"], mesh.shape["slab"]
    fine = Mesh(mesh.devices.reshape(regions // 4, 2, 2, slabs), SPLIT)
    split = P(SPLIT, None)
    return jax.shard_map(
        on_device,
        mesh=fine,
        in_specs=(split, split, split, P(), P(), split),
        out_specs=(split, split, P(), P()),
        check_vma=False,
    )
```

```python
import functools

import jax
import jax.numpy as jnp
from jax import lax
from jax.experimental import pallas as pl
from jax.experimental.pallas import tpu as pltpu
from jax.sharding import Mesh, PartitionSpec as P

SPLIT = ("far", "near", "core", "slab")
RING = ("far", "near", "core")
AROUND = ("near", "slab")
RIM = 64
LANES = 128
TILE = 16
F32 = jnp.float32
BF16 = jnp.bfloat16
NN = (((1,), (0,)), ((), ()))
NT = (((1,), (1,)), ((), ()))
VMEM_BYTES = 20 * 2**20


def mm(a, b, dims=NN):
    return lax.dot_general(a, b, dims, preferred_element_type=F32)


def table_lanes(neighbours, voxels, slabs):
    code = neighbours // voxels
    slot = neighbours - code * voxels
    row = code // 3
    col = code - row * 3
    if slabs == 2:
        rims = 2
        place = jnp.where(col == 1, 0, 1)
        beside = 0
    else:
        rims = 3
        place = col
        beside = col // 2
    rim = jnp.where(row == 1, 2 * rims + beside, (row // 2) * rims + place)
    lane = jnp.where(code == 4, slot, voxels + rim * RIM + slot)
    return jnp.where(code > 8, -1, lane)


def payload_tiles(channels, conv_columns, taps):
    tiles = []
    for column in range(0, conv_columns, LANES):
        for row in range(0, channels, TILE):
            tiles.append((0, row, column, min(LANES, conv_columns - column)))
    for row in range(0, taps * channels, TILE):
        tiles.append((1, row, 0, LANES))
    return tiles


def padded_halo(halo_refs):
    halo = [h[...] for h in halo_refs]
    width = sum(h.shape[1] for h in halo)
    slack = -width % LANES
    if slack:
        halo.append(jnp.zeros((halo[0].shape[0], slack), BF16))
    return jnp.concatenate(halo, axis=1)


def prepare_kernel(
    slabs, f_ref, near_ref, down_ref, cgrad_ref, wd_ref, first_ref, rest_ref, pick_ref, hgrad_ref
):
    channels, voxels = f_ref.shape
    offsets = near_ref.shape[0]
    taps, coarse_count = down_ref.shape
    cgrad_t = cgrad_ref[...].astype(F32).T.astype(BF16)
    down = down_ref[...].astype(F32).T
    lane_iota = lax.broadcasted_iota(jnp.int32, (coarse_count, voxels), 1).astype(F32)
    hgrad_t = jnp.zeros((channels, voxels), F32)
    for t in range(taps):
        pick = jnp.where(lane_iota == down[:, t : t + 1], 1.0, 0.0).astype(BF16)
        pick_ref[t] = pick
        wd = wd_ref[t * channels : (t + 1) * channels, :]
        hgrad_t += mm(wd, mm(cgrad_t, pick).astype(BF16))
    hgrad_ref[...] = hgrad_t
    table_t = f_ref[...]
    lanes = table_lanes(near_ref[...], voxels, slabs)
    near_iota = lax.broadcasted_iota(jnp.int32, (voxels, voxels), 0)
    for o in range(offsets):
        near = jnp.where(near_iota == lanes[o : o + 1, :], 1.0, 0.0).astype(BF16)
        own = mm(table_t, near).astype(BF16)
        first_ref[o * channels : (o + 1) * channels, :] = own[:, :LANES]
        rest_ref[o * channels : (o + 1) * channels, :] = own[:, LANES:]


def forward_kernel(slabs, core_ref, f_ref, near_ref, cgrad_ref, w_ref, wd_ref, *refs):
    first_ref, rest_ref, pick_ref, hgrad_ref = refs[:4]
    halo_refs, refs = (refs[4:7], refs[7:]) if slabs == 2 else (refs[4:8], refs[8:])
    coarse_ref, grad_ref, keep_ref, send_ref, rt, conv_w, down_w = refs
    channels, voxels = f_ref.shape
    offsets = near_ref.shape[0]
    taps = pick_ref.shape[0]
    conv_columns = offsets * channels
    halo_t = padded_halo(halo_refs)
    lanes = table_lanes(near_ref[:, :LANES], voxels, slabs)
    far_iota = lax.broadcasted_iota(jnp.int32, (halo_t.shape[1], LANES), 0) + voxels
    for o in range(offsets):
        rows = slice(o * channels, (o + 1) * channels)
        away = jnp.where(far_iota == lanes[o : o + 1, :], 1.0, 0.0).astype(BF16)
        first = first_ref[rows, :].astype(F32) + mm(halo_t, away)
        rt[rows, :LANES] = first.astype(BF16)
        rt[rows, LANES:] = rest_ref[rows, :]

    out_t = mm(w_ref[...], rt[...])
    sig = 1.0 / (1.0 + jnp.exp(-out_t))
    hidden_t = (f_ref[...].astype(F32) + out_t * sig).astype(BF16)
    grad_t = (hgrad_ref[...] * sig * (1.0 + out_t * (1.0 - sig))).astype(BF16)
    grad_ref[...] = grad_t
    conv_w[:, :conv_columns] = mm(grad_t, rt[...], NT)
    if conv_w.shape[1] > conv_columns:
        slack = conv_w.shape[1] - conv_columns
        conv_w[:, conv_columns:] = jnp.zeros((channels, slack), F32)

    cgrad = cgrad_ref[...]
    coarse = jnp.zeros(cgrad.shape, F32)
    for t in range(taps):
        rows = slice(t * channels, (t + 1) * channels)
        pick = pick_ref[t]
        coarse += mm(mm(pick, hidden_t, NT).astype(BF16), wd_ref[rows, :])
        picked_t = mm(hidden_t, pick, NT).astype(BF16)
        down_w[rows, :] = mm(picked_t, cgrad)
    coarse_ref[...] = coarse.astype(BF16)

    tiles = payload_tiles(channels, conv_columns, taps)
    half = keep_ref.shape[0]
    for core in range(2):

        @pl.when(core_ref[0] == core)
        def _(core=core):
            for i in range(2 * half):
                ref = keep_ref if i // half == core else send_ref
                if i < len(tiles):
                    kind, row, column, _ = tiles[i]
                    source = down_w if kind else conv_w
                    value = source[row : row + TILE, column : column + LANES]
                else:
                    value = jnp.zeros((TILE, LANES), F32)
                ref[i % half] = value.astype(ref.dtype)


def backward_kernel(slabs, near_ref, hgrad_ref, grad_ref, w_ref, *refs):
    base_ref, low_ref, high_ref, side_ref, drt, drt_far, hot, far, w_back = refs
    channels, voxels = hgrad_ref.shape
    offsets = near_ref.shape[0]
    group = low_ref.shape[1]
    lanes = table_lanes(near_ref[...], voxels, slabs)
    near_iota = lax.broadcasted_iota(jnp.int32, (voxels, voxels), 0)
    far_iota = lax.broadcasted_iota(jnp.int32, (far.shape[0], LANES), 0) + voxels
    w_back[:, :channels] = w_ref[...].astype(F32).T.astype(BF16)
    w_back[:, channels:] = jnp.zeros((offsets * channels, LANES - channels), BF16)
    slack = jnp.zeros((LANES - channels, voxels), BF16)
    grad_pad = jnp.concatenate([grad_ref[...], slack], axis=0)
    for o in range(offsets):
        lane = lanes[o : o + 1, :]
        near = jnp.where(near_iota == lane, 1.0, 0.0).astype(BF16)
        away = jnp.where(far_iota == lane[:, :LANES], 1.0, 0.0).astype(BF16)
        hot[:, o * voxels : (o + 1) * voxels] = near
        far[:, o * LANES : (o + 1) * LANES] = away
        spread = mm(w_back[o * channels : (o + 1) * channels, :], grad_pad).astype(BF16)
        drt[:, o * voxels : (o + 1) * voxels] = spread
        drt_far[:, o * LANES : (o + 1) * LANES] = spread[:, :LANES]
    base_ref[...] = hgrad_ref[...] + mm(drt[...], hot[...], NT)
    back_t = mm(drt_far[...], far[...], NT).astype(BF16)
    low_ref[...] = back_t[:, :group]
    high_ref[...] = back_t[:, group : 2 * group]
    side_ref[...] = back_t[:, 2 * group : 2 * group + side_ref.shape[1]]


def partner(index, step, count):
    if count & (count - 1):
        return (index + step) % count
    return index ^ step


def steps(axis_sizes, step):
    count = functools.reduce(lambda a, b: a * b, axis_sizes)
    return [(i, partner(i, step, count)) for i in range(count)]


def split_kernel(count, received, index_ref, own_ref, *refs):
    parts, pieces = refs[:received], refs[received:]
    length = own_ref.shape[0] // count
    for step in range(count):
        chosen = partner(index_ref[0], step, count)
        rows = pl.ds(chosen * length, length)
        value = own_ref[rows].astype(F32)
        for part in parts:
            value += part[rows].astype(F32)
        pieces[step][...] = value.astype(pieces[step].dtype)


def join_kernel(count, index_ref, *refs):
    pieces, full_ref = refs[:count], refs[count]
    length = pieces[0].shape[0]
    for step in range(count):
        chosen = partner(index_ref[0], step, count)
        full_ref[pl.ds(chosen * length, length)] = pieces[step][...]


def final_kernel(taps, core_ref, mine_ref, other_ref, base_ref, *refs):
    conv_ref, down_ref, grad_ref = refs[-3:]
    channels, conv_columns = conv_ref.shape
    half = mine_ref.shape[0]
    total = refs[0][...].astype(F32)
    for ref in refs[1:-3]:
        total += ref[...].astype(F32)
    grad_ref[:, RIM:] = base_ref[:, RIM:]
    grad_ref[:, :RIM] = base_ref[:, :RIM] + total
    for core in range(2):

        @pl.when(core_ref[0] == core)
        def _(core=core):
            for i, tile in enumerate(payload_tiles(channels, conv_columns, taps)):
                kind, row, column, columns = tile
                source = mine_ref if i // half == core else other_ref
                value = source[i % half].astype(F32)
                target = down_ref if kind else conv_ref
                target[row : row + TILE, column : column + columns] = value[:, :columns]


def shifts(count, step):
    return [(i, i + step) for i in range(count) if 0 <= i + step < count]


def on_device(features, neighbours, down_map, w_conv, w_down, coarse_grad):
    regions = lax.axis_size("far") * lax.axis_size("near") * lax.axis_size("core")
    slabs = lax.axis_size("slab")
    around, along = lax.axis_size("near") * slabs, lax.axis_size("far")
    voxels, channels = features.shape
    offsets, taps = neighbours.shape[1], down_map.shape[1]
    conv_columns = offsets * channels
    core = lax.axis_index("core").astype(jnp.int32).reshape(1)
    swap = [(0, 1), (1, 0)]
    up, down = shifts(regions, 1), shifts(regions, -1)

    features_t, neighbours_t, w_conv_t = features.T, neighbours.T, w_conv.T
    smem = pl.BlockSpec(memory_space=pltpu.SMEM)
    vmem = pl.BlockSpec(memory_space=pltpu.VMEM)
    params = pltpu.CompilerParams(vmem_limit_bytes=VMEM_BYTES)
    down_t = down_map.T
    rim = features_t[:, :RIM]
    if slabs == 2:
        side = [lax.ppermute(rim, "slab", swap)]
    else:
        side = [
            lax.ppermute(rim, "slab", shifts(slabs, 1)),
            lax.ppermute(rim, "slab", shifts(slabs, -1)),
        ]
    own = pl.pallas_call(
        functools.partial(prepare_kernel, slabs),
        out_shape=(
            jax.ShapeDtypeStruct((conv_columns, LANES), BF16),
            jax.ShapeDtypeStruct((conv_columns, voxels - LANES), BF16),
            jax.ShapeDtypeStruct((taps, coarse_grad.shape[0], voxels), BF16),
            jax.ShapeDtypeStruct((channels, voxels), F32),
        ),
        compiler_params=params,
        cost_estimate=pl.CostEstimate(flops=2 * 10**9, bytes_accessed=10**7, transcendentals=0),
        name="prepare",
    )(features_t, neighbours_t, down_t, coarse_grad, w_down)
    side, own = lax.optimization_barrier((side, own))
    row = [rim, side[0]] if slabs == 2 else [side[0], rim, side[1]]
    row = jnp.concatenate(row, axis=1)
    halos = [lax.ppermute(row, RING, up), lax.ppermute(row, RING, down), *side]

    tiles = len(payload_tiles(channels, conv_columns, taps))
    piece = -(-tiles // (2 * around * along))
    half = piece * around * along
    group, beside = row.shape[1], len(side) * RIM
    far_rows = -(-(2 * group + beside) // LANES) * LANES
    hgrad = own[3]
    coarse, grad, keep, send = pl.pallas_call(
        functools.partial(forward_kernel, slabs),
        out_shape=(
            jax.ShapeDtypeStruct(coarse_grad.shape, BF16),
            jax.ShapeDtypeStruct((channels, voxels), BF16),
            jax.ShapeDtypeStruct((half, TILE, LANES), F32),
            jax.ShapeDtypeStruct((half, TILE, LANES), BF16),
        ),
        in_specs=[smem] + [vmem] * (9 + len(halos)),
        scratch_shapes=[
            pltpu.VMEM((conv_columns, voxels), BF16),
            pltpu.VMEM((channels, -(-conv_columns // LANES) * LANES), F32),
            pltpu.VMEM((taps * channels, LANES), F32),
        ],
        compiler_params=params,
        name="forward",
    )(core, features_t, neighbours_t, coarse_grad, w_conv_t, w_down, *own, *halos)
    got = lax.ppermute(send, "core", swap)
    ring = (lax.axis_size("near"), slabs)
    line = (along,)
    here = lax.axis_index(AROUND).astype(jnp.int32).reshape(1)
    place = lax.axis_index("far").astype(jnp.int32).reshape(1)

    def split(name, index, count, own, received):
        shape = (own.shape[0] // count, TILE, LANES)
        return pl.pallas_call(
            functools.partial(split_kernel, count, len(received)),
            out_shape=[jax.ShapeDtypeStruct(shape, F32 if i == 0 else BF16) for i in range(count)],
            in_specs=[smem] + [vmem] * (1 + len(received)),
            compiler_params=params,
            name=name,
        )(index, own, *received)

    def join(name, index, pieces):
        count = len(pieces)
        shape = (pieces[0].shape[0] * count, TILE, LANES)
        return pl.pallas_call(
            functools.partial(join_kernel, count),
            out_shape=jax.ShapeDtypeStruct(shape, BF16),
            in_specs=[smem] + [vmem] * count,
            compiler_params=params,
            name=name,
        )(index, *pieces)

    square, *sent = split("split_pair", here, around, keep, [got])
    square, sent, grad = lax.optimization_barrier((square, sent, grad))
    sent = [lax.ppermute(x, AROUND, steps(ring, i + 1)) for i, x in enumerate(sent)]

    base, low, high, own_side = pl.pallas_call(
        functools.partial(backward_kernel, slabs),
        out_shape=(
            jax.ShapeDtypeStruct((channels, voxels), F32),
            jax.ShapeDtypeStruct((channels, group), BF16),
            jax.ShapeDtypeStruct((channels, group), BF16),
            jax.ShapeDtypeStruct((channels, beside), BF16),
        ),
        scratch_shapes=[
            pltpu.VMEM((channels, offsets * voxels), BF16),
            pltpu.VMEM((channels, offsets * LANES), BF16),
            pltpu.VMEM((voxels, offsets * voxels), BF16),
            pltpu.VMEM((far_rows, offsets * LANES), BF16),
            pltpu.VMEM((conv_columns, LANES), BF16),
        ],
        compiler_params=params,
        cost_estimate=pl.CostEstimate(flops=3 * 10**9, bytes_accessed=10**7, transcendentals=0),
        name="backward",
    )(neighbours_t, hgrad, grad, w_conv_t)

    sent, low, high, own_side, base = lax.optimization_barrier((sent, low, high, own_side, base))
    piece, *sent = split("split_square", place, along, square, sent)
    sent = [lax.ppermute(x, "far", steps(line, i + 1)) for i, x in enumerate(sent)]
    total = piece + sum(x.astype(F32) for x in sent)
    total = total.astype(BF16)
    pieces = [total] + [lax.ppermute(total, "far", steps(line, i)) for i in range(1, along)]
    square = join("join_square", place, pieces)
    square, low, high = lax.optimization_barrier((square, low, high))
    pieces = [square] + [lax.ppermute(square, AROUND, steps(ring, i)) for i in range(1, around)]
    low, high = lax.ppermute(low, RING, down), lax.ppermute(high, RING, up)
    pieces, low, high = lax.optimization_barrier((pieces, low, high))
    mine = join("join_half", here, pieces)
    row_grad = low.astype(F32) + high.astype(F32)
    columns = [row_grad[:, i : i + RIM] for i in range(0, group, RIM)]
    own = [own_side[:, i : i + RIM].astype(F32) for i in range(0, beside, RIM)]
    if slabs == 2:
        crossing = [(columns[1] + own[0]).astype(BF16)]
        crossing = [lax.ppermute(crossing[0], "slab", swap)]
        home = columns[0]
    else:
        crossing = [(columns[0] + own[0]).astype(BF16), (columns[2] + own[1]).astype(BF16)]
        crossing[0] = lax.ppermute(crossing[0], "slab", shifts(slabs, -1))
        crossing[1] = lax.ppermute(crossing[1], "slab", shifts(slabs, 1))
        home = columns[1]
    other = lax.ppermute(mine, "core", swap)
    conv_wgrad_t, down_wgrad, grad_input_t = pl.pallas_call(
        functools.partial(final_kernel, taps),
        out_shape=(
            jax.ShapeDtypeStruct((channels, conv_columns), F32),
            jax.ShapeDtypeStruct((taps * channels, LANES), F32),
            jax.ShapeDtypeStruct((channels, voxels), F32),
        ),
        in_specs=[smem] + [vmem] * (4 + len(crossing)),
        compiler_params=params,
        name="final",
    )(core, mine, other, base, home, *crossing)
    return coarse, grad_input_t.T, conv_wgrad_t.T, down_wgrad


def solution(mesh):
    regions, slabs = mesh.shape["region"], mesh.shape["slab"]
    fine = Mesh(mesh.devices.reshape(regions // 4, 2, 2, slabs), SPLIT)
    split = P(SPLIT, None)
    return jax.shard_map(
        on_device,
        mesh=fine,
        in_specs=(split, split, split, P(), P(), split),
        out_specs=(split, split, P(), P()),
        check_vma=False,
    )
```

```python
import functools

import jax
import jax.numpy as jnp
from jax import lax
from jax.experimental import pallas as pl
from jax.experimental.pallas import tpu as pltpu
from jax.sharding import Mesh, PartitionSpec as P

SPLIT = ("far", "near", "core", "slab")
RING = ("far", "near", "core")
RIM = 64
LANES = 128
TILE = 16
F32 = jnp.float32
BF16 = jnp.bfloat16
NN = (((1,), (0,)), ((), ()))
NT = (((1,), (1,)), ((), ()))
VMEM_BYTES = 20 * 2**20


def mm(a, b, dims=NN):
    return lax.dot_general(a, b, dims, preferred_element_type=F32)


def table_lanes(neighbours, voxels, slabs, core):
    code = neighbours // voxels
    slot = neighbours - code * voxels
    row = code // 3
    col = code - row * 3
    if slabs == 2:
        rims = 2
        place = jnp.where(col == 1, 0, 1)
        beside = 0
    else:
        rims = 3
        place = col
        beside = col // 2
    group = jnp.abs(row // 2 + core - 1)
    rim = jnp.where(row == 1, 2 * rims + beside, group * rims + place)
    lane = jnp.where(code == 4, slot, voxels + rim * RIM + slot)
    return jnp.where(code > 8, -1, lane)


def payload_tiles(channels, conv_columns, taps):
    tiles = []
    for column in range(0, conv_columns, LANES):
        for row in range(0, channels, TILE):
            tiles.append((0, row, column, min(LANES, conv_columns - column)))
    for row in range(0, taps * channels, TILE):
        tiles.append((1, row, 0, LANES))
    return tiles


def padded_halo(halo_refs):
    halo = [h[...] for h in halo_refs]
    width = sum(h.shape[1] for h in halo)
    slack = -width % LANES
    if slack:
        halo.append(jnp.zeros((halo[0].shape[0], slack), BF16))
    return jnp.concatenate(halo, axis=1)


def gather_kernel(slabs, f_ref, near_ref, first_ref, rest_ref):
    channels, voxels = f_ref.shape
    table_t = f_ref[...]
    lanes = table_lanes(near_ref[...], voxels, slabs, 0)
    near_iota = lax.broadcasted_iota(jnp.int32, (voxels, voxels), 0)
    for o in range(near_ref.shape[0]):
        near = jnp.where(near_iota == lanes[o : o + 1, :], 1.0, 0.0).astype(BF16)
        own = mm(table_t, near).astype(BF16)
        first_ref[o * channels : (o + 1) * channels, :] = own[:, :LANES]
        rest_ref[o * channels : (o + 1) * channels, :] = own[:, LANES:]


def taps_kernel(down_ref, cgrad_ref, wd_ref, pick_ref, hgrad_ref):
    channels, voxels = hgrad_ref.shape
    taps, coarse_count = down_ref.shape
    cgrad_t = cgrad_ref[...].astype(F32).T.astype(BF16)
    down = down_ref[...].astype(F32).T
    lane_iota = lax.broadcasted_iota(jnp.int32, (coarse_count, voxels), 1).astype(F32)
    hgrad_t = jnp.zeros((channels, voxels), F32)
    for t in range(taps):
        pick = jnp.where(lane_iota == down[:, t : t + 1], 1.0, 0.0).astype(BF16)
        pick_ref[t] = pick
        wd = wd_ref[t * channels : (t + 1) * channels, :]
        hgrad_t += mm(wd, mm(cgrad_t, pick).astype(BF16))
    hgrad_ref[...] = hgrad_t


def forward_kernel(slabs, core_ref, f_ref, near_ref, cgrad_ref, w_ref, wd_ref, *refs):
    first_ref, rest_ref, pick_ref, hgrad_ref = refs[:4]
    halo_refs, refs = (refs[4:7], refs[7:]) if slabs == 2 else (refs[4:8], refs[8:])
    coarse_ref, grad_ref, keep_ref, send_ref, rt, conv_w, down_w = refs
    channels, voxels = f_ref.shape
    offsets = near_ref.shape[0]
    taps = pick_ref.shape[0]
    conv_columns = offsets * channels
    halo_t = padded_halo(halo_refs)
    lanes = table_lanes(near_ref[:, :LANES], voxels, slabs, core_ref[0])
    far_iota = lax.broadcasted_iota(jnp.int32, (halo_t.shape[1], LANES), 0) + voxels
    for o in range(offsets):
        rows = slice(o * channels, (o + 1) * channels)
        away = jnp.where(far_iota == lanes[o : o + 1, :], 1.0, 0.0).astype(BF16)
        first = first_ref[rows, :].astype(F32) + mm(halo_t, away)
        rt[rows, :LANES] = first.astype(BF16)
        rt[rows, LANES:] = rest_ref[rows, :]

    out_t = mm(w_ref[...], rt[...])
    sig = 1.0 / (1.0 + jnp.exp(-out_t))
    hidden_t = (f_ref[...].astype(F32) + out_t * sig).astype(BF16)
    grad_t = (hgrad_ref[...] * sig * (1.0 + out_t * (1.0 - sig))).astype(BF16)
    grad_ref[...] = grad_t
    conv_w[:, :conv_columns] = mm(grad_t, rt[...], NT)
    if conv_w.shape[1] > conv_columns:
        slack = conv_w.shape[1] - conv_columns
        conv_w[:, conv_columns:] = jnp.zeros((channels, slack), F32)

    cgrad = cgrad_ref[...]
    coarse = jnp.zeros(cgrad.shape, F32)
    for t in range(taps):
        rows = slice(t * channels, (t + 1) * channels)
        pick = pick_ref[t]
        coarse += mm(mm(pick, hidden_t, NT).astype(BF16), wd_ref[rows, :])
        picked_t = mm(hidden_t, pick, NT).astype(BF16)
        down_w[rows, :] = mm(picked_t, cgrad)
    coarse_ref[...] = coarse.astype(BF16)

    tiles = payload_tiles(channels, conv_columns, taps)
    half = keep_ref.shape[0]
    for core in range(2):

        @pl.when(core_ref[0] == core)
        def _(core=core):
            for i in range(2 * half):
                ref = keep_ref if i // half == core else send_ref
                if i < len(tiles):
                    kind, row, column, _ = tiles[i]
                    source = down_w if kind else conv_w
                    value = source[row : row + TILE, column : column + LANES]
                else:
                    value = jnp.zeros((TILE, LANES), F32)
                ref[i % half] = value.astype(ref.dtype)


def backward_kernel(slabs, core_ref, near_ref, hgrad_ref, grad_ref, w_ref, *refs):
    base_ref, mate_ref, cross_ref, side_ref, drt, drt_far, hot, far, w_back = refs
    channels, voxels = hgrad_ref.shape
    offsets = near_ref.shape[0]
    group = mate_ref.shape[1]
    lanes = table_lanes(near_ref[...], voxels, slabs, core_ref[0])
    near_iota = lax.broadcasted_iota(jnp.int32, (voxels, voxels), 0)
    far_iota = lax.broadcasted_iota(jnp.int32, (far.shape[0], LANES), 0) + voxels
    w_back[:, :channels] = w_ref[...].astype(F32).T.astype(BF16)
    w_back[:, channels:] = jnp.zeros((offsets * channels, LANES - channels), BF16)
    slack = jnp.zeros((LANES - channels, voxels), BF16)
    grad_pad = jnp.concatenate([grad_ref[...], slack], axis=0)
    for o in range(offsets):
        lane = lanes[o : o + 1, :]
        near = jnp.where(near_iota == lane, 1.0, 0.0).astype(BF16)
        away = jnp.where(far_iota == lane[:, :LANES], 1.0, 0.0).astype(BF16)
        hot[:, o * voxels : (o + 1) * voxels] = near
        far[:, o * LANES : (o + 1) * LANES] = away
        spread = mm(w_back[o * channels : (o + 1) * channels, :], grad_pad).astype(BF16)
        drt[:, o * voxels : (o + 1) * voxels] = spread
        drt_far[:, o * LANES : (o + 1) * LANES] = spread[:, :LANES]
    base_ref[...] = hgrad_ref[...] + mm(drt[...], hot[...], NT)
    back_t = mm(drt_far[...], far[...], NT).astype(BF16)
    mate_ref[...] = back_t[:, :group]
    cross_ref[...] = back_t[:, group : 2 * group]
    side_ref[...] = back_t[:, 2 * group : 2 * group + side_ref.shape[1]]


def fold_kernel(bit_ref, own_ref, got_ref, keep_ref, send_ref):
    half = keep_ref.shape[0]
    for ref, part in ((keep_ref, bit_ref[0]), (send_ref, 1 - bit_ref[0])):
        rows = pl.ds(part * half, half)
        ref[...] = (own_ref[rows] + got_ref[rows].astype(F32)).astype(ref.dtype)


def join_kernel(bit_ref, own_ref, got_ref, full_ref):
    half = own_ref.shape[0]
    full_ref[pl.ds(bit_ref[0] * half, half)] = own_ref[...]
    full_ref[pl.ds((1 - bit_ref[0]) * half, half)] = got_ref[...]


def final_kernel(taps, core_ref, mine_ref, other_ref, base_ref, *refs):
    conv_ref, down_ref, grad_ref = refs[-3:]
    channels, conv_columns = conv_ref.shape
    half = mine_ref.shape[0]
    total = refs[0][...].astype(F32)
    for ref in refs[1:-3]:
        total += ref[...].astype(F32)
    grad_ref[:, RIM:] = base_ref[:, RIM:]
    grad_ref[:, :RIM] = base_ref[:, :RIM] + total
    for core in range(2):

        @pl.when(core_ref[0] == core)
        def _(core=core):
            for i, tile in enumerate(payload_tiles(channels, conv_columns, taps)):
                kind, row, column, columns = tile
                source = mine_ref if i // half == core else other_ref
                value = source[i % half].astype(F32)
                target = down_ref if kind else conv_ref
                target[row : row + TILE, column : column + columns] = value[:, :columns]


def shifts(count, step):
    return [(i, i + step) for i in range(count) if 0 <= i + step < count]


def chip_pairs(regions):
    mates = [(i, i ^ 1) for i in range(regions)]
    cross = [(i, i + 1) for i in range(1, regions - 1, 2)]
    return mates, cross + [(b, a) for a, b in cross]


def square_bits(nears, slabs, core):
    near = [("near", i) for i in range(nears.bit_length() - 1)]
    slab = [("slab", i) for i in range(slabs.bit_length() - 1)]
    return near + slab if core == 0 else slab + near


def bit_pairs(sizes, orders, phase):
    pairs = []
    for index in range(functools.reduce(lambda a, b: a * b, sizes.values())):
        place, left = {}, index
        for axis in reversed(SPLIT):
            left, place[axis] = divmod(left, sizes[axis])
        axis, bit = orders[place["core"]][phase]
        place[axis] ^= 1 << bit
        other = 0
        for name in SPLIT:
            other = other * sizes[name] + place[name]
        pairs.append((index, other))
    return pairs


def on_device(features, neighbours, down_map, w_conv, w_down, coarse_grad):
    sizes = {axis: lax.axis_size(axis) for axis in SPLIT}
    regions, slabs = sizes["far"] * sizes["near"] * sizes["core"], sizes["slab"]
    voxels, channels = features.shape
    offsets, taps = neighbours.shape[1], down_map.shape[1]
    conv_columns = offsets * channels
    core = lax.axis_index("core").astype(jnp.int32).reshape(1)
    swap = [(0, 1), (1, 0)]
    mates, crossings = chip_pairs(regions)
    orders = [square_bits(sizes["near"], slabs, c) for c in range(2)]
    phases = len(orders[0])
    bits = []
    for phase in range(phases):
        chosen = [(lax.axis_index(axis) >> bit) & 1 for axis, bit in (o[phase] for o in orders)]
        bits.append(jnp.where(core == 0, *chosen).astype(jnp.int32))

    smem = pl.BlockSpec(memory_space=pltpu.SMEM)
    vmem = pl.BlockSpec(memory_space=pltpu.VMEM)
    params = pltpu.CompilerParams(vmem_limit_bytes=VMEM_BYTES)
    light = pl.CostEstimate(flops=2 * 10**9, bytes_accessed=10**7, transcendentals=0)
    features_t, neighbours_t, w_conv_t = features.T, neighbours.T, w_conv.T
    rim = features_t[:, :RIM]
    if slabs == 2:
        side = [lax.ppermute(rim, "slab", swap)]
    else:
        side = [
            lax.ppermute(rim, "slab", shifts(slabs, 1)),
            lax.ppermute(rim, "slab", shifts(slabs, -1)),
        ]
    own = pl.pallas_call(
        functools.partial(gather_kernel, slabs),
        out_shape=(
            jax.ShapeDtypeStruct((conv_columns, LANES), BF16),
            jax.ShapeDtypeStruct((conv_columns, voxels - LANES), BF16),
        ),
        compiler_params=params,
        cost_estimate=light,
        name="gather",
    )(features_t, neighbours_t)
    side, own = lax.optimization_barrier((side, own))
    row = [rim, side[0]] if slabs == 2 else [side[0], rim, side[1]]
    row = jnp.concatenate(row, axis=1)
    cross = lax.ppermute(row, RING, crossings)
    mate = lax.ppermute(row, RING, mates)
    row, down_t = lax.optimization_barrier((row, down_map.T))
    pick, hgrad = pl.pallas_call(
        taps_kernel,
        out_shape=(
            jax.ShapeDtypeStruct((taps, coarse_grad.shape[0], voxels), BF16),
            jax.ShapeDtypeStruct((channels, voxels), F32),
        ),
        compiler_params=params,
        cost_estimate=light,
        name="taps",
    )(down_t, coarse_grad, w_down)
    halos = [mate, cross, *side]

    tiles = len(payload_tiles(channels, conv_columns, taps))
    squares = 1 << phases
    half = -(-tiles // (2 * squares)) * squares
    group, beside = row.shape[1], len(side) * RIM
    far_rows = -(-(2 * group + beside) // LANES) * LANES
    coarse, grad, keep, send = pl.pallas_call(
        functools.partial(forward_kernel, slabs),
        out_shape=(
            jax.ShapeDtypeStruct(coarse_grad.shape, BF16),
            jax.ShapeDtypeStruct((channels, voxels), BF16),
            jax.ShapeDtypeStruct((half, TILE, LANES), F32),
            jax.ShapeDtypeStruct((half, TILE, LANES), BF16),
        ),
        in_specs=[smem] + [vmem] * (9 + len(halos)),
        scratch_shapes=[
            pltpu.VMEM((conv_columns, voxels), BF16),
            pltpu.VMEM((channels, -(-conv_columns // LANES) * LANES), F32),
            pltpu.VMEM((taps * channels, LANES), F32),
        ],
        compiler_params=params,
        name="forward",
    )(core, features_t, neighbours_t, coarse_grad, w_conv_t, w_down, *own, pick, hgrad, *halos)

    def fold(phase, keep, got):
        shape = (keep.shape[0] // 2, TILE, LANES)
        return pl.pallas_call(
            fold_kernel,
            out_shape=(jax.ShapeDtypeStruct(shape, F32), jax.ShapeDtypeStruct(shape, BF16)),
            in_specs=[smem, vmem, vmem],
            compiler_params=params,
            name="fold",
        )(bits[phase], keep, got)

    def join(phase, own, got):
        return pl.pallas_call(
            join_kernel,
            out_shape=jax.ShapeDtypeStruct((own.shape[0] * 2, TILE, LANES), BF16),
            in_specs=[smem, vmem, vmem],
            compiler_params=params,
            name="join",
        )(bits[phase], own, got)

    got = lax.ppermute(send, "core", swap)
    for phase in range(phases):
        keep, send = fold(phase, keep, got)
        if phase == 0:
            send, grad = lax.optimization_barrier((send, grad))
        got = lax.ppermute(send, SPLIT, bit_pairs(sizes, orders, phase))
        if phase == 0:
            base, mate, cross, own_side = pl.pallas_call(
                functools.partial(backward_kernel, slabs),
                out_shape=(
                    jax.ShapeDtypeStruct((channels, voxels), F32),
                    jax.ShapeDtypeStruct((channels, group), BF16),
                    jax.ShapeDtypeStruct((channels, group), BF16),
                    jax.ShapeDtypeStruct((channels, beside), BF16),
                ),
                in_specs=[smem] + [vmem] * 4,
                scratch_shapes=[
                    pltpu.VMEM((channels, offsets * voxels), BF16),
                    pltpu.VMEM((channels, offsets * LANES), BF16),
                    pltpu.VMEM((voxels, offsets * voxels), BF16),
                    pltpu.VMEM((far_rows, offsets * LANES), BF16),
                    pltpu.VMEM((conv_columns, LANES), BF16),
                ],
                compiler_params=params,
                cost_estimate=light,
                name="backward",
            )(core, neighbours_t, hgrad, grad, w_conv_t)
            got, mate, cross, own_side, base = lax.optimization_barrier(
                (got, mate, cross, own_side, base)
            )
    total = (keep + got.astype(F32)).astype(BF16)
    far_bits = sizes["far"].bit_length() - 1
    for bit in range(far_bits):
        if bit == far_bits - 1:
            total, mate, cross = lax.optimization_barrier((total, mate, cross))
        pairs = [(i, i ^ (1 << bit)) for i in range(sizes["far"])]
        got = lax.ppermute(total, "far", pairs)
        if bit == far_bits - 1:
            cross, mate = lax.ppermute(cross, RING, crossings), lax.ppermute(mate, RING, mates)
            got, mate, cross = lax.optimization_barrier((got, mate, cross))
        total = (total.astype(F32) + got.astype(F32)).astype(BF16)
    row_grad = mate.astype(F32) + cross.astype(F32)
    columns = [row_grad[:, i : i + RIM] for i in range(0, group, RIM)]
    own = [own_side[:, i : i + RIM].astype(F32) for i in range(0, beside, RIM)]
    if slabs == 2:
        home = columns[0]
        edges = [((columns[1] + own[0]).astype(BF16), swap)]
    else:
        home = columns[1]
        edges = [
            ((columns[0] + own[0]).astype(BF16), shifts(slabs, -1)),
            ((columns[2] + own[1]).astype(BF16), shifts(slabs, 1)),
        ]
    for phase in reversed(range(phases)):
        got = lax.ppermute(total, SPLIT, bit_pairs(sizes, orders, phase))
        if phase == 0:
            edges = [lax.ppermute(x, "slab", pairs) for x, pairs in edges]
            got, edges = lax.optimization_barrier((got, edges))
        total = join(phase, total, got)
    other = lax.ppermute(total, "core", swap)
    conv_wgrad_t, down_wgrad, grad_input_t = pl.pallas_call(
        functools.partial(final_kernel, taps),
        out_shape=(
            jax.ShapeDtypeStruct((channels, conv_columns), F32),
            jax.ShapeDtypeStruct((taps * channels, LANES), F32),
            jax.ShapeDtypeStruct((channels, voxels), F32),
        ),
        in_specs=[smem] + [vmem] * (4 + len(edges)),
        compiler_params=params,
        name="final",
    )(core, total, other, base, home, *edges)
    return coarse, grad_input_t.T, conv_wgrad_t.T, down_wgrad


def solution(mesh):
    regions, slabs = mesh.shape["region"], mesh.shape["slab"]
    fine = Mesh(mesh.devices.reshape(regions // 4, 2, 2, slabs), SPLIT)
    split = P(SPLIT, None)
    return jax.shard_map(
        on_device,
        mesh=fine,
        in_specs=(split, split, split, P(), P(), split),
        out_specs=(split, split, P(), P()),
        check_vma=False,
    )
```

```python
import functools

import jax
import jax.numpy as jnp
from jax import lax
from jax.experimental import pallas as pl
from jax.experimental.pallas import tpu as pltpu
from jax.sharding import Mesh, PartitionSpec as P

SPLIT = ("far", "near", "core", "slab")
RING = ("far", "near", "core")
RIM = 64
LANES = 128
TILE = 16
CHUNKS = 2
F32 = jnp.float32
BF16 = jnp.bfloat16
NN = (((1,), (0,)), ((), ()))
NT = (((1,), (1,)), ((), ()))
VMEM_BYTES = 20 * 2**20


def mm(a, b, dims=NN):
    return lax.dot_general(a, b, dims, preferred_element_type=F32)


def table_lanes(neighbours, voxels, slabs, core):
    code = neighbours // voxels
    slot = neighbours - code * voxels
    row = code // 3
    col = code - row * 3
    if slabs == 2:
        rims = 2
        place = jnp.where(col == 1, 0, 1)
        beside = 0
    else:
        rims = 3
        place = col
        beside = col // 2
    group = jnp.abs(row // 2 + core - 1)
    rim = jnp.where(row == 1, 2 * rims + beside, group * rims + place)
    lane = jnp.where(code == 4, slot, voxels + rim * RIM + slot)
    return jnp.where(code > 8, -1, lane)


def payload_tiles(channels, conv_columns, taps):
    tiles = []
    for column in range(0, conv_columns, LANES):
        for row in range(0, channels, TILE):
            tiles.append((0, row, column, min(LANES, conv_columns - column)))
    for row in range(0, taps * channels, TILE):
        tiles.append((1, row, 0, LANES))
    return tiles


def padded_halo(halo_refs):
    halo = [h[...] for h in halo_refs]
    width = sum(h.shape[1] for h in halo)
    slack = -width % LANES
    if slack:
        halo.append(jnp.zeros((halo[0].shape[0], slack), BF16))
    return jnp.concatenate(halo, axis=1)


def gather_kernel(slabs, core_ref, f_ref, near_ref, first_ref, rest_ref, far_ref):
    channels, voxels = f_ref.shape
    table_t = f_ref[...]
    lanes = table_lanes(near_ref[...], voxels, slabs, core_ref[0])
    far_iota = lax.broadcasted_iota(jnp.int32, (far_ref.shape[0], LANES), 0) + voxels
    near_iota = lax.broadcasted_iota(jnp.int32, (voxels, voxels), 0)
    for o in range(near_ref.shape[0]):
        near = jnp.where(near_iota == lanes[o : o + 1, :], 1.0, 0.0).astype(BF16)
        own = mm(table_t, near).astype(BF16)
        first_ref[o * channels : (o + 1) * channels, :] = own[:, :LANES]
        rest_ref[o * channels : (o + 1) * channels, :] = own[:, LANES:]
        away = jnp.where(far_iota == lanes[o : o + 1, :LANES], 1.0, 0.0).astype(BF16)
        far_ref[:, o * LANES : (o + 1) * LANES] = away


def taps_kernel(down_ref, cgrad_ref, wd_ref, pick_ref, hgrad_ref):
    channels, voxels = hgrad_ref.shape
    taps, coarse_count = down_ref.shape
    cgrad_t = cgrad_ref[...].astype(F32).T.astype(BF16)
    down = down_ref[...].astype(F32).T
    lane_iota = lax.broadcasted_iota(jnp.int32, (coarse_count, voxels), 1).astype(F32)
    hgrad_t = jnp.zeros((channels, voxels), F32)
    for t in range(taps):
        pick = jnp.where(lane_iota == down[:, t : t + 1], 1.0, 0.0).astype(BF16)
        pick_ref[t] = pick
        wd = wd_ref[t * channels : (t + 1) * channels, :]
        hgrad_t += mm(wd, mm(cgrad_t, pick).astype(BF16))
    hgrad_ref[...] = hgrad_t


def forward_kernel(halo_count, core_ref, f_ref, cgrad_ref, w_ref, *refs):
    first_ref, rest_ref, far_ref, pick_ref, hgrad_ref = refs[:5]
    halo_refs, refs = refs[5 : 5 + halo_count], refs[5 + halo_count :]
    grad_ref, hidden_ref, *chunks, rt, conv_w, down_w = refs
    channels = f_ref.shape[0]
    offsets = far_ref.shape[1] // LANES
    taps = pick_ref.shape[0]
    conv_columns = offsets * channels
    halo_t = padded_halo(halo_refs)
    for pair in range(0, offsets, 2):
        away = mm(halo_t, far_ref[:, pair * LANES : min(pair + 2, offsets) * LANES])
        for o in range(pair, min(pair + 2, offsets)):
            rows = slice(o * channels, (o + 1) * channels)
            lanes = slice((o - pair) * LANES, (o - pair + 1) * LANES)
            first = first_ref[rows, :].astype(F32) + away[:, lanes]
            rt[rows, :LANES] = first.astype(BF16)
            rt[rows, LANES:] = rest_ref[rows, :]

    out_t = mm(w_ref[...], rt[...])
    sig = 1.0 / (1.0 + jnp.exp(-out_t))
    hidden_t = (f_ref[...].astype(F32) + out_t * sig).astype(BF16)
    grad_t = (hgrad_ref[...] * sig * (1.0 + out_t * (1.0 - sig))).astype(BF16)
    grad_ref[...] = grad_t
    conv_w[:, :conv_columns] = mm(grad_t, rt[...], NT)
    if conv_w.shape[1] > conv_columns:
        slack = conv_w.shape[1] - conv_columns
        conv_w[:, conv_columns:] = jnp.zeros((channels, slack), F32)

    hidden_ref[...] = hidden_t
    cgrad = cgrad_ref[...]
    for t in range(taps):
        picked_t = mm(hidden_t, pick_ref[t], NT).astype(BF16)
        down_w[t * channels : (t + 1) * channels, :] = mm(picked_t, cgrad)

    tiles = payload_tiles(channels, conv_columns, taps)
    count = len(chunks) // 2
    size = chunks[0].shape[0]
    for core in range(2):

        @pl.when(core_ref[0] == core)
        def _(core=core):
            for i in range(2 * count * size):
                half, chunk, place = i // (count * size), i // size % count, i % size
                ref = chunks[2 * chunk + (half != core)]
                if i < len(tiles):
                    kind, row, column, _ = tiles[i]
                    source = down_w if kind else conv_w
                    value = source[row : row + TILE, column : column + LANES]
                else:
                    value = jnp.zeros((TILE, LANES), F32)
                ref[place] = value.astype(ref.dtype)


def backward_kernel(slabs, core_ref, near_ref, far_ref, hgrad_ref, grad_ref, w_ref, *refs):
    pick_ref, hidden_ref, wd_ref, *refs = refs
    coarse_ref, base_ref, mate_ref, cross_ref, side_ref, drt, drt_far, hot, w_back = refs
    channels, voxels = hgrad_ref.shape
    offsets = near_ref.shape[0]
    group = mate_ref.shape[1]
    coarse = jnp.zeros(coarse_ref.shape, F32)
    for t in range(pick_ref.shape[0]):
        picked = mm(pick_ref[t], hidden_ref[...], NT).astype(BF16)
        coarse += mm(picked, wd_ref[t * channels : (t + 1) * channels, :])
    coarse_ref[...] = coarse.astype(BF16)
    lanes = table_lanes(near_ref[...], voxels, slabs, core_ref[0])
    near_iota = lax.broadcasted_iota(jnp.int32, (voxels, voxels), 0)
    w_back[:, :channels] = w_ref[...].astype(F32).T.astype(BF16)
    w_back[:, channels:] = jnp.zeros((offsets * channels, LANES - channels), BF16)
    slack = jnp.zeros((LANES - channels, voxels), BF16)
    grad_pad = jnp.concatenate([grad_ref[...], slack], axis=0)
    for o in range(offsets):
        near = jnp.where(near_iota == lanes[o : o + 1, :], 1.0, 0.0).astype(BF16)
        hot[:, o * voxels : (o + 1) * voxels] = near
        spread = mm(w_back[o * channels : (o + 1) * channels, :], grad_pad).astype(BF16)
        drt[:, o * voxels : (o + 1) * voxels] = spread
        drt_far[:, o * LANES : (o + 1) * LANES] = spread[:, :LANES]
    base_ref[...] = hgrad_ref[...] + mm(drt[...], hot[...], NT)
    back_t = mm(drt_far[...], far_ref[...], NT).astype(BF16)
    mate_ref[...] = back_t[:, :group]
    cross_ref[...] = back_t[:, group : 2 * group]
    side_ref[...] = back_t[:, 2 * group : 2 * group + side_ref.shape[1]]


def fold_kernel(bit_ref, own_ref, got_ref, keep_ref, send_ref):
    half = keep_ref.shape[0]
    for ref, part in ((keep_ref, bit_ref[0]), (send_ref, 1 - bit_ref[0])):
        rows = pl.ds(part * half, half)
        ref[...] = (own_ref[rows] + got_ref[rows].astype(F32)).astype(ref.dtype)


def join_kernel(bit_ref, own_ref, got_ref, full_ref):
    half = own_ref.shape[0]
    full_ref[pl.ds(bit_ref[0] * half, half)] = own_ref[...]
    full_ref[pl.ds((1 - bit_ref[0]) * half, half)] = got_ref[...]


def final_kernel(taps, count, core_ref, *refs):
    mine, other, refs = refs[:count], refs[count : 2 * count], refs[2 * count :]
    base_ref, *parts, conv_ref, down_ref, grad_ref = refs
    channels, conv_columns = conv_ref.shape
    size = mine[0].shape[0]
    total = parts[0][...].astype(F32)
    for ref in parts[1:]:
        total += ref[...].astype(F32)
    grad_ref[:, RIM:] = base_ref[:, RIM:]
    grad_ref[:, :RIM] = base_ref[:, :RIM] + total
    for core in range(2):

        @pl.when(core_ref[0] == core)
        def _(core=core):
            for i, tile in enumerate(payload_tiles(channels, conv_columns, taps)):
                kind, row, column, columns = tile
                source = mine if i // (count * size) == core else other
                value = source[i // size % count][i % size].astype(F32)
                target = down_ref if kind else conv_ref
                target[row : row + TILE, column : column + columns] = value[:, :columns]


def shifts(count, step):
    return [(i, i + step) for i in range(count) if 0 <= i + step < count]


def chip_pairs(regions):
    mates = [(i, i ^ 1) for i in range(regions)]
    cross = [(i, i + 1) for i in range(1, regions - 1, 2)]
    return mates, cross + [(b, a) for a, b in cross]


def halo_pairs(regions, slabs, links, step):
    pairs = []
    for owner, reader in links:
        for slab in range(slabs):
            other = (slab + step) % 2 if slabs == 2 else slab + step
            if 0 <= other < slabs:
                pairs.append((owner * slabs + other, reader * slabs + slab))
    return pairs


def square_bits(nears, slabs, core):
    near = [("near", i) for i in range(nears.bit_length() - 1)]
    slab = [("slab", i) for i in range(slabs.bit_length() - 1)]
    return near + slab if core == 0 else slab + near


def bit_pairs(sizes, orders, phase):
    pairs = []
    for index in range(functools.reduce(lambda a, b: a * b, sizes.values())):
        place, left = {}, index
        for axis in reversed(SPLIT):
            left, place[axis] = divmod(left, sizes[axis])
        axis, bit = orders[place["core"]][phase]
        place[axis] ^= 1 << bit
        other = 0
        for name in SPLIT:
            other = other * sizes[name] + place[name]
        pairs.append((index, other))
    return pairs


def on_device(features, neighbours, down_map, w_conv, w_down, coarse_grad):
    sizes = {axis: lax.axis_size(axis) for axis in SPLIT}
    regions, slabs = sizes["far"] * sizes["near"] * sizes["core"], sizes["slab"]
    voxels, channels = features.shape
    offsets, taps = neighbours.shape[1], down_map.shape[1]
    conv_columns = offsets * channels
    core = lax.axis_index("core").astype(jnp.int32).reshape(1)
    swap = [(0, 1), (1, 0)]
    mates, crossings = chip_pairs(regions)
    orders = [square_bits(sizes["near"], slabs, c) for c in range(2)]
    phases = len(orders[0])
    bits = []
    for phase in range(phases):
        chosen = [(lax.axis_index(axis) >> bit) & 1 for axis, bit in (o[phase] for o in orders)]
        bits.append(jnp.where(core == 0, *chosen).astype(jnp.int32))

    smem = pl.BlockSpec(memory_space=pltpu.SMEM)
    vmem = pl.BlockSpec(memory_space=pltpu.VMEM)
    params = pltpu.CompilerParams(vmem_limit_bytes=VMEM_BYTES)
    light = pl.CostEstimate(flops=2 * 10**9, bytes_accessed=10**7, transcendentals=0)
    features_t, neighbours_t, w_conv_t = features.T, neighbours.T, w_conv.T
    rim = features_t[:, :RIM]
    here = [(i, i) for i in range(regions)]
    around = (0, 1) if slabs == 2 else (-1, 0, 1)
    beside = (1,) if slabs == 2 else (-1, 1)
    sections = [(x, s) for x in (mates, crossings) for s in around] + [(here, s) for s in beside]
    halos = [None] * len(sections)
    for wanted in (crossings, mates, here):
        for i, (links, step) in sorted(enumerate(sections), key=lambda x: -abs(x[1][1])):
            if links is wanted:
                halos[i] = lax.ppermute(rim, SPLIT, halo_pairs(regions, slabs, links, step))
    group, beside = len(around) * RIM, len(beside) * RIM
    far_rows = -(-(2 * group + beside) // LANES) * LANES
    own = pl.pallas_call(
        functools.partial(gather_kernel, slabs),
        out_shape=(
            jax.ShapeDtypeStruct((conv_columns, LANES), BF16),
            jax.ShapeDtypeStruct((conv_columns, voxels - LANES), BF16),
            jax.ShapeDtypeStruct((far_rows, offsets * LANES), BF16),
        ),
        in_specs=[smem, vmem, vmem],
        compiler_params=params,
        cost_estimate=light,
        name="gather",
    )(core, features_t, neighbours_t)
    far = own[2]
    pick, hgrad = pl.pallas_call(
        taps_kernel,
        out_shape=(
            jax.ShapeDtypeStruct((taps, coarse_grad.shape[0], voxels), BF16),
            jax.ShapeDtypeStruct((channels, voxels), F32),
        ),
        compiler_params=params,
        cost_estimate=light,
        name="taps",
    )(down_map.T, coarse_grad, w_down)

    tiles = len(payload_tiles(channels, conv_columns, taps))
    size = -(-tiles // (2 * CHUNKS << phases)) << phases
    grad, hidden, *chunks = pl.pallas_call(
        functools.partial(forward_kernel, len(halos)),
        out_shape=[
            jax.ShapeDtypeStruct((channels, voxels), BF16),
            jax.ShapeDtypeStruct((channels, voxels), BF16),
        ]
        + [jax.ShapeDtypeStruct((size, TILE, LANES), kind) for kind in (F32, BF16)] * CHUNKS,
        in_specs=[smem] + [vmem] * (8 + len(halos)),
        scratch_shapes=[
            pltpu.VMEM((conv_columns, voxels), BF16),
            pltpu.VMEM((channels, -(-conv_columns // LANES) * LANES), F32),
            pltpu.VMEM((taps * channels, LANES), F32),
        ],
        compiler_params=params,
        name="forward",
    )(core, features_t, coarse_grad, w_conv_t, *own, pick, hgrad, *halos)

    def fold(phase, keep, got):
        shape = (keep.shape[0] // 2, TILE, LANES)
        return pl.pallas_call(
            fold_kernel,
            out_shape=(jax.ShapeDtypeStruct(shape, F32), jax.ShapeDtypeStruct(shape, BF16)),
            in_specs=[smem, vmem, vmem],
            compiler_params=params,
            name="fold",
        )(bits[phase], keep, got)

    def join(phase, own, got):
        return pl.pallas_call(
            join_kernel,
            out_shape=jax.ShapeDtypeStruct((own.shape[0] * 2, TILE, LANES), BF16),
            in_specs=[smem, vmem, vmem],
            compiler_params=params,
            name="join",
        )(bits[phase], own, got)

    keep, send = chunks[0::2], chunks[1::2]
    got = [lax.ppermute(x, "core", swap) for x in send]
    for phase in range(phases):
        pairs = bit_pairs(sizes, orders, phase)
        for i in range(CHUNKS):
            keep[i], send[i] = fold(phase, keep[i], got[i])
            if phase == 0 and i == 0:
                send[0], grad = lax.optimization_barrier((send[0], grad))
            got[i] = lax.ppermute(send[i], SPLIT, pairs)
        if phase == 0:
            coarse, base, mate, cross, own_side = pl.pallas_call(
                functools.partial(backward_kernel, slabs),
                out_shape=(
                    jax.ShapeDtypeStruct(coarse_grad.shape, BF16),
                    jax.ShapeDtypeStruct((channels, voxels), F32),
                    jax.ShapeDtypeStruct((channels, group), BF16),
                    jax.ShapeDtypeStruct((channels, group), BF16),
                    jax.ShapeDtypeStruct((channels, beside), BF16),
                ),
                in_specs=[smem] + [vmem] * 8,
                scratch_shapes=[
                    pltpu.VMEM((channels, offsets * voxels), BF16),
                    pltpu.VMEM((channels, offsets * LANES), BF16),
                    pltpu.VMEM((voxels, offsets * voxels), BF16),
                    pltpu.VMEM((conv_columns, LANES), BF16),
                ],
                compiler_params=params,
                cost_estimate=light,
                name="backward",
            )(core, neighbours_t, far, hgrad, grad, w_conv_t, pick, hidden, w_down)
            got[0], mate, cross, own_side, base = lax.optimization_barrier(
                (got[0], mate, cross, own_side, base)
            )
    total = [(x + y.astype(F32)).astype(BF16) for x, y in zip(keep, got)]
    far_bits = sizes["far"].bit_length() - 1
    for bit in range(far_bits):
        pairs = [(i, i ^ (1 << bit)) for i in range(sizes["far"])]
        if bit == far_bits - 1:
            total[0], mate, cross = lax.optimization_barrier((total[0], mate, cross))
        for i in range(CHUNKS):
            got[i] = lax.ppermute(total[i], "far", pairs)
            total[i] = (total[i].astype(F32) + got[i].astype(F32)).astype(BF16)
    cross, mate = lax.ppermute(cross, RING, crossings), lax.ppermute(mate, RING, mates)
    for phase in reversed(range(phases)):
        pairs = bit_pairs(sizes, orders, phase)
        got = [lax.ppermute(x, SPLIT, pairs) for x in total]
        if phase == phases - 1:
            got[0], mate, cross = lax.optimization_barrier((got[0], mate, cross))
            row_grad = mate.astype(F32) + cross.astype(F32)
            columns = [row_grad[:, i : i + RIM] for i in range(0, group, RIM)]
            own = [own_side[:, i : i + RIM].astype(F32) for i in range(0, beside, RIM)]
            if slabs == 2:
                home = columns[0]
                edges = [((columns[1] + own[0]).astype(BF16), swap)]
            else:
                home = columns[1]
                edges = [
                    ((columns[0] + own[0]).astype(BF16), shifts(slabs, -1)),
                    ((columns[2] + own[1]).astype(BF16), shifts(slabs, 1)),
                ]
            edges = [lax.ppermute(x, "slab", p) for x, p in edges]
        if phase == 0:
            got[0], edges = lax.optimization_barrier((got[0], edges))
        total = [join(phase, x, y) for x, y in zip(total, got)]
    other = [lax.ppermute(x, "core", swap) for x in total]
    conv_wgrad_t, down_wgrad, grad_input_t = pl.pallas_call(
        functools.partial(final_kernel, taps, CHUNKS),
        out_shape=(
            jax.ShapeDtypeStruct((channels, conv_columns), F32),
            jax.ShapeDtypeStruct((taps * channels, LANES), F32),
            jax.ShapeDtypeStruct((channels, voxels), F32),
        ),
        in_specs=[smem] + [vmem] * (2 * CHUNKS + 2 + len(edges)),
        compiler_params=params,
        name="final",
    )(core, *total, *other, base, home, *edges)
    return coarse, grad_input_t.T, conv_wgrad_t.T, down_wgrad


def solution(mesh):
    regions, slabs = mesh.shape["region"], mesh.shape["slab"]
    fine = Mesh(mesh.devices.reshape(regions // 4, 2, 2, slabs), SPLIT)
    split = P(SPLIT, None)
    return jax.shard_map(
        on_device,
        mesh=fine,
        in_specs=(split, split, split, P(), P(), split),
        out_specs=(split, split, P(), P()),
        check_vma=False,
    )
```

```python
import functools

import jax
import jax.numpy as jnp
from jax import lax
from jax.experimental import pallas as pl
from jax.experimental.pallas import tpu as pltpu
from jax.sharding import Mesh, PartitionSpec as P

SPLIT = ("far", "near", "core", "slab")
RING = ("far", "near", "core")
RIM = 64
LANES = 128
TILE = 16
CHUNKS = 2
F32 = jnp.float32
BF16 = jnp.bfloat16
NN = (((1,), (0,)), ((), ()))
NT = (((1,), (1,)), ((), ()))
VMEM_BYTES = 20 * 2**20


def mm(a, b, dims=NN):
    return lax.dot_general(a, b, dims, preferred_element_type=F32)


def table_lanes(neighbours, voxels, slabs, core):
    code = neighbours // voxels
    slot = neighbours - code * voxels
    row = code // 3
    col = code - row * 3
    if slabs == 2:
        rims = 2
        place = jnp.where(col == 1, 0, 1)
        beside = 0
    else:
        rims = 3
        place = col
        beside = col // 2
    group = jnp.abs(row // 2 + core - 1)
    rim = jnp.where(row == 1, 2 * rims + beside, group * rims + place)
    lane = jnp.where(code == 4, slot, voxels + rim * RIM + slot)
    return jnp.where(code > 8, -1, lane)


def payload_tiles(channels, conv_columns, taps):
    tiles = []
    for column in range(0, conv_columns, LANES):
        for row in range(0, channels, TILE):
            tiles.append((0, row, column, min(LANES, conv_columns - column)))
    for row in range(0, taps * channels, TILE):
        tiles.append((1, row, 0, LANES))
    return tiles


def padded_halo(halo_refs):
    halo = [h[...] for h in halo_refs]
    width = sum(h.shape[1] for h in halo)
    slack = -width % LANES
    if slack:
        halo.append(jnp.zeros((halo[0].shape[0], slack), BF16))
    return jnp.concatenate(halo, axis=1)


def gather_kernel(slabs, f_ref, near_ref, first_ref, rest_ref):
    channels, voxels = f_ref.shape
    table_t = f_ref[...]
    lanes = table_lanes(near_ref[...], voxels, slabs, 0)
    near_iota = lax.broadcasted_iota(jnp.int32, (voxels, voxels), 0)
    for o in range(near_ref.shape[0]):
        near = jnp.where(near_iota == lanes[o : o + 1, :], 1.0, 0.0).astype(BF16)
        own = mm(table_t, near).astype(BF16)
        first_ref[o * channels : (o + 1) * channels, :] = own[:, :LANES]
        rest_ref[o * channels : (o + 1) * channels, :] = own[:, LANES:]


def taps_kernel(down_ref, cgrad_ref, wd_ref, pick_ref, hgrad_ref):
    channels, voxels = hgrad_ref.shape
    taps, coarse_count = down_ref.shape
    cgrad_t = cgrad_ref[...].astype(F32).T.astype(BF16)
    down = down_ref[...].astype(F32).T
    lane_iota = lax.broadcasted_iota(jnp.int32, (coarse_count, voxels), 1).astype(F32)
    hgrad_t = jnp.zeros((channels, voxels), F32)
    for t in range(taps):
        pick = jnp.where(lane_iota == down[:, t : t + 1], 1.0, 0.0).astype(BF16)
        pick_ref[t] = pick
        wd = wd_ref[t * channels : (t + 1) * channels, :]
        hgrad_t += mm(wd, mm(cgrad_t, pick).astype(BF16))
    hgrad_ref[...] = hgrad_t


def far_one_hots(lanes, rows, voxels, offsets):
    iota = lax.broadcasted_iota(jnp.int32, (rows, LANES), 0) + voxels
    hots = [jnp.where(iota == lanes[o : o + 1, :LANES], 1.0, 0.0).astype(BF16) for o in offsets]
    return jnp.concatenate(hots, axis=1)


def forward_kernel(slabs, core_ref, f_ref, near_ref, cgrad_ref, w_ref, *refs):
    first_ref, rest_ref, pick_ref, hgrad_ref = refs[:4]
    halo_refs, refs = (refs[4:7], refs[7:]) if slabs == 2 else (refs[4:8], refs[8:])
    grad_ref, hidden_ref, *chunks, rt, conv_w, down_w = refs
    channels, voxels = f_ref.shape
    offsets = near_ref.shape[0]
    taps = pick_ref.shape[0]
    conv_columns = offsets * channels
    halo_t = padded_halo(halo_refs)
    lanes = table_lanes(near_ref[:, :LANES], voxels, slabs, core_ref[0])
    for pair in range(0, offsets, 2):
        pair = range(pair, min(pair + 2, offsets))
        away = mm(halo_t, far_one_hots(lanes, halo_t.shape[1], voxels, pair))
        for i, o in enumerate(pair):
            rows = slice(o * channels, (o + 1) * channels)
            first = first_ref[rows, :].astype(F32) + away[:, i * LANES : (i + 1) * LANES]
            rt[rows, :LANES] = first.astype(BF16)
            rt[rows, LANES:] = rest_ref[rows, :]

    out_t = mm(w_ref[...], rt[...])
    sig = 1.0 / (1.0 + jnp.exp(-out_t))
    hidden_t = (f_ref[...].astype(F32) + out_t * sig).astype(BF16)
    grad_t = (hgrad_ref[...] * sig * (1.0 + out_t * (1.0 - sig))).astype(BF16)
    grad_ref[...] = grad_t
    conv_w[:, :conv_columns] = mm(grad_t, rt[...], NT)
    if conv_w.shape[1] > conv_columns:
        slack = conv_w.shape[1] - conv_columns
        conv_w[:, conv_columns:] = jnp.zeros((channels, slack), F32)

    hidden_ref[...] = hidden_t
    cgrad = cgrad_ref[...]
    for t in range(taps):
        picked_t = mm(hidden_t, pick_ref[t], NT).astype(BF16)
        down_w[t * channels : (t + 1) * channels, :] = mm(picked_t, cgrad)

    tiles = payload_tiles(channels, conv_columns, taps)
    count = len(chunks) // 2
    size = chunks[0].shape[0]
    for core in range(2):

        @pl.when(core_ref[0] == core)
        def _(core=core):
            for i in range(2 * count * size):
                half, chunk, place = i // (count * size), i // size % count, i % size
                ref = chunks[2 * chunk + (half != core)]
                if i < len(tiles):
                    kind, row, column, _ = tiles[i]
                    source = down_w if kind else conv_w
                    value = source[row : row + TILE, column : column + LANES]
                else:
                    value = jnp.zeros((TILE, LANES), F32)
                ref[place] = value.astype(ref.dtype)


def backward_kernel(slabs, core_ref, near_ref, hgrad_ref, grad_ref, w_ref, *refs):
    pick_ref, hidden_ref, wd_ref, coarse_ref, base_ref, keep_ref, *refs = refs
    cross_refs, (drt, drt_far, hot, far, w_back) = refs[:-5], refs[-5:]
    channels, voxels = hgrad_ref.shape
    offsets = near_ref.shape[0]
    coarse = jnp.zeros(coarse_ref.shape, F32)
    for t in range(pick_ref.shape[0]):
        picked = mm(pick_ref[t], hidden_ref[...], NT).astype(BF16)
        coarse += mm(picked, wd_ref[t * channels : (t + 1) * channels, :])
    coarse_ref[...] = coarse.astype(BF16)
    lanes = table_lanes(near_ref[...], voxels, slabs, core_ref[0])
    near_iota = lax.broadcasted_iota(jnp.int32, (voxels, voxels), 0)
    w_back[:, :channels] = w_ref[...].astype(F32).T.astype(BF16)
    w_back[:, channels:] = jnp.zeros((offsets * channels, LANES - channels), BF16)
    slack = jnp.zeros((LANES - channels, voxels), BF16)
    grad_pad = jnp.concatenate([grad_ref[...], slack], axis=0)
    for o in range(offsets):
        near = jnp.where(near_iota == lanes[o : o + 1, :], 1.0, 0.0).astype(BF16)
        hot[:, o * voxels : (o + 1) * voxels] = near
        spread = mm(w_back[o * channels : (o + 1) * channels, :], grad_pad).astype(BF16)
        drt[:, o * voxels : (o + 1) * voxels] = spread
        drt_far[:, o * LANES : (o + 1) * LANES] = spread[:, :LANES]
        far[:, o * LANES : (o + 1) * LANES] = far_one_hots(lanes, far.shape[0], voxels, (o,))
    base_ref[...] = hgrad_ref[...] + mm(drt[...], hot[...], NT)
    back_t = mm(drt_far[...], far[...], NT)
    rims = 2 if slabs == 2 else 3
    mid = 0 if slabs == 2 else 1
    rim = [back_t[:, i * RIM : (i + 1) * RIM] for i in range(2 * rims + len(cross_refs))]
    keep_ref[...] = jnp.concatenate([rim[mid], rim[rims + mid]], axis=1)
    for i, ref in enumerate(cross_refs):
        place = 1 if slabs == 2 else 2 * i
        parts = [rim[place], rim[rims + place], rim[2 * rims + i], jnp.zeros_like(rim[0])]
        ref[...] = jnp.concatenate(parts, axis=1).astype(BF16)


def turn_kernel(base_ref, keep_ref, *refs):
    got_refs, (sum_ref, cross_ref, mate_ref) = refs[:-3], refs[-3:]
    got = got_refs[0][...].astype(F32)
    for ref in got_refs[1:]:
        got += ref[...].astype(F32)
    sum_ref[:, RIM:] = base_ref[:, RIM:]
    sum_ref[:, :RIM] = base_ref[:, :RIM] + got[:, 2 * RIM : 3 * RIM]
    pair = keep_ref[...] + got[:, : 2 * RIM]
    cross_ref[...] = pair[:, RIM:].astype(BF16)
    pair = pair.astype(BF16)
    for i in range(mate_ref.shape[0]):
        mate_ref[i] = pair[i * TILE : (i + 1) * TILE, :]


def fold_kernel(bit_ref, own_ref, got_ref, keep_ref, send_ref):
    half = keep_ref.shape[0]
    for ref, part in ((keep_ref, bit_ref[0]), (send_ref, 1 - bit_ref[0])):
        rows = pl.ds(part * half, half)
        ref[...] = (own_ref[rows] + got_ref[rows].astype(F32)).astype(ref.dtype)


def join_kernel(bit_ref, own_ref, got_ref, *refs):
    riders, full_ref = refs[:-1], refs[-1]
    half = own_ref.shape[0]
    for rider in riders:
        full_ref[2 * half :] = rider[...]
    full_ref[pl.ds(bit_ref[0] * half, half)] = own_ref[...]
    full_ref[pl.ds((1 - bit_ref[0]) * half, half)] = got_ref[...]


def final_kernel(taps, count, size, core_ref, *refs):
    mine, other, refs = refs[:count], refs[count : 2 * count], refs[2 * count :]
    base_ref, cross_ref, conv_ref, down_ref, grad_ref = refs
    channels, conv_columns = conv_ref.shape
    grad_ref[:, RIM:] = base_ref[:, RIM:]
    for i in range(channels // TILE):
        rows = slice(i * TILE, (i + 1) * TILE)
        total = base_ref[rows, :RIM] + cross_ref[rows, :].astype(F32)
        grad_ref[rows, :RIM] = total + other[-1][size + i][:, :RIM].astype(F32)
    for core in range(2):

        @pl.when(core_ref[0] == core)
        def _(core=core):
            for i, tile in enumerate(payload_tiles(channels, conv_columns, taps)):
                kind, row, column, columns = tile
                source = mine if i // (count * size) == core else other
                value = source[i // size % count][i % size].astype(F32)
                target = down_ref if kind else conv_ref
                target[row : row + TILE, column : column + columns] = value[:, :columns]


def shifts(count, step):
    return [(i, i + step) for i in range(count) if 0 <= i + step < count]


def chip_pairs(regions):
    mates = [(i, i ^ 1) for i in range(regions)]
    cross = [(i, i + 1) for i in range(1, regions - 1, 2)]
    return mates, cross + [(b, a) for a, b in cross]


def square_bits(nears, slabs, core):
    near = [("near", i) for i in range(nears.bit_length() - 1)]
    slab = [("slab", i) for i in range(slabs.bit_length() - 1)]
    return near + slab if core == 0 else slab + near


def bit_pairs(sizes, orders, phase):
    pairs = []
    for index in range(functools.reduce(lambda a, b: a * b, sizes.values())):
        place, left = {}, index
        for axis in reversed(SPLIT):
            left, place[axis] = divmod(left, sizes[axis])
        axis, bit = orders[place["core"]][phase]
        place[axis] ^= 1 << bit
        other = 0
        for name in SPLIT:
            other = other * sizes[name] + place[name]
        pairs.append((index, other))
    return pairs


def on_device(features, neighbours, down_map, w_conv, w_down, coarse_grad):
    sizes = {axis: lax.axis_size(axis) for axis in SPLIT}
    regions, slabs = sizes["far"] * sizes["near"] * sizes["core"], sizes["slab"]
    voxels, channels = features.shape
    offsets, taps = neighbours.shape[1], down_map.shape[1]
    conv_columns = offsets * channels
    core = lax.axis_index("core").astype(jnp.int32).reshape(1)
    swap = [(0, 1), (1, 0)]
    mates, crossings = chip_pairs(regions)
    orders = [square_bits(sizes["near"], slabs, c) for c in range(2)]
    phases = len(orders[0])
    bits = []
    for phase in range(phases):
        chosen = [(lax.axis_index(axis) >> bit) & 1 for axis, bit in (o[phase] for o in orders)]
        bits.append(jnp.where(core == 0, *chosen).astype(jnp.int32))

    smem = pl.BlockSpec(memory_space=pltpu.SMEM)
    vmem = pl.BlockSpec(memory_space=pltpu.VMEM)
    params = pltpu.CompilerParams(vmem_limit_bytes=VMEM_BYTES)
    light = pl.CostEstimate(flops=2 * 10**9, bytes_accessed=10**7, transcendentals=0)
    features_t, neighbours_t, w_conv_t = features.T, neighbours.T, w_conv.T
    rim = features_t[:, :RIM]
    if slabs == 2:
        beside = [swap]
    else:
        beside = [shifts(slabs, 1), shifts(slabs, -1)]
    side = [lax.ppermute(rim, "slab", pairs) for pairs in beside]
    own = pl.pallas_call(
        functools.partial(gather_kernel, slabs),
        out_shape=(
            jax.ShapeDtypeStruct((conv_columns, LANES), BF16),
            jax.ShapeDtypeStruct((conv_columns, voxels - LANES), BF16),
        ),
        compiler_params=params,
        cost_estimate=light,
        name="gather",
    )(features_t, neighbours_t)
    side, own = lax.optimization_barrier((side, own))
    row = [rim, side[0]] if slabs == 2 else [side[0], rim, side[1]]
    row = jnp.concatenate(row, axis=1)
    cross = lax.ppermute(row, RING, crossings)
    mate = lax.ppermute(row, RING, mates)
    row, down_t = lax.optimization_barrier((row, down_map.T))
    pick, hgrad = pl.pallas_call(
        taps_kernel,
        out_shape=(
            jax.ShapeDtypeStruct((taps, coarse_grad.shape[0], voxels), BF16),
            jax.ShapeDtypeStruct((channels, voxels), F32),
        ),
        compiler_params=params,
        cost_estimate=light,
        name="taps",
    )(down_t, coarse_grad, w_down)
    halos = [mate, cross, *side]
    far_rows = -(-sum(x.shape[1] for x in halos) // LANES) * LANES

    tiles = len(payload_tiles(channels, conv_columns, taps))
    size = -(-tiles // (2 * CHUNKS << phases)) << phases
    grad, hidden, *chunks = pl.pallas_call(
        functools.partial(forward_kernel, slabs),
        out_shape=[
            jax.ShapeDtypeStruct((channels, voxels), BF16),
            jax.ShapeDtypeStruct((channels, voxels), BF16),
        ]
        + [jax.ShapeDtypeStruct((size, TILE, LANES), kind) for kind in (F32, BF16)] * CHUNKS,
        in_specs=[smem] + [vmem] * (8 + len(halos)),
        scratch_shapes=[
            pltpu.VMEM((conv_columns, voxels), BF16),
            pltpu.VMEM((channels, -(-conv_columns // LANES) * LANES), F32),
            pltpu.VMEM((taps * channels, LANES), F32),
        ],
        compiler_params=params,
        name="forward",
    )(core, features_t, neighbours_t, coarse_grad, w_conv_t, *own, pick, hgrad, *halos)

    def fold(phase, keep, got):
        shape = (keep.shape[0] // 2, TILE, LANES)
        return pl.pallas_call(
            fold_kernel,
            out_shape=(jax.ShapeDtypeStruct(shape, F32), jax.ShapeDtypeStruct(shape, BF16)),
            in_specs=[smem, vmem, vmem],
            compiler_params=params,
            name="fold",
        )(bits[phase], keep, got)

    def join(phase, own, got, *riders):
        count = own.shape[0] * 2 + sum(x.shape[0] for x in riders)
        return pl.pallas_call(
            join_kernel,
            out_shape=jax.ShapeDtypeStruct((count, TILE, LANES), BF16),
            in_specs=[smem] + [vmem] * (2 + len(riders)),
            compiler_params=params,
            name="join",
        )(bits[phase], own, got, *riders)

    keep, send = chunks[0::2], chunks[1::2]
    got = [lax.ppermute(x, "core", swap) for x in send]
    for phase in range(phases):
        pairs = bit_pairs(sizes, orders, phase)
        for i in range(CHUNKS):
            keep[i], send[i] = fold(phase, keep[i], got[i])
            if phase == 0 and i == 0:
                send[0], grad = lax.optimization_barrier((send[0], grad))
            got[i] = lax.ppermute(send[i], SPLIT, pairs)
        if phase == 0:
            coarse, base, stay, *edges = pl.pallas_call(
                functools.partial(backward_kernel, slabs),
                out_shape=[
                    jax.ShapeDtypeStruct(coarse_grad.shape, BF16),
                    jax.ShapeDtypeStruct((channels, voxels), F32),
                    jax.ShapeDtypeStruct((channels, 2 * RIM), F32),
                ]
                + [jax.ShapeDtypeStruct((channels, 4 * RIM), BF16)] * len(beside),
                in_specs=[smem] + [vmem] * 7,
                scratch_shapes=[
                    pltpu.VMEM((channels, offsets * voxels), BF16),
                    pltpu.VMEM((channels, offsets * LANES), BF16),
                    pltpu.VMEM((voxels, offsets * voxels), BF16),
                    pltpu.VMEM((far_rows, offsets * LANES), BF16),
                    pltpu.VMEM((conv_columns, LANES), BF16),
                ],
                compiler_params=params,
                cost_estimate=light,
                name="backward",
            )(core, neighbours_t, hgrad, grad, w_conv_t, pick, hidden, w_down)
            got[0], stay, edges, base = lax.optimization_barrier((got[0], stay, edges, base))
        if phase == phases - 1:
            back = beside if slabs == 2 else beside[::-1]
            edges = [lax.ppermute(x, "slab", p) for x, p in zip(edges, back)]
            got[-1], edges = lax.optimization_barrier((got[-1], edges))
            base, cross, mate = pl.pallas_call(
                turn_kernel,
                out_shape=(
                    jax.ShapeDtypeStruct((channels, voxels), F32),
                    jax.ShapeDtypeStruct((channels, RIM), BF16),
                    jax.ShapeDtypeStruct((channels // TILE, TILE, LANES), BF16),
                ),
                compiler_params=params,
                name="turn",
            )(base, stay, *edges)
    total = [(x + y.astype(F32)).astype(BF16) for x, y in zip(keep, got)]
    far_bits = sizes["far"].bit_length() - 1
    for bit in range(far_bits):
        pairs = [(i, i ^ (1 << bit)) for i in range(sizes["far"])]
        got = [lax.ppermute(x, "far", pairs) for x in total]
        if bit == far_bits - 1:
            cross = lax.ppermute(cross, RING, crossings)
            got[-1], cross, mate = lax.optimization_barrier((got[-1], cross, mate))
        total = [(x.astype(F32) + y.astype(F32)).astype(BF16) for x, y in zip(total, got)]
    for phase in reversed(range(phases)):
        pairs = bit_pairs(sizes, orders, phase)
        got = [lax.ppermute(x, SPLIT, pairs) for x in total]
        riders = [()] * (CHUNKS - 1) + [(mate,) if phase == 0 else ()]
        total = [join(phase, x, y, *z) for x, y, z in zip(total, got, riders)]
    other = [lax.ppermute(x, "core", swap) for x in total]
    conv_wgrad_t, down_wgrad, grad_input_t = pl.pallas_call(
        functools.partial(final_kernel, taps, CHUNKS, size),
        out_shape=(
            jax.ShapeDtypeStruct((channels, conv_columns), F32),
            jax.ShapeDtypeStruct((taps * channels, LANES), F32),
            jax.ShapeDtypeStruct((channels, voxels), F32),
        ),
        in_specs=[smem] + [vmem] * (2 * CHUNKS + 2),
        compiler_params=params,
        name="final",
    )(core, *total, *other, base, cross)
    return coarse, grad_input_t.T, conv_wgrad_t.T, down_wgrad


def solution(mesh):
    regions, slabs = mesh.shape["region"], mesh.shape["slab"]
    fine = Mesh(mesh.devices.reshape(regions // 4, 2, 2, slabs), SPLIT)
    split = P(SPLIT, None)
    return jax.shard_map(
        on_device,
        mesh=fine,
        in_specs=(split, split, split, P(), P(), split),
        out_specs=(split, split, P(), P()),
        check_vma=False,
    )
```

```python
import functools

import jax
import jax.numpy as jnp
from jax import lax
from jax.experimental import pallas as pl
from jax.experimental.pallas import tpu as pltpu
from jax.sharding import Mesh, PartitionSpec as P

SPLIT = ("far", "near", "core", "slab")
RING = ("far", "near", "core")
RIM = 64
LANES = 128
TILE = 16
CHUNKS = 1
F32 = jnp.float32
BF16 = jnp.bfloat16
NN = (((1,), (0,)), ((), ()))
NT = (((1,), (1,)), ((), ()))
VMEM_BYTES = 20 * 2**20


def mm(a, b, dims=NN):
    return lax.dot_general(a, b, dims, preferred_element_type=F32)


def table_lanes(neighbours, voxels, slabs, core):
    code = neighbours // voxels
    slot = neighbours - code * voxels
    row = code // 3
    col = code - row * 3
    if slabs == 2:
        rims = 2
        place = jnp.where(col == 1, 0, 1)
        beside = 0
    else:
        rims = 3
        place = col
        beside = col // 2
    group = jnp.abs(row // 2 + core - 1)
    rim = jnp.where(row == 1, 2 * rims + beside, group * rims + place)
    lane = jnp.where(code == 4, slot, voxels + rim * RIM + slot)
    return jnp.where(code > 8, -1, lane)


def payload_tiles(channels, conv_columns, taps):
    tiles = []
    for column in range(0, conv_columns, LANES):
        for row in range(0, channels, TILE):
            tiles.append((0, row, column, min(LANES, conv_columns - column)))
    for row in range(0, taps * channels, TILE):
        tiles.append((1, row, 0, LANES))
    return tiles


def padded_halo(halo_refs):
    halo = [h[...] for h in halo_refs]
    width = sum(h.shape[1] for h in halo)
    slack = -width % LANES
    if slack:
        halo.append(jnp.zeros((halo[0].shape[0], slack), BF16))
    return jnp.concatenate(halo, axis=1)


def gather_kernel(slabs, f_ref, near_ref, first_ref, rest_ref):
    channels, voxels = f_ref.shape
    table_t = f_ref[...]
    lanes = table_lanes(near_ref[...], voxels, slabs, 0)
    near_iota = lax.broadcasted_iota(jnp.int32, (voxels, voxels), 0)
    for o in range(near_ref.shape[0]):
        near = jnp.where(near_iota == lanes[o : o + 1, :], 1.0, 0.0).astype(BF16)
        own = mm(table_t, near).astype(BF16)
        first_ref[o * channels : (o + 1) * channels, :] = own[:, :LANES]
        rest_ref[o * channels : (o + 1) * channels, :] = own[:, LANES:]


def taps_kernel(down_ref, cgrad_ref, wd_ref, pick_ref, hgrad_ref):
    channels, voxels = hgrad_ref.shape
    taps, coarse_count = down_ref.shape
    cgrad_t = cgrad_ref[...].astype(F32).T.astype(BF16)
    down = down_ref[...].astype(F32).T
    lane_iota = lax.broadcasted_iota(jnp.int32, (coarse_count, voxels), 1).astype(F32)
    hgrad_t = jnp.zeros((channels, voxels), F32)
    for t in range(taps):
        pick = jnp.where(lane_iota == down[:, t : t + 1], 1.0, 0.0).astype(BF16)
        pick_ref[t] = pick
        wd = wd_ref[t * channels : (t + 1) * channels, :]
        hgrad_t += mm(wd, mm(cgrad_t, pick).astype(BF16))
    hgrad_ref[...] = hgrad_t


def far_one_hots(lanes, rows, voxels, offsets):
    iota = lax.broadcasted_iota(jnp.int32, (rows, LANES), 0) + voxels
    hots = [jnp.where(iota == lanes[o : o + 1, :LANES], 1.0, 0.0).astype(BF16) for o in offsets]
    return jnp.concatenate(hots, axis=1)


def forward_kernel(slabs, core_ref, f_ref, near_ref, cgrad_ref, w_ref, *refs):
    first_ref, rest_ref, pick_ref, hgrad_ref = refs[:4]
    halo_refs, refs = (refs[4:7], refs[7:]) if slabs == 2 else (refs[4:8], refs[8:])
    grad_ref, hidden_ref, *chunks, rt, conv_w, down_w = refs
    channels, voxels = f_ref.shape
    offsets = near_ref.shape[0]
    taps = pick_ref.shape[0]
    conv_columns = offsets * channels
    halo_t = padded_halo(halo_refs)
    lanes = table_lanes(near_ref[:, :LANES], voxels, slabs, core_ref[0])
    for pair in range(0, offsets, 2):
        pair = range(pair, min(pair + 2, offsets))
        away = mm(halo_t, far_one_hots(lanes, halo_t.shape[1], voxels, pair))
        for i, o in enumerate(pair):
            rows = slice(o * channels, (o + 1) * channels)
            first = first_ref[rows, :].astype(F32) + away[:, i * LANES : (i + 1) * LANES]
            rt[rows, :LANES] = first.astype(BF16)
            rt[rows, LANES:] = rest_ref[rows, :]

    out_t = mm(w_ref[...], rt[...])
    sig = 1.0 / (1.0 + jnp.exp(-out_t))
    hidden_t = (f_ref[...].astype(F32) + out_t * sig).astype(BF16)
    grad_t = (hgrad_ref[...] * sig * (1.0 + out_t * (1.0 - sig))).astype(BF16)
    grad_ref[...] = grad_t
    conv_w[:, :conv_columns] = mm(grad_t, rt[...], NT)
    if conv_w.shape[1] > conv_columns:
        slack = conv_w.shape[1] - conv_columns
        conv_w[:, conv_columns:] = jnp.zeros((channels, slack), F32)

    hidden_ref[...] = hidden_t
    cgrad = cgrad_ref[...]
    for t in range(taps):
        picked_t = mm(hidden_t, pick_ref[t], NT).astype(BF16)
        down_w[t * channels : (t + 1) * channels, :] = mm(picked_t, cgrad)

    tiles = payload_tiles(channels, conv_columns, taps)
    count = len(chunks) // 2
    size = chunks[0].shape[0]
    for core in range(2):

        @pl.when(core_ref[0] == core)
        def _(core=core):
            for i in range(2 * count * size):
                half, chunk, place = i // (count * size), i // size % count, i % size
                ref = chunks[2 * chunk + (half != core)]
                if i < len(tiles):
                    kind, row, column, _ = tiles[i]
                    source = down_w if kind else conv_w
                    value = source[row : row + TILE, column : column + LANES]
                else:
                    value = jnp.zeros((TILE, LANES), F32)
                ref[place] = value.astype(ref.dtype)


def coarse_kernel(pick_ref, hidden_ref, wd_ref, coarse_ref):
    channels = hidden_ref.shape[0]
    coarse = jnp.zeros(coarse_ref.shape, F32)
    for t in range(pick_ref.shape[0]):
        picked = mm(pick_ref[t], hidden_ref[...], NT).astype(BF16)
        coarse += mm(picked, wd_ref[t * channels : (t + 1) * channels, :])
    coarse_ref[...] = coarse.astype(BF16)


def backward_kernel(slabs, core_ref, near_ref, hgrad_ref, grad_ref, w_ref, *refs):
    base_ref, mate_ref, first_ref, second_ref, drt, drt_far, hot, far, w_back = refs
    channels, voxels = hgrad_ref.shape
    offsets = near_ref.shape[0]
    lanes = table_lanes(near_ref[...], voxels, slabs, core_ref[0])
    near_iota = lax.broadcasted_iota(jnp.int32, (voxels, voxels), 0)
    w_back[:, :channels] = w_ref[...].astype(F32).T.astype(BF16)
    w_back[:, channels:] = jnp.zeros((offsets * channels, LANES - channels), BF16)
    slack = jnp.zeros((LANES - channels, voxels), BF16)
    grad_pad = jnp.concatenate([grad_ref[...], slack], axis=0)
    for o in range(offsets):
        near = jnp.where(near_iota == lanes[o : o + 1, :], 1.0, 0.0).astype(BF16)
        hot[:, o * voxels : (o + 1) * voxels] = near
        spread = mm(w_back[o * channels : (o + 1) * channels, :], grad_pad).astype(BF16)
        drt[:, o * voxels : (o + 1) * voxels] = spread
        drt_far[:, o * LANES : (o + 1) * LANES] = spread[:, :LANES]
        far[:, o * LANES : (o + 1) * LANES] = far_one_hots(lanes, far.shape[0], voxels, (o,))
    base_ref[...] = hgrad_ref[...] + mm(drt[...], hot[...], NT)
    back_t = mm(drt_far[...], far[...], NT)
    rims = 2 if slabs == 2 else 3
    rim = [back_t[:, i * RIM : (i + 1) * RIM] for i in range(back_t.shape[1] // RIM)]
    mate, cross, side = rim[:rims], rim[rims : 2 * rims], rim[2 * rims : 3 * rims - 1]
    if slabs == 2:
        mate_ref[...] = mate[0]
        slots = [cross[0], cross[1], mate[1], side[0]]
    else:
        mate_ref[...] = mate[1]
        slots = [cross[1], cross[0], cross[2], jnp.zeros_like(cross[0])]
        slots += [mate[0], mate[2], side[0], side[1]]
    pairs = [jnp.concatenate(slots[i : i + 2], axis=1).astype(BF16) for i in range(0, len(slots), 2)]
    rows = channels // TILE
    for ref, part in ((first_ref, pairs[: len(pairs) // 2]), (second_ref, pairs[len(pairs) // 2 :])):
        for i, pair in enumerate(part):
            for j in range(rows):
                ref[i * rows + j] = pair[j * TILE : (j + 1) * TILE, :]


def slot_table(slabs):
    if slabs == 2:
        return [("cross", 1, 0), ("cross", 1, 1), ("mate", 0, 1), ("side", 0, 1)]
    table = [("cross", 1, 0), ("cross", 1, -1), ("cross", 1, 1), ("none", 0, 0)]
    return table + [("mate", 0, -1), ("mate", 0, 1), ("side", 0, -1), ("side", 0, 1)]


def place_of(me, sizes):
    place = {}
    for axis in reversed(SPLIT):
        place[axis] = me & (sizes[axis] - 1)
        me = me >> (sizes[axis].bit_length() - 1)
    return place


def goes(slot, axis, bit, place, sizes):
    _, chips, step = slot
    low = (1 << bit) - 1
    yes, no = jnp.int32(1), jnp.int32(0)
    if axis == "far":
        if not chips:
            return no
        far = place["far"] & low
        up = (place["near"] == 1) & (far == 0)
        down = (place["near"] == 0) & (far == low)
        return jnp.where(place["core"] == 1, up.astype(jnp.int32), down.astype(jnp.int32))
    if axis == "near":
        return yes if chips else no
    if step == 0:
        return no
    if sizes["slab"] == 2:
        return yes
    return ((place["slab"] & low) == (0 if step > 0 else low)).astype(jnp.int32)


def chosen_bit(choice, place):
    return jnp.where(place["core"] == 0, *[(place[axis] >> bit) & 1 for axis, bit in choice])


def riders_after(choice, sizes, place, rows, mine, got):
    slots = slot_table(sizes["slab"])
    lane = lax.broadcasted_iota(jnp.int32, (TILE, LANES), 1)
    masks = []
    for i in range(0, len(slots), 2):
        flags = []
        for slot in slots[i : i + 2]:
            each = [goes(slot, axis, bit, place, sizes) for axis, bit in choice]
            flags.append(jnp.where(place["core"] == 0, *each))
        masks.append(jnp.where(lane < RIM, flags[0], flags[1]) > 0)
    return [
        jnp.where(masks[i // rows], got[i].astype(F32), mine[i].astype(F32))
        for i in range(mine.shape[0])
    ]


def close_kernel(keep_ref, got_ref, *refs):
    riders, full_ref = refs[:-1], refs[-1]
    count = keep_ref.shape[0]
    full_ref[:count] = (keep_ref[...] + got_ref[...].astype(F32)).astype(BF16)
    for rider in riders:
        full_ref[count : count + rider.shape[0]] = rider[...]
        count += rider.shape[0]


def meet_kernel(choice, sizes, rows, count, me_ref, own_ref, got_ref, *refs):
    riders, full_ref = refs[:-1], refs[-1]
    place = place_of(me_ref[0], sizes)
    total = own_ref[:count].astype(F32) + got_ref[:count].astype(F32)
    full_ref[:count] = total.astype(BF16)
    parts = riders_after(choice, sizes, place, rows, own_ref.at[count:], got_ref.at[count:])
    for part in parts:
        full_ref[count] = part.astype(BF16)
        count += 1
    for rider in riders:
        full_ref[count : count + rider.shape[0]] = rider[...]


def fold_kernel(choice, sizes, me_ref, own_ref, got_ref, keep_ref, send_ref):
    half = keep_ref.shape[0]
    bit = chosen_bit(choice, place_of(me_ref[0], sizes))
    for ref, part in ((keep_ref, bit), (send_ref, 1 - bit)):
        rows = pl.ds(part * half, half)
        ref[...] = (own_ref[rows] + got_ref[rows].astype(F32)).astype(ref.dtype)


def join_kernel(choice, sizes, rows, half, last, me_ref, own_ref, got_ref, *refs):
    full_ref = refs[1] if last else refs[0]
    place = place_of(me_ref[0], sizes)
    bit = chosen_bit(choice, place)
    full_ref[pl.ds(bit * half, half)] = own_ref[:half]
    full_ref[pl.ds((1 - bit) * half, half)] = got_ref[:half]
    if own_ref.shape[0] == half:
        return
    parts = riders_after(choice, sizes, place, rows, own_ref.at[half:], got_ref.at[half:])
    if not last:
        for i, part in enumerate(parts):
            full_ref[2 * half + i] = part.astype(BF16)
        return
    mate_ref, side_ref = refs[0], refs[2]
    for j in range(rows):
        mate, side = mate_ref[j * TILE : (j + 1) * TILE, :], jnp.zeros((TILE, RIM), F32)
        for i, (kind, _, _) in enumerate(slot_table(sizes["slab"])):
            value = parts[i // 2 * rows + j][:, i % 2 * RIM : (i % 2 + 1) * RIM]
            if kind == "side":
                side += value
            elif kind != "none":
                mate += value
        pair = jnp.concatenate([mate, jnp.zeros_like(mate)], axis=1)
        full_ref[2 * half + j] = pair.astype(BF16)
        side_ref[j * TILE : (j + 1) * TILE, :] = side


def final_kernel(taps, count, size, core_ref, *refs):
    mine, other, refs = refs[:count], refs[count : 2 * count], refs[2 * count :]
    base_ref, side_ref, conv_ref, down_ref, grad_ref = refs
    channels, conv_columns = conv_ref.shape
    grad_ref[:, RIM:] = base_ref[:, RIM:]
    for i in range(channels // TILE):
        rows = slice(i * TILE, (i + 1) * TILE)
        total = base_ref[rows, :RIM] + side_ref[rows, :]
        grad_ref[rows, :RIM] = total + other[0][size + i][:, :RIM].astype(F32)
    for core in range(2):

        @pl.when(core_ref[0] == core)
        def _(core=core):
            for i, tile in enumerate(payload_tiles(channels, conv_columns, taps)):
                kind, row, column, columns = tile
                source = mine if i // (count * size) == core else other
                value = source[i // size % count][i % size].astype(F32)
                target = down_ref if kind else conv_ref
                target[row : row + TILE, column : column + columns] = value[:, :columns]


def shifts(count, step):
    return [(i, i + step) for i in range(count) if 0 <= i + step < count]


def chip_pairs(regions):
    mates = [(i, i ^ 1) for i in range(regions)]
    cross = [(i, i + 1) for i in range(1, regions - 1, 2)]
    return mates, cross + [(b, a) for a, b in cross]


def square_bits(nears, slabs, core):
    near = [("near", i) for i in range(nears.bit_length() - 1)]
    slab = [("slab", i) for i in reversed(range(slabs.bit_length() - 1))]
    return near + slab if core == 0 else slab + near


def bit_pairs(sizes, orders, phase):
    pairs = []
    for index in range(functools.reduce(lambda a, b: a * b, sizes.values())):
        place, left = {}, index
        for axis in reversed(SPLIT):
            left, place[axis] = divmod(left, sizes[axis])
        axis, bit = orders[place["core"]][phase]
        place[axis] ^= 1 << bit
        other = 0
        for name in SPLIT:
            other = other * sizes[name] + place[name]
        pairs.append((index, other))
    return pairs


def on_device(features, neighbours, down_map, w_conv, w_down, coarse_grad):
    sizes = {axis: lax.axis_size(axis) for axis in SPLIT}
    regions, slabs = sizes["far"] * sizes["near"] * sizes["core"], sizes["slab"]
    voxels, channels = features.shape
    offsets, taps = neighbours.shape[1], down_map.shape[1]
    conv_columns = offsets * channels
    core = lax.axis_index("core").astype(jnp.int32).reshape(1)
    swap = [(0, 1), (1, 0)]
    mates, crossings = chip_pairs(regions)
    orders = [square_bits(sizes["near"], slabs, c) for c in range(2)]
    phases = len(orders[0])
    me = lax.axis_index(SPLIT).astype(jnp.int32).reshape(1)
    choices = [tuple(order[phase] for order in orders) for phase in range(phases)]
    smem = pl.BlockSpec(memory_space=pltpu.SMEM)
    vmem = pl.BlockSpec(memory_space=pltpu.VMEM)
    params = pltpu.CompilerParams(vmem_limit_bytes=VMEM_BYTES)
    light = pl.CostEstimate(flops=2 * 10**9, bytes_accessed=10**7, transcendentals=0)
    features_t, neighbours_t, w_conv_t = features.T, neighbours.T, w_conv.T
    rim = features_t[:, :RIM]
    if slabs == 2:
        beside = [swap]
    else:
        beside = [shifts(slabs, 1), shifts(slabs, -1)]
    side = [lax.ppermute(rim, "slab", pairs) for pairs in beside]
    own = pl.pallas_call(
        functools.partial(gather_kernel, slabs),
        out_shape=(
            jax.ShapeDtypeStruct((conv_columns, LANES), BF16),
            jax.ShapeDtypeStruct((conv_columns, voxels - LANES), BF16),
        ),
        compiler_params=params,
        cost_estimate=light,
        name="gather",
    )(features_t, neighbours_t)
    side, own = lax.optimization_barrier((side, own))
    row = [rim, side[0]] if slabs == 2 else [side[0], rim, side[1]]
    row = jnp.concatenate(row, axis=1)
    cross = lax.ppermute(row, RING, crossings)
    mate = lax.ppermute(row, RING, mates)
    row, down_t = lax.optimization_barrier((row, down_map.T))
    pick, hgrad = pl.pallas_call(
        taps_kernel,
        out_shape=(
            jax.ShapeDtypeStruct((taps, coarse_grad.shape[0], voxels), BF16),
            jax.ShapeDtypeStruct((channels, voxels), F32),
        ),
        compiler_params=params,
        cost_estimate=light,
        name="taps",
    )(down_t, coarse_grad, w_down)
    halos = [mate, cross, *side]
    far_rows = -(-sum(x.shape[1] for x in halos) // LANES) * LANES

    tiles = len(payload_tiles(channels, conv_columns, taps))
    size = -(-tiles // (2 * CHUNKS << phases)) << phases
    grad, hidden, *chunks = pl.pallas_call(
        functools.partial(forward_kernel, slabs),
        out_shape=[
            jax.ShapeDtypeStruct((channels, voxels), BF16),
            jax.ShapeDtypeStruct((channels, voxels), BF16),
        ]
        + [jax.ShapeDtypeStruct((size, TILE, LANES), kind) for kind in (F32, BF16)] * CHUNKS,
        in_specs=[smem] + [vmem] * (8 + len(halos)),
        scratch_shapes=[
            pltpu.VMEM((conv_columns, voxels), BF16),
            pltpu.VMEM((channels, -(-conv_columns // LANES) * LANES), F32),
            pltpu.VMEM((taps * channels, LANES), F32),
        ],
        compiler_params=params,
        name="forward",
    )(core, features_t, neighbours_t, coarse_grad, w_conv_t, *own, pick, hgrad, *halos)

    rows = channels // TILE

    def tile_shape(count, kind=BF16):
        return jax.ShapeDtypeStruct((count, TILE, LANES), kind)

    def call(name, kernel, out_shape, *operands):
        return pl.pallas_call(
            kernel,
            out_shape=out_shape,
            in_specs=[smem] + [vmem] * (len(operands) - 1),
            compiler_params=params,
            name=name,
        )(*operands)

    def fold(phase, keep, got):
        half = keep.shape[0] // 2
        kernel = functools.partial(fold_kernel, choices[phase], sizes)
        return call("fold", kernel, (tile_shape(half, F32), tile_shape(half)), me, keep, got)

    keep, send = chunks[0::2], chunks[1::2]
    got = [lax.ppermute(x, "core", swap) for x in send]
    for phase in range(phases):
        pairs = bit_pairs(sizes, orders, phase)
        for i in range(CHUNKS):
            keep[i], send[i] = fold(phase, keep[i], got[i])
            if i == CHUNKS - 1 and phase == 0:
                send[i], grad = lax.optimization_barrier((send[i], grad))
            got[i] = lax.ppermute(send[i], SPLIT, pairs)
        if phase == 0:
            slots = len(slot_table(slabs)) // 4 * rows
            base, stay, *riders = pl.pallas_call(
                functools.partial(backward_kernel, slabs),
                out_shape=(
                    jax.ShapeDtypeStruct((channels, voxels), F32),
                    jax.ShapeDtypeStruct((channels, RIM), F32),
                    tile_shape(slots),
                    tile_shape(slots),
                ),
                in_specs=[smem] + [vmem] * 4,
                scratch_shapes=[
                    pltpu.VMEM((channels, offsets * voxels), BF16),
                    pltpu.VMEM((channels, offsets * LANES), BF16),
                    pltpu.VMEM((voxels, offsets * voxels), BF16),
                    pltpu.VMEM((far_rows, offsets * LANES), BF16),
                    pltpu.VMEM((conv_columns, LANES), BF16),
                ],
                compiler_params=params,
                cost_estimate=light,
                name="backward",
            )(core, neighbours_t, hgrad, grad, w_conv_t)
            got[0], stay, riders, base = lax.optimization_barrier((got[0], stay, riders, base))
        if phase == phases - 1:
            coarse = pl.pallas_call(
                coarse_kernel,
                out_shape=jax.ShapeDtypeStruct(coarse_grad.shape, BF16),
                compiler_params=params,
                cost_estimate=light,
                name="coarse",
            )(pick, hidden, w_down)

    far_bits = sizes["far"].bit_length() - 1
    count = keep[0].shape[0]
    first = riders[:1] if far_bits else riders
    total = [(x + y.astype(F32)).astype(BF16) for x, y in zip(keep, got)]
    total[0] = pl.pallas_call(
        close_kernel,
        out_shape=tile_shape(count + sum(x.shape[0] for x in first)),
        compiler_params=params,
        name="close",
    )(keep[0], got[0], *first)
    for bit in range(far_bits):
        pairs = [(i, i ^ (1 << bit)) for i in range(sizes["far"])]
        got = [lax.ppermute(x, "far", pairs) for x in total]
        more = riders[1:] if bit == far_bits - 1 else []
        kernel = functools.partial(meet_kernel, (("far", bit),) * 2, sizes, rows, count)
        shape = tile_shape(total[0].shape[0] + sum(x.shape[0] for x in more))
        carried = call("meet", kernel, shape, me, total[0], got[0], *more)
        total = [(x.astype(F32) + y.astype(F32)).astype(BF16) for x, y in zip(total, got)]
        total[0] = carried
    for phase in reversed(range(phases)):
        pairs = bit_pairs(sizes, orders, phase)
        got = [lax.ppermute(x, SPLIT, pairs) for x in total]
        for i in range(CHUNKS):
            last = i == 0 and phase == 0
            kernel = functools.partial(join_kernel, choices[phase], sizes, rows, count, last)
            if last:
                shape = (tile_shape(2 * count + rows), jax.ShapeDtypeStruct((channels, RIM), F32))
                total[0], side = call("join", kernel, shape, me, total[0], got[0], stay)
            else:
                shape = tile_shape(total[i].shape[0] + count)
                total[i] = call("join", kernel, shape, me, total[i], got[i])
        count *= 2
    other = [lax.ppermute(x, "core", swap) for x in total]
    conv_wgrad_t, down_wgrad, grad_input_t = pl.pallas_call(
        functools.partial(final_kernel, taps, CHUNKS, size),
        out_shape=(
            jax.ShapeDtypeStruct((channels, conv_columns), F32),
            jax.ShapeDtypeStruct((taps * channels, LANES), F32),
            jax.ShapeDtypeStruct((channels, voxels), F32),
        ),
        in_specs=[smem] + [vmem] * (2 * CHUNKS + 2),
        compiler_params=params,
        name="final",
    )(core, *total, *other, base, side)
    return coarse, grad_input_t.T, conv_wgrad_t.T, down_wgrad


def solution(mesh):
    regions, slabs = mesh.shape["region"], mesh.shape["slab"]
    fine = Mesh(mesh.devices.reshape(regions // 4, 2, 2, slabs), SPLIT)
    split = P(SPLIT, None)
    return jax.shard_map(
        on_device,
        mesh=fine,
        in_specs=(split, split, split, P(), P(), split),
        out_specs=(split, split, P(), P()),
        check_vma=False,
    )
```

```python
import functools

import jax
import jax.numpy as jnp
from jax import lax
from jax.experimental import pallas as pl
from jax.experimental.pallas import tpu as pltpu
from jax.sharding import Mesh, PartitionSpec as P

SPLIT = ("far", "near", "core", "slab")
RING = ("far", "near", "core")
RIM = 64
LANES = 128
TILE = 16
EXTRA = 0.27
F32 = jnp.float32
BF16 = jnp.bfloat16
NN = (((1,), (0,)), ((), ()))
NT = (((1,), (1,)), ((), ()))
VMEM_BYTES = 20 * 2**20


def mm(a, b, dims=NN):
    return lax.dot_general(a, b, dims, preferred_element_type=F32)


def table_lanes(neighbours, voxels, slabs, core):
    code = neighbours // voxels
    slot = neighbours - code * voxels
    row = code // 3
    col = code - row * 3
    if slabs == 2:
        rims = 2
        place = jnp.where(col == 1, 0, 1)
        beside = 0
    else:
        rims = 3
        place = col
        beside = col // 2
    group = jnp.abs(row // 2 + core - 1)
    rim = jnp.where(row == 1, 2 * rims + beside, group * rims + place)
    lane = jnp.where(code == 4, slot, voxels + rim * RIM + slot)
    return jnp.where(code > 8, -1, lane)


def payload_tiles(channels, conv_columns, taps):
    tiles = []
    for column in range(0, conv_columns, LANES):
        for row in range(0, channels, TILE):
            tiles.append((0, row, column, min(LANES, conv_columns - column)))
    for row in range(0, taps * channels, TILE):
        tiles.append((1, row, 0, LANES))
    return tiles


def padded_halo(halo_refs):
    halo = [h[...] for h in halo_refs]
    width = sum(h.shape[1] for h in halo)
    slack = -width % LANES
    if slack:
        halo.append(jnp.zeros((halo[0].shape[0], slack), BF16))
    return jnp.concatenate(halo, axis=1)


def gather_kernel(slabs, f_ref, near_ref, first_ref, rest_ref):
    channels, voxels = f_ref.shape
    table_t = f_ref[...]
    lanes = table_lanes(near_ref[...], voxels, slabs, 0)
    near_iota = lax.broadcasted_iota(jnp.int32, (voxels, voxels), 0)
    for o in range(near_ref.shape[0]):
        near = jnp.where(near_iota == lanes[o : o + 1, :], 1.0, 0.0).astype(BF16)
        own = mm(table_t, near).astype(BF16)
        first_ref[o * channels : (o + 1) * channels, :] = own[:, :LANES]
        rest_ref[o * channels : (o + 1) * channels, :] = own[:, LANES:]


def taps_kernel(down_ref, cgrad_ref, wd_ref, pick_ref, hgrad_ref):
    channels, voxels = hgrad_ref.shape
    taps, coarse_count = down_ref.shape
    cgrad_t = cgrad_ref[...].astype(F32).T.astype(BF16)
    down = down_ref[...].astype(F32).T
    lane_iota = lax.broadcasted_iota(jnp.int32, (coarse_count, voxels), 1).astype(F32)
    hgrad_t = jnp.zeros((channels, voxels), F32)
    for t in range(taps):
        pick = jnp.where(lane_iota == down[:, t : t + 1], 1.0, 0.0).astype(BF16)
        pick_ref[t] = pick
        wd = wd_ref[t * channels : (t + 1) * channels, :]
        hgrad_t += mm(wd, mm(cgrad_t, pick).astype(BF16))
    hgrad_ref[...] = hgrad_t


def far_one_hots(lanes, rows, voxels, offsets):
    iota = lax.broadcasted_iota(jnp.int32, (rows, LANES), 0) + voxels
    hots = [jnp.where(iota == lanes[o : o + 1, :LANES], 1.0, 0.0).astype(BF16) for o in offsets]
    return jnp.concatenate(hots, axis=1)


def forward_kernel(slabs, core_ref, f_ref, near_ref, cgrad_ref, w_ref, *refs):
    first_ref, rest_ref, pick_ref, hgrad_ref = refs[:4]
    halo_refs, refs = (refs[4:7], refs[7:]) if slabs == 2 else (refs[4:8], refs[8:])
    grad_ref, hidden_ref, keep_ref, send_ref, more_keep_ref, more_send_ref, *refs = refs
    rt, conv_w, down_w = refs
    channels, voxels = f_ref.shape
    offsets = near_ref.shape[0]
    taps = pick_ref.shape[0]
    conv_columns = offsets * channels
    halo_t = padded_halo(halo_refs)
    lanes = table_lanes(near_ref[:, :LANES], voxels, slabs, core_ref[0])
    for pair in range(0, offsets, 2):
        pair = range(pair, min(pair + 2, offsets))
        away = mm(halo_t, far_one_hots(lanes, halo_t.shape[1], voxels, pair))
        for i, o in enumerate(pair):
            rows = slice(o * channels, (o + 1) * channels)
            first = first_ref[rows, :].astype(F32) + away[:, i * LANES : (i + 1) * LANES]
            rt[rows, :LANES] = first.astype(BF16)
            rt[rows, LANES:] = rest_ref[rows, :]

    out_t = mm(w_ref[...], rt[...])
    sig = 1.0 / (1.0 + jnp.exp(-out_t))
    hidden_t = (f_ref[...].astype(F32) + out_t * sig).astype(BF16)
    grad_t = (hgrad_ref[...] * sig * (1.0 + out_t * (1.0 - sig))).astype(BF16)
    grad_ref[...] = grad_t
    conv_w[:, :conv_columns] = mm(grad_t, rt[...], NT)
    if conv_w.shape[1] > conv_columns:
        slack = conv_w.shape[1] - conv_columns
        conv_w[:, conv_columns:] = jnp.zeros((channels, slack), F32)

    hidden_ref[...] = hidden_t
    cgrad = cgrad_ref[...]
    for t in range(taps):
        picked_t = mm(hidden_t, pick_ref[t], NT).astype(BF16)
        down_w[t * channels : (t + 1) * channels, :] = mm(picked_t, cgrad)

    tiles = payload_tiles(channels, conv_columns, taps)
    shared = keep_ref.shape[0]
    for core in range(2):

        @pl.when(core_ref[0] == core)
        def _(core=core):
            for i in range(2 * shared + more_keep_ref.shape[0]):
                if i < 2 * shared:
                    ref, place = keep_ref if i // shared == core else send_ref, i % shared
                else:
                    ref, place = more_keep_ref if core else more_send_ref, i - 2 * shared
                if i < len(tiles):
                    kind, row, column, _ = tiles[i]
                    source = down_w if kind else conv_w
                    value = source[row : row + TILE, column : column + LANES]
                else:
                    value = jnp.zeros((TILE, LANES), F32)
                ref[place] = value.astype(ref.dtype)


def coarse_kernel(pick_ref, hidden_ref, wd_ref, coarse_ref):
    channels = hidden_ref.shape[0]
    coarse = jnp.zeros(coarse_ref.shape, F32)
    for t in range(pick_ref.shape[0]):
        picked = mm(pick_ref[t], hidden_ref[...], NT).astype(BF16)
        coarse += mm(picked, wd_ref[t * channels : (t + 1) * channels, :])
    coarse_ref[...] = coarse.astype(BF16)


def backward_kernel(slabs, core_ref, near_ref, hgrad_ref, grad_ref, w_ref, *refs):
    base_ref, mate_ref, first_ref, second_ref, drt, drt_far, hot, far, w_back = refs
    channels, voxels = hgrad_ref.shape
    offsets = near_ref.shape[0]
    lanes = table_lanes(near_ref[...], voxels, slabs, core_ref[0])
    near_iota = lax.broadcasted_iota(jnp.int32, (voxels, voxels), 0)
    w_back[:, :channels] = w_ref[...].astype(F32).T.astype(BF16)
    w_back[:, channels:] = jnp.zeros((offsets * channels, LANES - channels), BF16)
    slack = jnp.zeros((LANES - channels, voxels), BF16)
    grad_pad = jnp.concatenate([grad_ref[...], slack], axis=0)
    for o in range(offsets):
        near = jnp.where(near_iota == lanes[o : o + 1, :], 1.0, 0.0).astype(BF16)
        hot[:, o * voxels : (o + 1) * voxels] = near
        spread = mm(w_back[o * channels : (o + 1) * channels, :], grad_pad).astype(BF16)
        drt[:, o * voxels : (o + 1) * voxels] = spread
        drt_far[:, o * LANES : (o + 1) * LANES] = spread[:, :LANES]
        far[:, o * LANES : (o + 1) * LANES] = far_one_hots(lanes, far.shape[0], voxels, (o,))
    base_ref[...] = hgrad_ref[...] + mm(drt[...], hot[...], NT)
    back_t = mm(drt_far[...], far[...], NT)
    rims = 2 if slabs == 2 else 3
    rim = [back_t[:, i * RIM : (i + 1) * RIM] for i in range(back_t.shape[1] // RIM)]
    mate, cross, side = rim[:rims], rim[rims : 2 * rims], rim[2 * rims : 3 * rims - 1]
    if slabs == 2:
        mate_ref[...] = mate[0]
        slots = [cross[0], cross[1], mate[1], side[0]]
    else:
        mate_ref[...] = mate[1]
        slots = [cross[1], cross[0], cross[2], jnp.zeros_like(cross[0])]
        slots += [mate[0], mate[2], side[0], side[1]]
    pairs = [jnp.concatenate(slots[i : i + 2], axis=1).astype(BF16) for i in range(0, len(slots), 2)]
    rows = channels // TILE
    for ref, part in ((first_ref, pairs[: len(pairs) // 2]), (second_ref, pairs[len(pairs) // 2 :])):
        for i, pair in enumerate(part):
            for j in range(rows):
                ref[i * rows + j] = pair[j * TILE : (j + 1) * TILE, :]


def slot_table(slabs):
    if slabs == 2:
        return [("cross", 1, 0), ("cross", 1, 1), ("mate", 0, 1), ("side", 0, 1)]
    table = [("cross", 1, 0), ("cross", 1, -1), ("cross", 1, 1), ("none", 0, 0)]
    return table + [("mate", 0, -1), ("mate", 0, 1), ("side", 0, -1), ("side", 0, 1)]


def place_of(me, sizes):
    place = {}
    for axis in reversed(SPLIT):
        place[axis] = me & (sizes[axis] - 1)
        me = me >> (sizes[axis].bit_length() - 1)
    return place


def goes(slot, axis, bit, place, sizes):
    _, chips, step = slot
    low = (1 << bit) - 1
    yes, no = jnp.int32(1), jnp.int32(0)
    if axis == "far":
        if not chips:
            return no
        far = place["far"] & low
        up = (place["near"] == 1) & (far == 0)
        down = (place["near"] == 0) & (far == low)
        return jnp.where(place["core"] == 1, up.astype(jnp.int32), down.astype(jnp.int32))
    if axis == "near":
        return yes if chips else no
    if step == 0:
        return no
    if sizes["slab"] == 2:
        return yes
    return ((place["slab"] & low) == (0 if step > 0 else low)).astype(jnp.int32)


def chosen_bit(choice, place):
    return jnp.where(place["core"] == 0, *[(place[axis] >> bit) & 1 for axis, bit in choice])


def riders_after(choice, sizes, place, rows, mine, got):
    slots = slot_table(sizes["slab"])
    lane = lax.broadcasted_iota(jnp.int32, (TILE, LANES), 1)
    masks = []
    for i in range(0, len(slots), 2):
        flags = []
        for slot in slots[i : i + 2]:
            each = [goes(slot, axis, bit, place, sizes) for axis, bit in choice]
            flags.append(jnp.where(place["core"] == 0, *each))
        masks.append(jnp.where(lane < RIM, flags[0], flags[1]) > 0)
    return [
        jnp.where(masks[i // rows], got[i].astype(F32), mine[i].astype(F32))
        for i in range(mine.shape[0])
    ]


def close_kernel(keep_ref, got_ref, *refs):
    riders, full_ref = refs[:-1], refs[-1]
    count = keep_ref.shape[0]
    full_ref[:count] = (keep_ref[...] + got_ref[...].astype(F32)).astype(BF16)
    for rider in riders:
        full_ref[count : count + rider.shape[0]] = rider[...]
        count += rider.shape[0]


def meet_kernel(choice, sizes, rows, count, me_ref, own_ref, got_ref, *refs):
    riders, full_ref = refs[:-1], refs[-1]
    place = place_of(me_ref[0], sizes)
    total = own_ref[:count].astype(F32) + got_ref[:count].astype(F32)
    full_ref[:count] = total.astype(BF16)
    parts = riders_after(choice, sizes, place, rows, own_ref.at[count:], got_ref.at[count:])
    for part in parts:
        full_ref[count] = part.astype(BF16)
        count += 1
    for rider in riders:
        full_ref[count : count + rider.shape[0]] = rider[...]


def fold_kernel(choice, sizes, me_ref, own_ref, got_ref, keep_ref, send_ref):
    half = keep_ref.shape[0]
    bit = chosen_bit(choice, place_of(me_ref[0], sizes))
    for ref, part in ((keep_ref, bit), (send_ref, 1 - bit)):
        rows = pl.ds(part * half, half)
        ref[...] = (own_ref[rows] + got_ref[rows].astype(F32)).astype(ref.dtype)


def join_kernel(choice, sizes, rows, half, last, me_ref, own_ref, got_ref, *refs):
    full_ref = refs[1] if last else refs[0]
    place = place_of(me_ref[0], sizes)
    bit = chosen_bit(choice, place)
    full_ref[pl.ds(bit * half, half)] = own_ref[:half]
    full_ref[pl.ds((1 - bit) * half, half)] = got_ref[:half]
    if own_ref.shape[0] == half:
        return
    parts = riders_after(choice, sizes, place, rows, own_ref.at[half:], got_ref.at[half:])
    if not last:
        for i, part in enumerate(parts):
            full_ref[2 * half + i] = part.astype(BF16)
        return
    mate_ref, side_ref = refs[0], refs[2]
    for j in range(rows):
        mate, side = mate_ref[j * TILE : (j + 1) * TILE, :], jnp.zeros((TILE, RIM), F32)
        for i, (kind, _, _) in enumerate(slot_table(sizes["slab"])):
            value = parts[i // 2 * rows + j][:, i % 2 * RIM : (i % 2 + 1) * RIM]
            if kind == "side":
                side += value
            elif kind != "none":
                mate += value
        pair = jnp.concatenate([mate, jnp.zeros_like(mate)], axis=1)
        full_ref[2 * half + j] = pair.astype(BF16)
        side_ref[j * TILE : (j + 1) * TILE, :] = side


def final_kernel(taps, shared, core_ref, *refs):
    mine_ref, more_ref, other_ref, other_more_ref, base_ref, side_ref, *refs = refs
    conv_ref, down_ref, grad_ref = refs
    channels, conv_columns = conv_ref.shape
    grad_ref[:, RIM:] = base_ref[:, RIM:]
    for i in range(channels // TILE):
        rows = slice(i * TILE, (i + 1) * TILE)
        total = base_ref[rows, :RIM] + side_ref[rows, :]
        grad_ref[rows, :RIM] = total + other_ref[shared + i][:, :RIM].astype(F32)
    for core in range(2):

        @pl.when(core_ref[0] == core)
        def _(core=core):
            for i, tile in enumerate(payload_tiles(channels, conv_columns, taps)):
                kind, row, column, columns = tile
                if i < 2 * shared:
                    value = (mine_ref if i // shared == core else other_ref)[i % shared]
                else:
                    value = (more_ref if core else other_more_ref)[i - 2 * shared]
                target = down_ref if kind else conv_ref
                value = value.astype(F32)[:, :columns]
                target[row : row + TILE, column : column + columns] = value


def shifts(count, step):
    return [(i, i + step) for i in range(count) if 0 <= i + step < count]


def chip_pairs(regions):
    mates = [(i, i ^ 1) for i in range(regions)]
    cross = [(i, i + 1) for i in range(1, regions - 1, 2)]
    return mates, cross + [(b, a) for a, b in cross]


def square_bits(nears, slabs, core):
    near = [("near", i) for i in range(nears.bit_length() - 1)]
    slab = [("slab", i) for i in reversed(range(slabs.bit_length() - 1))]
    return near + slab if core == 0 else slab + near


def bit_pairs(sizes, choice, cores):
    pairs = []
    for index in range(functools.reduce(lambda a, b: a * b, sizes.values())):
        place, left = {}, index
        for axis in reversed(SPLIT):
            left, place[axis] = divmod(left, sizes[axis])
        if place["core"] not in cores:
            continue
        axis, bit = choice[place["core"]]
        place[axis] ^= 1 << bit
        other = 0
        for name in SPLIT:
            other = other * sizes[name] + place[name]
        pairs.append((index, other))
    return pairs


def on_device(features, neighbours, down_map, w_conv, w_down, coarse_grad):
    sizes = {axis: lax.axis_size(axis) for axis in SPLIT}
    regions, slabs = sizes["far"] * sizes["near"] * sizes["core"], sizes["slab"]
    voxels, channels = features.shape
    offsets, taps = neighbours.shape[1], down_map.shape[1]
    conv_columns = offsets * channels
    core = lax.axis_index("core").astype(jnp.int32).reshape(1)
    swap = [(0, 1), (1, 0)]
    mates, crossings = chip_pairs(regions)
    orders = [square_bits(sizes["near"], slabs, c) for c in range(2)]
    phases = len(orders[0])
    me = lax.axis_index(SPLIT).astype(jnp.int32).reshape(1)
    choices = [tuple(order[phase] for order in orders) for phase in range(phases)]
    smem = pl.BlockSpec(memory_space=pltpu.SMEM)
    vmem = pl.BlockSpec(memory_space=pltpu.VMEM)
    params = pltpu.CompilerParams(vmem_limit_bytes=VMEM_BYTES)
    light = pl.CostEstimate(flops=2 * 10**9, bytes_accessed=10**7, transcendentals=0)
    features_t, neighbours_t, w_conv_t = features.T, neighbours.T, w_conv.T
    rim = features_t[:, :RIM]
    if slabs == 2:
        beside = [swap]
    else:
        beside = [shifts(slabs, 1), shifts(slabs, -1)]
    side = [lax.ppermute(features_t, "slab", pairs) for pairs in beside]
    own = pl.pallas_call(
        functools.partial(gather_kernel, slabs),
        out_shape=(
            jax.ShapeDtypeStruct((conv_columns, LANES), BF16),
            jax.ShapeDtypeStruct((conv_columns, voxels - LANES), BF16),
        ),
        compiler_params=params,
        cost_estimate=light,
        name="gather",
    )(features_t, neighbours_t)
    side, own = lax.optimization_barrier((side, own))
    side = [x[:, :RIM] for x in side]
    row = [rim, side[0]] if slabs == 2 else [side[0], rim, side[1]]
    row = jnp.concatenate(row, axis=1)
    cross = lax.ppermute(row, RING, crossings)
    mate = lax.ppermute(row, RING, mates)
    row, down_t = lax.optimization_barrier((row, down_map.T))
    pick, hgrad = pl.pallas_call(
        taps_kernel,
        out_shape=(
            jax.ShapeDtypeStruct((taps, coarse_grad.shape[0], voxels), BF16),
            jax.ShapeDtypeStruct((channels, voxels), F32),
        ),
        compiler_params=params,
        cost_estimate=light,
        name="taps",
    )(down_t, coarse_grad, w_down)
    halos = [mate, cross, *side]
    far_rows = -(-sum(x.shape[1] for x in halos) // LANES) * LANES

    tiles = len(payload_tiles(channels, conv_columns, taps))
    more = round(tiles * EXTRA / (1 << phases)) << phases
    shared = -(-(tiles - more) // (2 << phases)) << phases
    grad, hidden, *chunks = pl.pallas_call(
        functools.partial(forward_kernel, slabs),
        out_shape=[
            jax.ShapeDtypeStruct((channels, voxels), BF16),
            jax.ShapeDtypeStruct((channels, voxels), BF16),
        ]
        + [
            jax.ShapeDtypeStruct((size, TILE, LANES), kind)
            for size in (shared, more)
            for kind in (F32, BF16)
        ],
        in_specs=[smem] + [vmem] * (8 + len(halos)),
        scratch_shapes=[
            pltpu.VMEM((conv_columns, voxels), BF16),
            pltpu.VMEM((channels, -(-conv_columns // LANES) * LANES), F32),
            pltpu.VMEM((taps * channels, LANES), F32),
        ],
        compiler_params=params,
        name="forward",
    )(core, features_t, neighbours_t, coarse_grad, w_conv_t, *own, pick, hgrad, *halos)

    rows = channels // TILE

    def tile_shape(count, kind=BF16):
        return jax.ShapeDtypeStruct((count, TILE, LANES), kind)

    def call(name, kernel, out_shape, *operands):
        return pl.pallas_call(
            kernel,
            out_shape=out_shape,
            in_specs=[smem] + [vmem] * (len(operands) - 1),
            compiler_params=params,
            name=name,
        )(*operands)

    def fold(phase, keep, got):
        half = keep.shape[0] // 2
        kernel = functools.partial(fold_kernel, choices[phase], sizes)
        return call("fold", kernel, (tile_shape(half, F32), tile_shape(half)), me, keep, got)

    keep, send = chunks[0::2], chunks[1::2]
    cores = ((0, 1), (1,))
    got = [lax.ppermute(x, "core", p) for x, p in zip(send, (swap, swap[:1]))]
    for phase in range(phases):
        for i in (1, 0):
            keep[i], send[i] = fold(phase, keep[i], got[i])
            if i == 0:
                send[0], _ = lax.optimization_barrier((send[0], send[1]))
            if i == 0 and phase == 0:
                send[0], grad = lax.optimization_barrier((send[0], grad))
            got[i] = lax.ppermute(send[i], SPLIT, bit_pairs(sizes, choices[phase], cores[i]))
        if phase == 0:
            slots = len(slot_table(slabs)) // 4 * rows
            base, stay, *riders = pl.pallas_call(
                functools.partial(backward_kernel, slabs),
                out_shape=(
                    jax.ShapeDtypeStruct((channels, voxels), F32),
                    jax.ShapeDtypeStruct((channels, RIM), F32),
                    tile_shape(slots),
                    tile_shape(slots),
                ),
                in_specs=[smem] + [vmem] * 4,
                scratch_shapes=[
                    pltpu.VMEM((channels, offsets * voxels), BF16),
                    pltpu.VMEM((channels, offsets * LANES), BF16),
                    pltpu.VMEM((voxels, offsets * voxels), BF16),
                    pltpu.VMEM((far_rows, offsets * LANES), BF16),
                    pltpu.VMEM((conv_columns, LANES), BF16),
                ],
                compiler_params=params,
                cost_estimate=light,
                name="backward",
            )(core, neighbours_t, hgrad, grad, w_conv_t)
            got[0], stay, riders, base = lax.optimization_barrier((got[0], stay, riders, base))
        if phase == phases - 1:
            coarse = pl.pallas_call(
                coarse_kernel,
                out_shape=jax.ShapeDtypeStruct(coarse_grad.shape, BF16),
                compiler_params=params,
                cost_estimate=light,
                name="coarse",
            )(pick, hidden, w_down)

    far_bits = sizes["far"].bit_length() - 1
    count = [x.shape[0] for x in keep]
    first = riders[:1] if far_bits else riders
    total = [(x + y.astype(F32)).astype(BF16) for x, y in zip(keep, got)]
    total[0] = pl.pallas_call(
        close_kernel,
        out_shape=tile_shape(count[0] + sum(x.shape[0] for x in first)),
        compiler_params=params,
        name="close",
    )(keep[0], got[0], *first)
    for bit in range(far_bits):
        choice = (("far", bit),) * 2
        total[0], _ = lax.optimization_barrier((total[0], total[1]))
        got = [lax.ppermute(x, SPLIT, bit_pairs(sizes, choice, c)) for x, c in zip(total, cores)]
        late = riders[1:] if bit == far_bits - 1 else []
        kernel = functools.partial(meet_kernel, choice, sizes, rows, count[0])
        shape = tile_shape(total[0].shape[0] + sum(x.shape[0] for x in late))
        carried = call("meet", kernel, shape, me, total[0], got[0], *late)
        total = [(x.astype(F32) + y.astype(F32)).astype(BF16) for x, y in zip(total, got)]
        total[0] = carried
    for phase in reversed(range(phases)):
        choice = choices[phase]
        total[0], _ = lax.optimization_barrier((total[0], total[1]))
        got = [lax.ppermute(x, SPLIT, bit_pairs(sizes, choice, c)) for x, c in zip(total, cores)]
        for i in range(2):
            last = i == 0 and phase == 0
            kernel = functools.partial(join_kernel, choice, sizes, rows, count[i], last)
            if last:
                shape = (tile_shape(2 * count[0] + rows), jax.ShapeDtypeStruct((channels, RIM), F32))
                total[0], side = call("join", kernel, shape, me, total[0], got[0], stay)
            else:
                shape = tile_shape(total[i].shape[0] + count[i])
                total[i] = call("join", kernel, shape, me, total[i], got[i])
            count[i] *= 2
    total[0], _ = lax.optimization_barrier((total[0], total[1]))
    other = [lax.ppermute(x, "core", p) for x, p in zip(total, (swap, swap[1:]))]
    conv_wgrad_t, down_wgrad, grad_input_t = pl.pallas_call(
        functools.partial(final_kernel, taps, shared),
        out_shape=(
            jax.ShapeDtypeStruct((channels, conv_columns), F32),
            jax.ShapeDtypeStruct((taps * channels, LANES), F32),
            jax.ShapeDtypeStruct((channels, voxels), F32),
        ),
        in_specs=[smem] + [vmem] * 6,
        compiler_params=params,
        name="final",
    )(core, *total, *other, base, side)
    return coarse, grad_input_t.T, conv_wgrad_t.T, down_wgrad


def solution(mesh):
    regions, slabs = mesh.shape["region"], mesh.shape["slab"]
    fine = Mesh(mesh.devices.reshape(regions // 4, 2, 2, slabs), SPLIT)
    split = P(SPLIT, None)
    return jax.shard_map(
        on_device,
        mesh=fine,
        in_specs=(split, split, split, P(), P(), split),
        out_specs=(split, split, P(), P()),
        check_vma=False,
    )
```

```python
import functools

import jax
import jax.numpy as jnp
from jax import lax
from jax.experimental import pallas as pl
from jax.experimental.pallas import tpu as pltpu
from jax.sharding import Mesh, PartitionSpec as P

SPLIT = ("far", "near", "core", "slab")
RING = ("far", "near", "core")
RIM = 64
LANES = 128
TILE = 16
CHUNKS = 1
F32 = jnp.float32
BF16 = jnp.bfloat16
NN = (((1,), (0,)), ((), ()))
NT = (((1,), (1,)), ((), ()))
VMEM_BYTES = 20 * 2**20


def mm(a, b, dims=NN):
    return lax.dot_general(a, b, dims, preferred_element_type=F32)


def table_lanes(neighbours, voxels, slabs, core):
    code = neighbours // voxels
    slot = neighbours - code * voxels
    row = code // 3
    col = code - row * 3
    if slabs == 2:
        rims = 2
        place = jnp.where(col == 1, 0, 1)
        beside = 0
    else:
        rims = 3
        place = col
        beside = col // 2
    group = jnp.abs(row // 2 + core - 1)
    rim = jnp.where(row == 1, 2 * rims + beside, group * rims + place)
    lane = jnp.where(code == 4, slot, voxels + rim * RIM + slot)
    return jnp.where(code > 8, -1, lane)


def payload_tiles(channels, conv_columns, taps):
    tiles = []
    for column in range(0, conv_columns, LANES):
        for row in range(0, channels, TILE):
            tiles.append((0, row, column, min(LANES, conv_columns - column)))
    for row in range(0, taps * channels, TILE):
        tiles.append((1, row, 0, LANES))
    return tiles


def padded_halo(halo_refs):
    halo = [h[...] for h in halo_refs]
    width = sum(h.shape[1] for h in halo)
    slack = -width % LANES
    if slack:
        halo.append(jnp.zeros((halo[0].shape[0], slack), BF16))
    return jnp.concatenate(halo, axis=1)


def gather_kernel(slabs, f_ref, near_ref, first_ref, rest_ref):
    channels, voxels = f_ref.shape
    table_t = f_ref[...]
    lanes = table_lanes(near_ref[...], voxels, slabs, 0)
    near_iota = lax.broadcasted_iota(jnp.int32, (voxels, voxels), 0)
    for o in range(near_ref.shape[0]):
        near = jnp.where(near_iota == lanes[o : o + 1, :], 1.0, 0.0).astype(BF16)
        own = mm(table_t, near).astype(BF16)
        first_ref[o * channels : (o + 1) * channels, :] = own[:, :LANES]
        rest_ref[o * channels : (o + 1) * channels, :] = own[:, LANES:]


def taps_kernel(down_ref, cgrad_ref, wd_ref, pick_ref, hgrad_ref):
    channels, voxels = hgrad_ref.shape
    taps, coarse_count = down_ref.shape
    cgrad_t = cgrad_ref[...].astype(F32).T.astype(BF16)
    down = down_ref[...].astype(F32).T
    lane_iota = lax.broadcasted_iota(jnp.int32, (coarse_count, voxels), 1).astype(F32)
    hgrad_t = jnp.zeros((channels, voxels), F32)
    for t in range(taps):
        pick = jnp.where(lane_iota == down[:, t : t + 1], 1.0, 0.0).astype(BF16)
        pick_ref[t] = pick
        wd = wd_ref[t * channels : (t + 1) * channels, :]
        hgrad_t += mm(wd, mm(cgrad_t, pick).astype(BF16))
    hgrad_ref[...] = hgrad_t


def far_one_hots(lanes, rows, voxels, offsets):
    iota = lax.broadcasted_iota(jnp.int32, (rows, LANES), 0) + voxels
    hots = [jnp.where(iota == lanes[o : o + 1, :LANES], 1.0, 0.0).astype(BF16) for o in offsets]
    return jnp.concatenate(hots, axis=1)


def forward_kernel(slabs, core_ref, f_ref, near_ref, cgrad_ref, w_ref, *refs):
    first_ref, rest_ref, pick_ref, hgrad_ref = refs[:4]
    halo_refs, refs = (refs[4:7], refs[7:]) if slabs == 2 else (refs[4:8], refs[8:])
    grad_ref, hidden_ref, *chunks, rt, conv_w, down_w = refs
    channels, voxels = f_ref.shape
    offsets = near_ref.shape[0]
    taps = pick_ref.shape[0]
    conv_columns = offsets * channels
    halo_t = padded_halo(halo_refs)
    lanes = table_lanes(near_ref[:, :LANES], voxels, slabs, core_ref[0])
    for pair in range(0, offsets, 2):
        pair = range(pair, min(pair + 2, offsets))
        away = mm(halo_t, far_one_hots(lanes, halo_t.shape[1], voxels, pair))
        for i, o in enumerate(pair):
            rows = slice(o * channels, (o + 1) * channels)
            first = first_ref[rows, :].astype(F32) + away[:, i * LANES : (i + 1) * LANES]
            rt[rows, :LANES] = first.astype(BF16)
            rt[rows, LANES:] = rest_ref[rows, :]

    out_t = mm(w_ref[...], rt[...])
    sig = 1.0 / (1.0 + jnp.exp(-out_t))
    hidden_t = (f_ref[...].astype(F32) + out_t * sig).astype(BF16)
    grad_t = (hgrad_ref[...] * sig * (1.0 + out_t * (1.0 - sig))).astype(BF16)
    grad_ref[...] = grad_t
    conv_w[:, :conv_columns] = mm(grad_t, rt[...], NT)
    if conv_w.shape[1] > conv_columns:
        slack = conv_w.shape[1] - conv_columns
        conv_w[:, conv_columns:] = jnp.zeros((channels, slack), F32)

    hidden_ref[...] = hidden_t
    cgrad = cgrad_ref[...]
    for t in range(taps):
        picked_t = mm(hidden_t, pick_ref[t], NT).astype(BF16)
        down_w[t * channels : (t + 1) * channels, :] = mm(picked_t, cgrad)

    tiles = payload_tiles(channels, conv_columns, taps)
    count = len(chunks) // 2
    size = chunks[0].shape[0]
    for core in range(2):

        @pl.when(core_ref[0] == core)
        def _(core=core):
            for i in range(2 * count * size):
                half, chunk, place = i // (count * size), i // size % count, i % size
                ref = chunks[2 * chunk + (half != core)]
                if i < len(tiles):
                    kind, row, column, _ = tiles[i]
                    source = down_w if kind else conv_w
                    value = source[row : row + TILE, column : column + LANES]
                else:
                    value = jnp.zeros((TILE, LANES), F32)
                ref[place] = value.astype(ref.dtype)


def coarse_kernel(pick_ref, hidden_ref, wd_ref, coarse_ref):
    channels = hidden_ref.shape[0]
    coarse = jnp.zeros(coarse_ref.shape, F32)
    for t in range(pick_ref.shape[0]):
        picked = mm(pick_ref[t], hidden_ref[...], NT).astype(BF16)
        coarse += mm(picked, wd_ref[t * channels : (t + 1) * channels, :])
    coarse_ref[...] = coarse.astype(BF16)


def backward_kernel(slabs, core_ref, near_ref, hgrad_ref, grad_ref, w_ref, *refs):
    base_ref, keep_ref, *refs = refs
    cross_refs, (drt, drt_far, hot, far, w_back) = refs[:-5], refs[-5:]
    channels, voxels = hgrad_ref.shape
    offsets = near_ref.shape[0]
    lanes = table_lanes(near_ref[...], voxels, slabs, core_ref[0])
    near_iota = lax.broadcasted_iota(jnp.int32, (voxels, voxels), 0)
    w_back[:, :channels] = w_ref[...].astype(F32).T.astype(BF16)
    w_back[:, channels:] = jnp.zeros((offsets * channels, LANES - channels), BF16)
    slack = jnp.zeros((LANES - channels, voxels), BF16)
    grad_pad = jnp.concatenate([grad_ref[...], slack], axis=0)
    for o in range(offsets):
        near = jnp.where(near_iota == lanes[o : o + 1, :], 1.0, 0.0).astype(BF16)
        hot[:, o * voxels : (o + 1) * voxels] = near
        spread = mm(w_back[o * channels : (o + 1) * channels, :], grad_pad).astype(BF16)
        drt[:, o * voxels : (o + 1) * voxels] = spread
        drt_far[:, o * LANES : (o + 1) * LANES] = spread[:, :LANES]
        far[:, o * LANES : (o + 1) * LANES] = far_one_hots(lanes, far.shape[0], voxels, (o,))
    base_ref[...] = hgrad_ref[...] + mm(drt[...], hot[...], NT)
    back_t = mm(drt_far[...], far[...], NT)
    rims = 2 if slabs == 2 else 3
    mid = 0 if slabs == 2 else 1
    rim = [back_t[:, i * RIM : (i + 1) * RIM] for i in range(2 * rims + len(cross_refs))]
    keep_ref[...] = jnp.concatenate([rim[mid], rim[rims + mid]], axis=1)
    for i, ref in enumerate(cross_refs):
        place = 1 if slabs == 2 else 2 * i
        parts = [rim[place], rim[rims + place], rim[2 * rims + i], jnp.zeros_like(rim[0])]
        ref[...] = jnp.concatenate(parts, axis=1).astype(BF16)


def turn_kernel(base_ref, keep_ref, *refs):
    got_refs, (sum_ref, cross_ref, mate_ref) = refs[:-3], refs[-3:]
    got = got_refs[0][...].astype(F32)
    for ref in got_refs[1:]:
        got += ref[...].astype(F32)
    sum_ref[:, RIM:] = base_ref[:, RIM:]
    sum_ref[:, :RIM] = base_ref[:, :RIM] + got[:, 2 * RIM : 3 * RIM]
    pair = keep_ref[...] + got[:, : 2 * RIM]
    cross_ref[...] = pair[:, RIM:].astype(BF16)
    pair = pair.astype(BF16)
    for i in range(mate_ref.shape[0]):
        mate_ref[i] = pair[i * TILE : (i + 1) * TILE, :]


def fold_kernel(bit_ref, own_ref, got_ref, keep_ref, send_ref):
    half = keep_ref.shape[0]
    for ref, part in ((keep_ref, bit_ref[0]), (send_ref, 1 - bit_ref[0])):
        rows = pl.ds(part * half, half)
        ref[...] = (own_ref[rows] + got_ref[rows].astype(F32)).astype(ref.dtype)


def join_kernel(bit_ref, own_ref, got_ref, *refs):
    riders, full_ref = refs[:-1], refs[-1]
    half = own_ref.shape[0]
    for rider in riders:
        full_ref[2 * half :] = rider[...]
    full_ref[pl.ds(bit_ref[0] * half, half)] = own_ref[...]
    full_ref[pl.ds((1 - bit_ref[0]) * half, half)] = got_ref[...]


def final_kernel(taps, count, size, core_ref, *refs):
    mine, other, refs = refs[:count], refs[count : 2 * count], refs[2 * count :]
    base_ref, cross_ref, conv_ref, down_ref, grad_ref = refs
    channels, conv_columns = conv_ref.shape
    grad_ref[:, RIM:] = base_ref[:, RIM:]
    for i in range(channels // TILE):
        rows = slice(i * TILE, (i + 1) * TILE)
        total = base_ref[rows, :RIM] + cross_ref[rows, :].astype(F32)
        grad_ref[rows, :RIM] = total + other[-1][size + i][:, :RIM].astype(F32)
    for core in range(2):

        @pl.when(core_ref[0] == core)
        def _(core=core):
            for i, tile in enumerate(payload_tiles(channels, conv_columns, taps)):
                kind, row, column, columns = tile
                source = mine if i // (count * size) == core else other
                value = source[i // size % count][i % size].astype(F32)
                target = down_ref if kind else conv_ref
                target[row : row + TILE, column : column + columns] = value[:, :columns]


def shifts(count, step):
    return [(i, i + step) for i in range(count) if 0 <= i + step < count]


def chip_pairs(regions):
    mates = [(i, i ^ 1) for i in range(regions)]
    cross = [(i, i + 1) for i in range(1, regions - 1, 2)]
    return mates, cross + [(b, a) for a, b in cross]


def square_bits(nears, slabs, core):
    near = [("near", i) for i in range(nears.bit_length() - 1)]
    slab = [("slab", i) for i in range(slabs.bit_length() - 1)]
    return near + slab if core == 0 else slab + near


def bit_pairs(sizes, orders, phase):
    pairs = []
    for index in range(functools.reduce(lambda a, b: a * b, sizes.values())):
        place, left = {}, index
        for axis in reversed(SPLIT):
            left, place[axis] = divmod(left, sizes[axis])
        axis, bit = orders[place["core"]][phase]
        place[axis] ^= 1 << bit
        other = 0
        for name in SPLIT:
            other = other * sizes[name] + place[name]
        pairs.append((index, other))
    return pairs


def on_device(features, neighbours, down_map, w_conv, w_down, coarse_grad):
    sizes = {axis: lax.axis_size(axis) for axis in SPLIT}
    regions, slabs = sizes["far"] * sizes["near"] * sizes["core"], sizes["slab"]
    voxels, channels = features.shape
    offsets, taps = neighbours.shape[1], down_map.shape[1]
    conv_columns = offsets * channels
    core = lax.axis_index("core").astype(jnp.int32).reshape(1)
    swap = [(0, 1), (1, 0)]
    mates, crossings = chip_pairs(regions)
    orders = [square_bits(sizes["near"], slabs, c) for c in range(2)]
    phases = len(orders[0])
    bits = []
    for phase in range(phases):
        chosen = [(lax.axis_index(axis) >> bit) & 1 for axis, bit in (o[phase] for o in orders)]
        bits.append(jnp.where(core == 0, *chosen).astype(jnp.int32))

    smem = pl.BlockSpec(memory_space=pltpu.SMEM)
    vmem = pl.BlockSpec(memory_space=pltpu.VMEM)
    params = pltpu.CompilerParams(vmem_limit_bytes=VMEM_BYTES)
    light = pl.CostEstimate(flops=2 * 10**9, bytes_accessed=10**7, transcendentals=0)
    features_t, neighbours_t, w_conv_t = features.T, neighbours.T, w_conv.T
    rim = features_t[:, :RIM]
    if slabs == 2:
        beside = [swap]
    else:
        beside = [shifts(slabs, 1), shifts(slabs, -1)]
    side = [lax.ppermute(features_t, "slab", pairs) for pairs in beside]
    own = pl.pallas_call(
        functools.partial(gather_kernel, slabs),
        out_shape=(
            jax.ShapeDtypeStruct((conv_columns, LANES), BF16),
            jax.ShapeDtypeStruct((conv_columns, voxels - LANES), BF16),
        ),
        compiler_params=params,
        cost_estimate=light,
        name="gather",
    )(features_t, neighbours_t)
    side, own = lax.optimization_barrier((side, own))
    side = [x[:, :RIM] for x in side]
    row = [rim, side[0]] if slabs == 2 else [side[0], rim, side[1]]
    row = jnp.concatenate(row, axis=1)
    cross = lax.ppermute(row, RING, crossings)
    mate = lax.ppermute(row, RING, mates)
    row, down_t = lax.optimization_barrier((row, down_map.T))
    pick, hgrad = pl.pallas_call(
        taps_kernel,
        out_shape=(
            jax.ShapeDtypeStruct((taps, coarse_grad.shape[0], voxels), BF16),
            jax.ShapeDtypeStruct((channels, voxels), F32),
        ),
        compiler_params=params,
        cost_estimate=light,
        name="taps",
    )(down_t, coarse_grad, w_down)
    halos = [mate, cross, *side]
    far_rows = -(-sum(x.shape[1] for x in halos) // LANES) * LANES

    tiles = len(payload_tiles(channels, conv_columns, taps))
    size = -(-tiles // (2 * CHUNKS << phases)) << phases
    grad, hidden, *chunks = pl.pallas_call(
        functools.partial(forward_kernel, slabs),
        out_shape=[
            jax.ShapeDtypeStruct((channels, voxels), BF16),
            jax.ShapeDtypeStruct((channels, voxels), BF16),
        ]
        + [jax.ShapeDtypeStruct((size, TILE, LANES), kind) for kind in (F32, BF16)] * CHUNKS,
        in_specs=[smem] + [vmem] * (8 + len(halos)),
        scratch_shapes=[
            pltpu.VMEM((conv_columns, voxels), BF16),
            pltpu.VMEM((channels, -(-conv_columns // LANES) * LANES), F32),
            pltpu.VMEM((taps * channels, LANES), F32),
        ],
        compiler_params=params,
        name="forward",
    )(core, features_t, neighbours_t, coarse_grad, w_conv_t, *own, pick, hgrad, *halos)

    def fold(phase, keep, got):
        shape = (keep.shape[0] // 2, TILE, LANES)
        return pl.pallas_call(
            fold_kernel,
            out_shape=(jax.ShapeDtypeStruct(shape, F32), jax.ShapeDtypeStruct(shape, BF16)),
            in_specs=[smem, vmem, vmem],
            compiler_params=params,
            name="fold",
        )(bits[phase], keep, got)

    def join(phase, own, got, *riders):
        count = own.shape[0] * 2 + sum(x.shape[0] for x in riders)
        return pl.pallas_call(
            join_kernel,
            out_shape=jax.ShapeDtypeStruct((count, TILE, LANES), BF16),
            in_specs=[smem] + [vmem] * (2 + len(riders)),
            compiler_params=params,
            name="join",
        )(bits[phase], own, got, *riders)

    keep, send = chunks[0::2], chunks[1::2]
    got = [lax.ppermute(x, "core", swap) for x in send]
    for phase in range(phases):
        pairs = bit_pairs(sizes, orders, phase)
        for i in range(CHUNKS):
            keep[i], send[i] = fold(phase, keep[i], got[i])
            if phase == 0 and i == 0:
                send[0], grad = lax.optimization_barrier((send[0], grad))
            got[i] = lax.ppermute(send[i], SPLIT, pairs)
        if phase == 0:
            base, stay, *edges = pl.pallas_call(
                functools.partial(backward_kernel, slabs),
                out_shape=[
                    jax.ShapeDtypeStruct((channels, voxels), F32),
                    jax.ShapeDtypeStruct((channels, 2 * RIM), F32),
                ]
                + [jax.ShapeDtypeStruct((channels, 4 * RIM), BF16)] * len(beside),
                in_specs=[smem] + [vmem] * 4,
                scratch_shapes=[
                    pltpu.VMEM((channels, offsets * voxels), BF16),
                    pltpu.VMEM((channels, offsets * LANES), BF16),
                    pltpu.VMEM((voxels, offsets * voxels), BF16),
                    pltpu.VMEM((far_rows, offsets * LANES), BF16),
                    pltpu.VMEM((conv_columns, LANES), BF16),
                ],
                compiler_params=params,
                cost_estimate=light,
                name="backward",
            )(core, neighbours_t, hgrad, grad, w_conv_t)
            got[0], stay, edges, base = lax.optimization_barrier((got[0], stay, edges, base))
        if phase == phases - 1:
            back = beside if slabs == 2 else beside[::-1]
            edges = [lax.ppermute(x, "slab", p) for x, p in zip(edges, back)]
    coarse = pl.pallas_call(
        coarse_kernel,
        out_shape=jax.ShapeDtypeStruct(coarse_grad.shape, BF16),
        compiler_params=params,
        cost_estimate=light,
        name="coarse",
    )(pick, hidden, w_down)
    total = [(x + y.astype(F32)).astype(BF16) for x, y in zip(keep, got)]
    far_bits = sizes["far"].bit_length() - 1
    for bit in range(far_bits):
        pairs = [(i, i ^ (1 << bit)) for i in range(sizes["far"])]
        got = [lax.ppermute(x, "far", pairs) for x in total]
        total = [(x.astype(F32) + y.astype(F32)).astype(BF16) for x, y in zip(total, got)]
        if bit == 0:
            total[-1], edges = lax.optimization_barrier((total[-1], edges))
    base, cross, mate = pl.pallas_call(
        turn_kernel,
        out_shape=(
            jax.ShapeDtypeStruct((channels, voxels), F32),
            jax.ShapeDtypeStruct((channels, RIM), BF16),
            jax.ShapeDtypeStruct((channels // TILE, TILE, LANES), BF16),
        ),
        compiler_params=params,
        name="turn",
    )(base, stay, *edges)
    cross = lax.ppermute(cross, RING, crossings)
    total[-1], cross = lax.optimization_barrier((total[-1], cross))
    for phase in reversed(range(phases)):
        pairs = bit_pairs(sizes, orders, phase)
        got = [lax.ppermute(x, SPLIT, pairs) for x in total]
        riders = [()] * (CHUNKS - 1) + [(mate,) if phase == 0 else ()]
        total = [join(phase, x, y, *z) for x, y, z in zip(total, got, riders)]
    other = [lax.ppermute(x, "core", swap) for x in total]
    conv_wgrad_t, down_wgrad, grad_input_t = pl.pallas_call(
        functools.partial(final_kernel, taps, CHUNKS, size),
        out_shape=(
            jax.ShapeDtypeStruct((channels, conv_columns), F32),
            jax.ShapeDtypeStruct((taps * channels, LANES), F32),
            jax.ShapeDtypeStruct((channels, voxels), F32),
        ),
        in_specs=[smem] + [vmem] * (2 * CHUNKS + 2),
        compiler_params=params,
        name="final",
    )(core, *total, *other, base, cross)
    return coarse, grad_input_t.T, conv_wgrad_t.T, down_wgrad


def solution(mesh):
    regions, slabs = mesh.shape["region"], mesh.shape["slab"]
    fine = Mesh(mesh.devices.reshape(regions // 4, 2, 2, slabs), SPLIT)
    split = P(SPLIT, None)
    return jax.shard_map(
        on_device,
        mesh=fine,
        in_specs=(split, split, split, P(), P(), split),
        out_specs=(split, split, P(), P()),
        check_vma=False,
    )
```

```python
import functools

import jax
import jax.numpy as jnp
from jax import lax
from jax.experimental import pallas as pl
from jax.experimental.pallas import tpu as pltpu
from jax.sharding import Mesh, PartitionSpec as P

SPLIT = ("far", "near", "core", "slab")
RING = ("far", "near", "core")
RIM = 64
LANES = 128
TILE = 16
F32 = jnp.float32
BF16 = jnp.bfloat16
NN = (((1,), (0,)), ((), ()))
NT = (((1,), (1,)), ((), ()))
VMEM_BYTES = 20 * 2**20


def mm(a, b, dims=NN):
    return lax.dot_general(a, b, dims, preferred_element_type=F32)


def table_lanes(neighbours, voxels, slabs, core):
    code = neighbours // voxels
    slot = neighbours - code * voxels
    row = code // 3
    col = code - row * 3
    if slabs == 2:
        rims = 2
        place = jnp.where(col == 1, 0, 1)
        beside = 0
    else:
        rims = 3
        place = col
        beside = col // 2
    group = jnp.abs(row // 2 + core - 1)
    rim = jnp.where(row == 1, 2 * rims + beside, group * rims + place)
    lane = jnp.where(code == 4, slot, voxels + rim * RIM + slot)
    return jnp.where(code > 8, -1, lane)


def payload_tiles(channels, conv_columns, taps):
    tiles = []
    for column in range(0, conv_columns, LANES):
        for row in range(0, channels, TILE):
            tiles.append((0, row, column, min(LANES, conv_columns - column)))
    for row in range(0, taps * channels, TILE):
        tiles.append((1, row, 0, LANES))
    return tiles


def padded_halo(halo_refs):
    halo = [h[...] for h in halo_refs]
    width = sum(h.shape[1] for h in halo)
    slack = -width % LANES
    if slack:
        halo.append(jnp.zeros((halo[0].shape[0], slack), BF16))
    return jnp.concatenate(halo, axis=1)


def gather_kernel(slabs, f_ref, near_ref, first_ref, rest_ref):
    channels, voxels = f_ref.shape
    table_t = f_ref[...]
    lanes = table_lanes(near_ref[...], voxels, slabs, 0)
    near_iota = lax.broadcasted_iota(jnp.int32, (voxels, voxels), 0)
    for o in range(near_ref.shape[0]):
        near = jnp.where(near_iota == lanes[o : o + 1, :], 1.0, 0.0).astype(BF16)
        own = mm(table_t, near).astype(BF16)
        first_ref[o * channels : (o + 1) * channels, :] = own[:, :LANES]
        rest_ref[o * channels : (o + 1) * channels, :] = own[:, LANES:]


def taps_kernel(down_ref, cgrad_ref, wd_ref, pick_ref, hgrad_ref):
    channels, voxels = hgrad_ref.shape
    taps, coarse_count = down_ref.shape
    cgrad_t = cgrad_ref[...].astype(F32).T.astype(BF16)
    down = down_ref[...].astype(F32).T
    lane_iota = lax.broadcasted_iota(jnp.int32, (coarse_count, voxels), 1).astype(F32)
    hgrad_t = jnp.zeros((channels, voxels), F32)
    for t in range(taps):
        pick = jnp.where(lane_iota == down[:, t : t + 1], 1.0, 0.0).astype(BF16)
        pick_ref[t] = pick
        wd = wd_ref[t * channels : (t + 1) * channels, :]
        hgrad_t += mm(wd, mm(cgrad_t, pick).astype(BF16))
    hgrad_ref[...] = hgrad_t


def far_one_hots(lanes, rows, voxels, offsets):
    iota = lax.broadcasted_iota(jnp.int32, (rows, LANES), 0) + voxels
    hots = [jnp.where(iota == lanes[o : o + 1, :LANES], 1.0, 0.0).astype(BF16) for o in offsets]
    return jnp.concatenate(hots, axis=1)


def forward_kernel(slabs, core_ref, f_ref, near_ref, cgrad_ref, w_ref, *refs):
    first_ref, rest_ref, pick_ref, hgrad_ref = refs[:4]
    halo_refs, refs = (refs[4:7], refs[7:]) if slabs == 2 else (refs[4:8], refs[8:])
    grad_ref, hidden_ref, keep_ref, send_ref, rt, conv_w, down_w = refs
    channels, voxels = f_ref.shape
    offsets = near_ref.shape[0]
    taps = pick_ref.shape[0]
    conv_columns = offsets * channels
    halo_t = padded_halo(halo_refs)
    lanes = table_lanes(near_ref[:, :LANES], voxels, slabs, core_ref[0])
    for pair in range(0, offsets, 2):
        pair = range(pair, min(pair + 2, offsets))
        away = mm(halo_t, far_one_hots(lanes, halo_t.shape[1], voxels, pair))
        for i, o in enumerate(pair):
            rows = slice(o * channels, (o + 1) * channels)
            first = first_ref[rows, :].astype(F32) + away[:, i * LANES : (i + 1) * LANES]
            rt[rows, :LANES] = first.astype(BF16)
            rt[rows, LANES:] = rest_ref[rows, :]

    out_t = mm(w_ref[...], rt[...])
    sig = 1.0 / (1.0 + jnp.exp(-out_t))
    hidden_t = (f_ref[...].astype(F32) + out_t * sig).astype(BF16)
    grad_t = (hgrad_ref[...] * sig * (1.0 + out_t * (1.0 - sig))).astype(BF16)
    grad_ref[...] = grad_t
    conv_w[:, :conv_columns] = mm(grad_t, rt[...], NT)
    if conv_w.shape[1] > conv_columns:
        slack = conv_w.shape[1] - conv_columns
        conv_w[:, conv_columns:] = jnp.zeros((channels, slack), F32)

    hidden_ref[...] = hidden_t
    cgrad = cgrad_ref[...]
    for t in range(taps):
        picked_t = mm(hidden_t, pick_ref[t], NT).astype(BF16)
        down_w[t * channels : (t + 1) * channels, :] = mm(picked_t, cgrad)

    tiles = payload_tiles(channels, conv_columns, taps)
    size = keep_ref.shape[0]
    for core in range(2):

        @pl.when(core_ref[0] == core)
        def _(core=core):
            for i in range(2 * size):
                ref = keep_ref if i // size == core else send_ref
                if i < len(tiles):
                    kind, row, column, _ = tiles[i]
                    source = down_w if kind else conv_w
                    value = source[row : row + TILE, column : column + LANES]
                else:
                    value = jnp.zeros((TILE, LANES), F32)
                ref[i % size] = value.astype(ref.dtype)


def coarse_kernel(pick_ref, hidden_ref, wd_ref, coarse_ref):
    channels = hidden_ref.shape[0]
    coarse = jnp.zeros(coarse_ref.shape, F32)
    for t in range(pick_ref.shape[0]):
        picked = mm(pick_ref[t], hidden_ref[...], NT).astype(BF16)
        coarse += mm(picked, wd_ref[t * channels : (t + 1) * channels, :])
    coarse_ref[...] = coarse.astype(BF16)


def backward_kernel(slabs, core_ref, near_ref, hgrad_ref, grad_ref, w_ref, *refs):
    base_ref, keep_ref, *refs = refs
    cross_refs, (drt, drt_far, hot, far, w_back) = refs[:-5], refs[-5:]
    channels, voxels = hgrad_ref.shape
    offsets = near_ref.shape[0]
    lanes = table_lanes(near_ref[...], voxels, slabs, core_ref[0])
    near_iota = lax.broadcasted_iota(jnp.int32, (voxels, voxels), 0)
    w_back[:, :channels] = w_ref[...].astype(F32).T.astype(BF16)
    w_back[:, channels:] = jnp.zeros((offsets * channels, LANES - channels), BF16)
    slack = jnp.zeros((LANES - channels, voxels), BF16)
    grad_pad = jnp.concatenate([grad_ref[...], slack], axis=0)
    for o in range(offsets):
        near = jnp.where(near_iota == lanes[o : o + 1, :], 1.0, 0.0).astype(BF16)
        hot[:, o * voxels : (o + 1) * voxels] = near
        spread = mm(w_back[o * channels : (o + 1) * channels, :], grad_pad).astype(BF16)
        drt[:, o * voxels : (o + 1) * voxels] = spread
        drt_far[:, o * LANES : (o + 1) * LANES] = spread[:, :LANES]
        far[:, o * LANES : (o + 1) * LANES] = far_one_hots(lanes, far.shape[0], voxels, (o,))
    base_ref[...] = hgrad_ref[...] + mm(drt[...], hot[...], NT)
    back_t = mm(drt_far[...], far[...], NT)
    rims = 2 if slabs == 2 else 3
    mid = 0 if slabs == 2 else 1
    rim = [back_t[:, i * RIM : (i + 1) * RIM] for i in range(2 * rims + len(cross_refs))]
    keep_ref[...] = jnp.concatenate([rim[mid], rim[rims + mid]], axis=1)
    for i, ref in enumerate(cross_refs):
        place = 1 if slabs == 2 else 2 * i
        parts = [rim[place], rim[rims + place], rim[2 * rims + i], jnp.zeros_like(rim[0])]
        ref[...] = jnp.concatenate(parts, axis=1).astype(BF16)


def turn_kernel(base_ref, keep_ref, *refs):
    got_refs, (sum_ref, cross_ref, mate_ref) = refs[:-3], refs[-3:]
    got = got_refs[0][...].astype(F32)
    for ref in got_refs[1:]:
        got += ref[...].astype(F32)
    sum_ref[:, RIM:] = base_ref[:, RIM:]
    sum_ref[:, :RIM] = base_ref[:, :RIM] + got[:, 2 * RIM : 3 * RIM]
    pair = keep_ref[...] + got[:, : 2 * RIM]
    cross_ref[...] = pair[:, RIM:].astype(BF16)
    pair = pair.astype(BF16)
    for i in range(mate_ref.shape[0]):
        mate_ref[i] = pair[i * TILE : (i + 1) * TILE, :]


def step_of(steps, core):
    return jnp.where(core == 0, *steps)


def split_kernel(orders, core_ref, here_ref, own_ref, got_ref, *piece_refs):
    length = piece_refs[0].shape[0]
    for ref, steps in zip(piece_refs, ((0, 0),) + orders):
        rows = pl.ds((here_ref[0] ^ step_of(steps, core_ref[0])) * length, length)
        ref[...] = (own_ref[rows] + got_ref[rows].astype(F32)).astype(ref.dtype)


def join_kernel(orders, core_ref, here_ref, *refs):
    piece_refs, rider_ref, full_ref = refs[:-2], refs[-2], refs[-1]
    length = piece_refs[0].shape[0]
    for ref, steps in zip(piece_refs, ((0, 0),) + orders):
        place = here_ref[0] ^ step_of(steps, core_ref[0])
        full_ref[pl.ds(place * length, length)] = ref[...]
    full_ref[len(piece_refs) * length :] = rider_ref[...]


def final_kernel(taps, size, core_ref, mine_ref, other_ref, *refs):
    base_ref, cross_ref, conv_ref, down_ref, grad_ref = refs
    channels, conv_columns = conv_ref.shape
    grad_ref[:, RIM:] = base_ref[:, RIM:]
    for i in range(channels // TILE):
        rows = slice(i * TILE, (i + 1) * TILE)
        total = base_ref[rows, :RIM] + cross_ref[rows, :].astype(F32)
        grad_ref[rows, :RIM] = total + other_ref[size + i][:, :RIM].astype(F32)
    for core in range(2):

        @pl.when(core_ref[0] == core)
        def _(core=core):
            for i, tile in enumerate(payload_tiles(channels, conv_columns, taps)):
                kind, row, column, columns = tile
                source = mine_ref if i // size == core else other_ref
                value = source[i % size].astype(F32)
                target = down_ref if kind else conv_ref
                target[row : row + TILE, column : column + columns] = value[:, :columns]


def shifts(count, step):
    return [(i, i + step) for i in range(count) if 0 <= i + step < count]


def chip_pairs(regions):
    mates = [(i, i ^ 1) for i in range(regions)]
    cross = [(i, i + 1) for i in range(1, regions - 1, 2)]
    return mates, cross + [(b, a) for a, b in cross]


def around_orders(nears, slabs):
    count = nears * slabs
    if count == 4:
        return ((3, 3), (2, 1), (1, 2))
    return tuple((i, i) for i in range(count - 1, 0, -1))


def around_pairs(sizes, steps):
    pairs = []
    slabs = sizes["slab"]
    for far in range(sizes["far"]):
        for here in range(sizes["near"] * slabs):
            for core in range(2):
                spots = []
                for spot in (here, here ^ steps[core]):
                    near, slab = divmod(spot, slabs)
                    spots.append(((far * sizes["near"] + near) * 2 + core) * slabs + slab)
                pairs.append(tuple(spots))
    return pairs


def on_device(features, neighbours, down_map, w_conv, w_down, coarse_grad):
    sizes = {axis: lax.axis_size(axis) for axis in SPLIT}
    regions, slabs = sizes["far"] * sizes["near"] * sizes["core"], sizes["slab"]
    voxels, channels = features.shape
    offsets, taps = neighbours.shape[1], down_map.shape[1]
    conv_columns = offsets * channels
    core = lax.axis_index("core").astype(jnp.int32).reshape(1)
    swap = [(0, 1), (1, 0)]
    mates, crossings = chip_pairs(regions)
    here = lax.axis_index(("near", "slab")).astype(jnp.int32).reshape(1)
    orders = around_orders(sizes["near"], slabs)
    routes = [around_pairs(sizes, steps) for steps in orders]
    squares = len(orders) + 1

    smem = pl.BlockSpec(memory_space=pltpu.SMEM)
    vmem = pl.BlockSpec(memory_space=pltpu.VMEM)
    params = pltpu.CompilerParams(vmem_limit_bytes=VMEM_BYTES)
    light = pl.CostEstimate(flops=2 * 10**9, bytes_accessed=10**7, transcendentals=0)
    features_t, neighbours_t, w_conv_t = features.T, neighbours.T, w_conv.T
    rim = features_t[:, :RIM]
    if slabs == 2:
        beside = [swap]
    else:
        beside = [shifts(slabs, 1), shifts(slabs, -1)]
    side = [lax.ppermute(features_t, "slab", pairs) for pairs in beside]
    own = pl.pallas_call(
        functools.partial(gather_kernel, slabs),
        out_shape=(
            jax.ShapeDtypeStruct((conv_columns, LANES), BF16),
            jax.ShapeDtypeStruct((conv_columns, voxels - LANES), BF16),
        ),
        compiler_params=params,
        cost_estimate=light,
        name="gather",
    )(features_t, neighbours_t)
    side, own = lax.optimization_barrier((side, own))
    side = [x[:, :RIM] for x in side]
    row = [rim, side[0]] if slabs == 2 else [side[0], rim, side[1]]
    row = jnp.concatenate(row, axis=1)
    cross = lax.ppermute(row, RING, crossings)
    row, down_t = lax.optimization_barrier((row, down_map.T))
    pick, hgrad = pl.pallas_call(
        taps_kernel,
        out_shape=(
            jax.ShapeDtypeStruct((taps, coarse_grad.shape[0], voxels), BF16),
            jax.ShapeDtypeStruct((channels, voxels), F32),
        ),
        compiler_params=params,
        cost_estimate=light,
        name="taps",
    )(down_t, coarse_grad, w_down)
    row, pick, hgrad = lax.optimization_barrier((row, pick, hgrad))
    mate = lax.ppermute(row, RING, mates)
    halos = [mate, cross, *side]
    far_rows = -(-sum(x.shape[1] for x in halos) // LANES) * LANES

    tiles = len(payload_tiles(channels, conv_columns, taps))
    size = -(-tiles // (2 * squares)) * squares
    grad, hidden, keep, send = pl.pallas_call(
        functools.partial(forward_kernel, slabs),
        out_shape=(
            jax.ShapeDtypeStruct((channels, voxels), BF16),
            jax.ShapeDtypeStruct((channels, voxels), BF16),
            jax.ShapeDtypeStruct((size, TILE, LANES), F32),
            jax.ShapeDtypeStruct((size, TILE, LANES), BF16),
        ),
        in_specs=[smem] + [vmem] * (8 + len(halos)),
        scratch_shapes=[
            pltpu.VMEM((conv_columns, voxels), BF16),
            pltpu.VMEM((channels, -(-conv_columns // LANES) * LANES), F32),
            pltpu.VMEM((taps * channels, LANES), F32),
        ],
        compiler_params=params,
        name="forward",
    )(core, features_t, neighbours_t, coarse_grad, w_conv_t, *own, pick, hgrad, *halos)

    got = lax.ppermute(send, "core", swap)
    piece = size // squares
    keep, *sent = pl.pallas_call(
        functools.partial(split_kernel, orders),
        out_shape=[
            jax.ShapeDtypeStruct((piece, TILE, LANES), BF16 if i else F32) for i in range(squares)
        ],
        in_specs=[smem, smem, vmem, vmem],
        compiler_params=params,
        name="split",
    )(core, here, keep, got)
    sent, grad = lax.optimization_barrier((sent, grad))
    got = [lax.ppermute(x, SPLIT, route) for x, route in zip(sent, routes)]
    base, stay, *edges = pl.pallas_call(
        functools.partial(backward_kernel, slabs),
        out_shape=[
            jax.ShapeDtypeStruct((channels, voxels), F32),
            jax.ShapeDtypeStruct((channels, 2 * RIM), F32),
        ]
        + [jax.ShapeDtypeStruct((channels, 4 * RIM), BF16)] * len(beside),
        in_specs=[smem] + [vmem] * 4,
        scratch_shapes=[
            pltpu.VMEM((channels, offsets * voxels), BF16),
            pltpu.VMEM((channels, offsets * LANES), BF16),
            pltpu.VMEM((voxels, offsets * voxels), BF16),
            pltpu.VMEM((far_rows, offsets * LANES), BF16),
            pltpu.VMEM((conv_columns, LANES), BF16),
        ],
        compiler_params=params,
        cost_estimate=light,
        name="backward",
    )(core, neighbours_t, hgrad, grad, w_conv_t)
    got, stay, edges, base = lax.optimization_barrier((got, stay, edges, base))
    back = beside if slabs == 2 else beside[::-1]
    edges = [lax.ppermute(x, "slab", p) for x, p in zip(edges, back)]
    coarse = pl.pallas_call(
        coarse_kernel,
        out_shape=jax.ShapeDtypeStruct(coarse_grad.shape, BF16),
        compiler_params=params,
        cost_estimate=light,
        name="coarse",
    )(pick, hidden, w_down)
    total = functools.reduce(lambda x, y: x + y.astype(F32), got, keep).astype(BF16)
    far_bits = sizes["far"].bit_length() - 1
    for bit in range(far_bits):
        pairs = [(i, i ^ (1 << bit)) for i in range(sizes["far"])]
        got = lax.ppermute(total, "far", pairs)
        total = (total.astype(F32) + got.astype(F32)).astype(BF16)
        if bit == 0:
            total, edges = lax.optimization_barrier((total, edges))
    base, cross, mate = pl.pallas_call(
        turn_kernel,
        out_shape=(
            jax.ShapeDtypeStruct((channels, voxels), F32),
            jax.ShapeDtypeStruct((channels, RIM), BF16),
            jax.ShapeDtypeStruct((channels // TILE, TILE, LANES), BF16),
        ),
        compiler_params=params,
        name="turn",
    )(base, stay, *edges)
    cross = lax.ppermute(cross, RING, crossings)
    total, cross = lax.optimization_barrier((total, cross))
    got = [lax.ppermute(total, SPLIT, route) for route in routes[::-1]]
    mine = pl.pallas_call(
        functools.partial(join_kernel, orders[::-1]),
        out_shape=jax.ShapeDtypeStruct((size + mate.shape[0], TILE, LANES), BF16),
        in_specs=[smem, smem] + [vmem] * (squares + 1),
        compiler_params=params,
        name="join",
    )(core, here, total, *got, mate)
    other = lax.ppermute(mine, "core", swap)
    conv_wgrad_t, down_wgrad, grad_input_t = pl.pallas_call(
        functools.partial(final_kernel, taps, size),
        out_shape=(
            jax.ShapeDtypeStruct((channels, conv_columns), F32),
            jax.ShapeDtypeStruct((taps * channels, LANES), F32),
            jax.ShapeDtypeStruct((channels, voxels), F32),
        ),
        in_specs=[smem] + [vmem] * 4,
        compiler_params=params,
        name="final",
    )(core, mine, other, base, cross)
    return coarse, grad_input_t.T, conv_wgrad_t.T, down_wgrad


def solution(mesh):
    regions, slabs = mesh.shape["region"], mesh.shape["slab"]
    fine = Mesh(mesh.devices.reshape(regions // 4, 2, 2, slabs), SPLIT)
    split = P(SPLIT, None)
    return jax.shard_map(
        on_device,
        mesh=fine,
        in_specs=(split, split, split, P(), P(), split),
        out_specs=(split, split, P(), P()),
        check_vma=False,
    )
```

```python
import functools

import jax
import jax.numpy as jnp
from jax import lax
from jax.experimental import pallas as pl
from jax.experimental.pallas import tpu as pltpu
from jax.sharding import Mesh, PartitionSpec as P

SPLIT = ("far", "near", "core", "slab")
RING = ("far", "near", "core")
RIM = 64
LANES = 128
TILE = 16
F32 = jnp.float32
BF16 = jnp.bfloat16
NN = (((1,), (0,)), ((), ()))
NT = (((1,), (1,)), ((), ()))
VMEM_BYTES = 20 * 2**20


def mm(a, b, dims=NN):
    return lax.dot_general(a, b, dims, preferred_element_type=F32)


def table_lanes(neighbours, voxels, slabs, core):
    code = neighbours // voxels
    slot = neighbours - code * voxels
    row = code // 3
    col = code - row * 3
    if slabs == 2:
        rims = 2
        place = jnp.where(col == 1, 0, 1)
        beside = 0
    else:
        rims = 3
        place = col
        beside = col // 2
    group = jnp.abs(row // 2 + core - 1)
    rim = jnp.where(row == 1, 2 * rims + beside, group * rims + place)
    lane = jnp.where(code == 4, slot, voxels + rim * RIM + slot)
    return jnp.where(code > 8, -1, lane)


def payload_tiles(channels, conv_columns, taps):
    tiles = []
    for column in range(0, conv_columns, LANES):
        for row in range(0, channels, TILE):
            tiles.append((0, row, column, min(LANES, conv_columns - column)))
    for row in range(0, taps * channels, TILE):
        tiles.append((1, row, 0, LANES))
    return tiles


def padded_halo(halo_refs):
    halo = [h[...] for h in halo_refs]
    width = sum(h.shape[1] for h in halo)
    slack = -width % LANES
    if slack:
        halo.append(jnp.zeros((halo[0].shape[0], slack), BF16))
    return jnp.concatenate(halo, axis=1)


def gather_kernel(slabs, f_ref, near_ref, first_ref, rest_ref):
    channels, voxels = f_ref.shape
    table_t = f_ref[...]
    lanes = table_lanes(near_ref[...], voxels, slabs, 0)
    near_iota = lax.broadcasted_iota(jnp.int32, (voxels, voxels), 0)
    for o in range(near_ref.shape[0]):
        near = jnp.where(near_iota == lanes[o : o + 1, :], 1.0, 0.0).astype(BF16)
        own = mm(table_t, near).astype(BF16)
        first_ref[o * channels : (o + 1) * channels, :] = own[:, :LANES]
        rest_ref[o * channels : (o + 1) * channels, :] = own[:, LANES:]


def taps_kernel(down_ref, cgrad_ref, wd_ref, pick_ref, hgrad_ref):
    channels, voxels = hgrad_ref.shape
    taps, coarse_count = down_ref.shape
    cgrad_t = cgrad_ref[...].astype(F32).T.astype(BF16)
    down = down_ref[...].astype(F32).T
    lane_iota = lax.broadcasted_iota(jnp.int32, (coarse_count, voxels), 1).astype(F32)
    hgrad_t = jnp.zeros((channels, voxels), F32)
    for t in range(taps):
        pick = jnp.where(lane_iota == down[:, t : t + 1], 1.0, 0.0).astype(BF16)
        pick_ref[t] = pick
        wd = wd_ref[t * channels : (t + 1) * channels, :]
        hgrad_t += mm(wd, mm(cgrad_t, pick).astype(BF16))
    hgrad_ref[...] = hgrad_t


def far_one_hots(lanes, rows, voxels, offsets):
    iota = lax.broadcasted_iota(jnp.int32, (rows, LANES), 0) + voxels
    hots = [jnp.where(iota == lanes[o : o + 1, :LANES], 1.0, 0.0).astype(BF16) for o in offsets]
    return jnp.concatenate(hots, axis=1)


def forward_kernel(slabs, core_ref, f_ref, near_ref, cgrad_ref, w_ref, *refs):
    first_ref, rest_ref, pick_ref, hgrad_ref = refs[:4]
    halo_refs, refs = (refs[4:7], refs[7:]) if slabs == 2 else (refs[4:8], refs[8:])
    grad_ref, hidden_ref, keep_ref, send_ref, rt, conv_w, down_w = refs
    channels, voxels = f_ref.shape
    offsets = near_ref.shape[0]
    taps = pick_ref.shape[0]
    conv_columns = offsets * channels
    halo_t = padded_halo(halo_refs)
    lanes = table_lanes(near_ref[:, :LANES], voxels, slabs, core_ref[0])
    for pair in range(0, offsets, 2):
        pair = range(pair, min(pair + 2, offsets))
        away = mm(halo_t, far_one_hots(lanes, halo_t.shape[1], voxels, pair))
        for i, o in enumerate(pair):
            rows = slice(o * channels, (o + 1) * channels)
            first = first_ref[rows, :].astype(F32) + away[:, i * LANES : (i + 1) * LANES]
            rt[rows, :LANES] = first.astype(BF16)
            rt[rows, LANES:] = rest_ref[rows, :]

    out_t = mm(w_ref[...], rt[...])
    sig = 1.0 / (1.0 + jnp.exp(-out_t))
    hidden_t = (f_ref[...].astype(F32) + out_t * sig).astype(BF16)
    grad_t = (hgrad_ref[...] * sig * (1.0 + out_t * (1.0 - sig))).astype(BF16)
    grad_ref[...] = grad_t
    conv_w[:, :conv_columns] = mm(grad_t, rt[...], NT)
    if conv_w.shape[1] > conv_columns:
        slack = conv_w.shape[1] - conv_columns
        conv_w[:, conv_columns:] = jnp.zeros((channels, slack), F32)

    hidden_ref[...] = hidden_t
    cgrad = cgrad_ref[...]
    for t in range(taps):
        picked_t = mm(hidden_t, pick_ref[t], NT).astype(BF16)
        down_w[t * channels : (t + 1) * channels, :] = mm(picked_t, cgrad)

    tiles = payload_tiles(channels, conv_columns, taps)
    size = keep_ref.shape[0]
    for core in range(2):

        @pl.when(core_ref[0] == core)
        def _(core=core):
            for i in range(2 * size):
                ref = keep_ref if i // size == core else send_ref
                if i < len(tiles):
                    kind, row, column, _ = tiles[i]
                    source = down_w if kind else conv_w
                    value = source[row : row + TILE, column : column + LANES]
                else:
                    value = jnp.zeros((TILE, LANES), F32)
                ref[i % size] = value.astype(ref.dtype)


def coarse_kernel(pick_ref, hidden_ref, wd_ref, coarse_ref):
    channels = hidden_ref.shape[0]
    coarse = jnp.zeros(coarse_ref.shape, F32)
    for t in range(pick_ref.shape[0]):
        picked = mm(pick_ref[t], hidden_ref[...], NT).astype(BF16)
        coarse += mm(picked, wd_ref[t * channels : (t + 1) * channels, :])
    coarse_ref[...] = coarse.astype(BF16)


def backward_kernel(slabs, core_ref, near_ref, hgrad_ref, grad_ref, w_ref, *refs):
    base_ref, mate_ref, beside_ref, cross_ref, drt, drt_far, hot, far, w_back = refs
    channels, voxels = hgrad_ref.shape
    offsets = near_ref.shape[0]
    lanes = table_lanes(near_ref[...], voxels, slabs, core_ref[0])
    near_iota = lax.broadcasted_iota(jnp.int32, (voxels, voxels), 0)
    w_back[:, :channels] = w_ref[...].astype(F32).T.astype(BF16)
    w_back[:, channels:] = jnp.zeros((offsets * channels, LANES - channels), BF16)
    slack = jnp.zeros((LANES - channels, voxels), BF16)
    grad_pad = jnp.concatenate([grad_ref[...], slack], axis=0)
    for o in range(offsets):
        near = jnp.where(near_iota == lanes[o : o + 1, :], 1.0, 0.0).astype(BF16)
        hot[:, o * voxels : (o + 1) * voxels] = near
        spread = mm(w_back[o * channels : (o + 1) * channels, :], grad_pad).astype(BF16)
        drt[:, o * voxels : (o + 1) * voxels] = spread
        drt_far[:, o * LANES : (o + 1) * LANES] = spread[:, :LANES]
        far[:, o * LANES : (o + 1) * LANES] = far_one_hots(lanes, far.shape[0], voxels, (o,))
    base_ref[...] = hgrad_ref[...] + mm(drt[...], hot[...], NT)
    back_t = mm(drt_far[...], far[...], NT)
    rims = 2 if slabs == 2 else 3
    rim = [back_t[:, i * RIM : (i + 1) * RIM] for i in range(3 * rims - 1)]
    mate, cross, side = rim[:rims], rim[rims : 2 * rims], rim[2 * rims :]
    own, away = (0, (1,)) if slabs == 2 else (1, (0, 2))
    mate_ref[...] = mate[own]
    parts = []
    for place, part in zip(away, side):
        parts += [mate[place], part]
    beside_ref[...] = jnp.concatenate(parts, axis=1)
    cross_ref[...] = jnp.concatenate(cross, axis=1).astype(BF16)


def cross_turn_kernel(own, beside_ref, got_ref, home_ref, *edge_refs):
    got = got_ref[...].astype(F32)
    rim = [got[:, i * RIM : (i + 1) * RIM] for i in range(got.shape[1] // RIM)]
    home_ref[...] = rim.pop(own)
    for i, (ref, part) in enumerate(zip(edge_refs, rim)):
        mine = beside_ref[:, 2 * i * RIM : 2 * (i + 1) * RIM]
        ref[...] = (mine + jnp.concatenate([jnp.zeros_like(part), part], axis=1)).astype(BF16)


def slab_turn_kernel(mate_ref, home_ref, *refs):
    got_refs, (rider_ref, sum_ref) = refs[:-2], refs[-2:]
    got = got_refs[0][...].astype(F32)
    for ref in got_refs[1:]:
        got += ref[...].astype(F32)
    mate = mate_ref[...] + got[:, :RIM]
    sum_ref[...] = home_ref[...] + got[:, RIM:]
    pair = jnp.concatenate([mate, jnp.zeros_like(mate)], axis=1).astype(BF16)
    for i in range(rider_ref.shape[0]):
        rider_ref[i] = pair[i * TILE : (i + 1) * TILE, :]


def step_of(steps, core):
    return jnp.where(core == 0, *steps)


def split_kernel(orders, core_ref, here_ref, own_ref, got_ref, *piece_refs):
    length = piece_refs[0].shape[0]
    for ref, steps in zip(piece_refs, ((0, 0),) + orders):
        rows = pl.ds((here_ref[0] ^ step_of(steps, core_ref[0])) * length, length)
        ref[...] = (own_ref[rows] + got_ref[rows].astype(F32)).astype(ref.dtype)


def join_kernel(orders, core_ref, here_ref, *refs):
    piece_refs, rider_ref, full_ref = refs[:-2], refs[-2], refs[-1]
    length = piece_refs[0].shape[0]
    for ref, steps in zip(piece_refs, ((0, 0),) + orders):
        place = here_ref[0] ^ step_of(steps, core_ref[0])
        full_ref[pl.ds(place * length, length)] = ref[...]
    full_ref[len(piece_refs) * length :] = rider_ref[...]


def final_kernel(taps, size, core_ref, mine_ref, other_ref, *refs):
    base_ref, home_ref, conv_ref, down_ref, grad_ref = refs
    channels, conv_columns = conv_ref.shape
    grad_ref[:, RIM:] = base_ref[:, RIM:]
    for i in range(channels // TILE):
        rows = slice(i * TILE, (i + 1) * TILE)
        total = base_ref[rows, :RIM] + home_ref[rows, :]
        grad_ref[rows, :RIM] = total + other_ref[size + i][:, :RIM].astype(F32)
    for core in range(2):

        @pl.when(core_ref[0] == core)
        def _(core=core):
            for i, tile in enumerate(payload_tiles(channels, conv_columns, taps)):
                kind, row, column, columns = tile
                source = mine_ref if i // size == core else other_ref
                value = source[i % size].astype(F32)
                target = down_ref if kind else conv_ref
                target[row : row + TILE, column : column + columns] = value[:, :columns]


def shifts(count, step):
    return [(i, i + step) for i in range(count) if 0 <= i + step < count]


def chip_pairs(regions):
    mates = [(i, i ^ 1) for i in range(regions)]
    cross = [(i, i + 1) for i in range(1, regions - 1, 2)]
    return mates, cross + [(b, a) for a, b in cross]


def around_orders(nears, slabs):
    count = nears * slabs
    if count == 4:
        return ((3, 3), (2, 1), (1, 2))
    return tuple((i, i) for i in range(count - 1, 0, -1))


def around_pairs(sizes, steps):
    pairs = []
    slabs = sizes["slab"]
    for far in range(sizes["far"]):
        for here in range(sizes["near"] * slabs):
            for core in range(2):
                spots = []
                for spot in (here, here ^ steps[core]):
                    near, slab = divmod(spot, slabs)
                    spots.append(((far * sizes["near"] + near) * 2 + core) * slabs + slab)
                pairs.append(tuple(spots))
    return pairs


def on_device(features, neighbours, down_map, w_conv, w_down, coarse_grad):
    sizes = {axis: lax.axis_size(axis) for axis in SPLIT}
    regions, slabs = sizes["far"] * sizes["near"] * sizes["core"], sizes["slab"]
    voxels, channels = features.shape
    offsets, taps = neighbours.shape[1], down_map.shape[1]
    conv_columns = offsets * channels
    core = lax.axis_index("core").astype(jnp.int32).reshape(1)
    swap = [(0, 1), (1, 0)]
    mates, crossings = chip_pairs(regions)
    here = lax.axis_index(("near", "slab")).astype(jnp.int32).reshape(1)
    orders = around_orders(sizes["near"], slabs)
    routes = [around_pairs(sizes, steps) for steps in orders]
    squares = len(orders) + 1

    smem = pl.BlockSpec(memory_space=pltpu.SMEM)
    vmem = pl.BlockSpec(memory_space=pltpu.VMEM)
    params = pltpu.CompilerParams(vmem_limit_bytes=VMEM_BYTES)
    light = pl.CostEstimate(flops=2 * 10**9, bytes_accessed=10**7, transcendentals=0)
    features_t, neighbours_t, w_conv_t = features.T, neighbours.T, w_conv.T
    rim = features_t[:, :RIM]
    if slabs == 2:
        beside = [swap]
    else:
        beside = [shifts(slabs, 1), shifts(slabs, -1)]
    side = [lax.ppermute(features_t, "slab", pairs) for pairs in beside]
    own = pl.pallas_call(
        functools.partial(gather_kernel, slabs),
        out_shape=(
            jax.ShapeDtypeStruct((conv_columns, LANES), BF16),
            jax.ShapeDtypeStruct((conv_columns, voxels - LANES), BF16),
        ),
        compiler_params=params,
        cost_estimate=light,
        name="gather",
    )(features_t, neighbours_t)
    side, own = lax.optimization_barrier((side, own))
    side = [x[:, :RIM] for x in side]
    row = [rim, side[0]] if slabs == 2 else [side[0], rim, side[1]]
    row = jnp.concatenate(row, axis=1)
    cross = lax.ppermute(row, RING, crossings)
    row, down_t = lax.optimization_barrier((row, down_map.T))
    pick, hgrad = pl.pallas_call(
        taps_kernel,
        out_shape=(
            jax.ShapeDtypeStruct((taps, coarse_grad.shape[0], voxels), BF16),
            jax.ShapeDtypeStruct((channels, voxels), F32),
        ),
        compiler_params=params,
        cost_estimate=light,
        name="taps",
    )(down_t, coarse_grad, w_down)
    row, pick, hgrad = lax.optimization_barrier((row, pick, hgrad))
    mate = lax.ppermute(row, RING, mates)
    halos = [mate, cross, *side]
    far_rows = -(-sum(x.shape[1] for x in halos) // LANES) * LANES

    tiles = len(payload_tiles(channels, conv_columns, taps))
    size = -(-tiles // (2 * squares)) * squares
    grad, hidden, keep, send = pl.pallas_call(
        functools.partial(forward_kernel, slabs),
        out_shape=(
            jax.ShapeDtypeStruct((channels, voxels), BF16),
            jax.ShapeDtypeStruct((channels, voxels), BF16),
            jax.ShapeDtypeStruct((size, TILE, LANES), F32),
            jax.ShapeDtypeStruct((size, TILE, LANES), BF16),
        ),
        in_specs=[smem] + [vmem] * (8 + len(halos)),
        scratch_shapes=[
            pltpu.VMEM((conv_columns, voxels), BF16),
            pltpu.VMEM((channels, -(-conv_columns // LANES) * LANES), F32),
            pltpu.VMEM((taps * channels, LANES), F32),
        ],
        compiler_params=params,
        name="forward",
    )(core, features_t, neighbours_t, coarse_grad, w_conv_t, *own, pick, hgrad, *halos)

    got = lax.ppermute(send, "core", swap)
    piece = size // squares
    keep, *sent = pl.pallas_call(
        functools.partial(split_kernel, orders),
        out_shape=[
            jax.ShapeDtypeStruct((piece, TILE, LANES), BF16 if i else F32) for i in range(squares)
        ],
        in_specs=[smem, smem, vmem, vmem],
        compiler_params=params,
        name="split",
    )(core, here, keep, got)
    sent, grad = lax.optimization_barrier((sent, grad))
    got = [lax.ppermute(x, SPLIT, route) for x, route in zip(sent, routes)]
    base, mate, stay, cross = pl.pallas_call(
        functools.partial(backward_kernel, slabs),
        out_shape=(
            jax.ShapeDtypeStruct((channels, voxels), F32),
            jax.ShapeDtypeStruct((channels, RIM), F32),
            jax.ShapeDtypeStruct((channels, 2 * len(beside) * RIM), F32),
            jax.ShapeDtypeStruct((channels, row.shape[1]), BF16),
        ),
        in_specs=[smem] + [vmem] * 4,
        scratch_shapes=[
            pltpu.VMEM((channels, offsets * voxels), BF16),
            pltpu.VMEM((channels, offsets * LANES), BF16),
            pltpu.VMEM((voxels, offsets * voxels), BF16),
            pltpu.VMEM((far_rows, offsets * LANES), BF16),
            pltpu.VMEM((conv_columns, LANES), BF16),
        ],
        compiler_params=params,
        cost_estimate=light,
        name="backward",
    )(core, neighbours_t, hgrad, grad, w_conv_t)
    got, cross, base = lax.optimization_barrier((got, cross, base))
    coarse = pl.pallas_call(
        coarse_kernel,
        out_shape=jax.ShapeDtypeStruct(coarse_grad.shape, BF16),
        compiler_params=params,
        cost_estimate=light,
        name="coarse",
    )(pick, hidden, w_down)
    total = functools.reduce(lambda x, y: x + y.astype(F32), got, keep).astype(BF16)
    parts = [total]
    for step in range(1, sizes["far"]):
        parts.append(lax.ppermute(total, "far", [(i, i ^ step) for i in range(sizes["far"])]))
    cross = lax.ppermute(cross, RING, crossings)
    parts = [x.astype(F32) for x in parts]
    while len(parts) > 1:
        parts = [x + y for x, y in zip(parts[0::2], parts[1::2])]
    total = parts[0].astype(BF16)
    total, cross = lax.optimization_barrier((total, cross))
    home, *edges = pl.pallas_call(
        functools.partial(cross_turn_kernel, 0 if slabs == 2 else 1),
        out_shape=[jax.ShapeDtypeStruct((channels, RIM), F32)]
        + [jax.ShapeDtypeStruct((channels, 2 * RIM), BF16)] * len(beside),
        compiler_params=params,
        name="cross_turn",
    )(stay, cross)
    back = beside if slabs == 2 else beside[::-1]
    edges = [lax.ppermute(x, "slab", p) for x, p in zip(edges, back)]
    edges, coarse = lax.optimization_barrier((edges, coarse))
    mate, home = pl.pallas_call(
        slab_turn_kernel,
        out_shape=(
            jax.ShapeDtypeStruct((channels // TILE, TILE, LANES), BF16),
            jax.ShapeDtypeStruct((channels, RIM), F32),
        ),
        compiler_params=params,
        name="slab_turn",
    )(mate, home, *edges)
    got = [lax.ppermute(total, SPLIT, route) for route in routes[::-1]]
    mine = pl.pallas_call(
        functools.partial(join_kernel, orders[::-1]),
        out_shape=jax.ShapeDtypeStruct((size + mate.shape[0], TILE, LANES), BF16),
        in_specs=[smem, smem] + [vmem] * (squares + 1),
        compiler_params=params,
        name="join",
    )(core, here, total, *got, mate)
    other = lax.ppermute(mine, "core", swap)
    conv_wgrad_t, down_wgrad, grad_input_t = pl.pallas_call(
        functools.partial(final_kernel, taps, size),
        out_shape=(
            jax.ShapeDtypeStruct((channels, conv_columns), F32),
            jax.ShapeDtypeStruct((taps * channels, LANES), F32),
            jax.ShapeDtypeStruct((channels, voxels), F32),
        ),
        in_specs=[smem] + [vmem] * 4,
        compiler_params=params,
        name="final",
    )(core, mine, other, base, home)
    return coarse, grad_input_t.T, conv_wgrad_t.T, down_wgrad


def solution(mesh):
    regions, slabs = mesh.shape["region"], mesh.shape["slab"]
    fine = Mesh(mesh.devices.reshape(regions // 4, 2, 2, slabs), SPLIT)
    split = P(SPLIT, None)
    return jax.shard_map(
        on_device,
        mesh=fine,
        in_specs=(split, split, split, P(), P(), split),
        out_specs=(split, split, P(), P()),
        check_vma=False,
    )
```

```python
import functools

import jax
import jax.numpy as jnp
from jax import lax
from jax.experimental import pallas as pl
from jax.experimental.pallas import tpu as pltpu
from jax.sharding import Mesh, PartitionSpec as P

SPLIT = ("far", "near", "core", "slab")
RING = ("far", "near", "core")
RIM = 64
LANES = 128
TILE = 16
F32 = jnp.float32
BF16 = jnp.bfloat16
NN = (((1,), (0,)), ((), ()))
NT = (((1,), (1,)), ((), ()))
VMEM_BYTES = 20 * 2**20


def mm(a, b, dims=NN):
    return lax.dot_general(a, b, dims, preferred_element_type=F32)


def table_lanes(neighbours, voxels, slabs, core):
    code = neighbours // voxels
    slot = neighbours - code * voxels
    row = code // 3
    col = code - row * 3
    if slabs == 2:
        rims = 2
        place = jnp.where(col == 1, 0, 1)
        beside = 0
    else:
        rims = 3
        place = col
        beside = col // 2
    group = jnp.abs(row // 2 + core - 1)
    rim = jnp.where(row == 1, 2 * rims + beside, group * rims + place)
    lane = jnp.where(code == 4, slot, voxels + rim * RIM + slot)
    return jnp.where(code > 8, -1, lane)


def half_tiles(channels, conv_columns, taps):
    tiles = []
    for column in range(0, conv_columns, LANES):
        for row in range(0, channels // 2, TILE):
            tiles.append((0, row, column, min(LANES, conv_columns - column)))
    for row in range(0, taps * channels // 2, TILE):
        tiles.append((1, row, 0, LANES))
    return tiles


def padded_halo(halo_refs):
    halo = [h[...] for h in halo_refs]
    width = sum(h.shape[1] for h in halo)
    slack = -width % LANES
    if slack:
        halo.append(jnp.zeros((halo[0].shape[0], slack), BF16))
    return jnp.concatenate(halo, axis=1)


def gather_kernel(slabs, f_ref, near_ref, first_ref, rest_ref):
    channels, voxels = f_ref.shape
    table_t = f_ref[...]
    lanes = table_lanes(near_ref[...], voxels, slabs, 0)
    near_iota = lax.broadcasted_iota(jnp.int32, (voxels, voxels), 0)
    for o in range(near_ref.shape[0]):
        near = jnp.where(near_iota == lanes[o : o + 1, :], 1.0, 0.0).astype(BF16)
        own = mm(table_t, near).astype(BF16)
        first_ref[o * channels : (o + 1) * channels, :] = own[:, :LANES]
        rest_ref[o * channels : (o + 1) * channels, :] = own[:, LANES:]


def taps_kernel(down_ref, cgrad_ref, wd_ref, pick_ref, hgrad_ref):
    channels, voxels = hgrad_ref.shape
    taps, coarse_count = down_ref.shape
    cgrad_t = cgrad_ref[...].astype(F32).T.astype(BF16)
    down = down_ref[...].astype(F32).T
    lane_iota = lax.broadcasted_iota(jnp.int32, (coarse_count, voxels), 1).astype(F32)
    hgrad_t = jnp.zeros((channels, voxels), F32)
    for t in range(taps):
        pick = jnp.where(lane_iota == down[:, t : t + 1], 1.0, 0.0).astype(BF16)
        pick_ref[t] = pick
        wd = wd_ref[t * channels : (t + 1) * channels, :]
        hgrad_t += mm(wd, mm(cgrad_t, pick).astype(BF16))
    hgrad_ref[...] = hgrad_t


def far_one_hots(lanes, rows, voxels, offsets):
    iota = lax.broadcasted_iota(jnp.int32, (rows, LANES), 0) + voxels
    hots = [jnp.where(iota == lanes[o : o + 1, :LANES], 1.0, 0.0).astype(BF16) for o in offsets]
    return jnp.concatenate(hots, axis=1)


def forward_kernel(slabs, core_ref, f_ref, near_ref, cgrad_ref, w_ref, *refs):
    first_ref, rest_ref, pick_ref, hgrad_ref = refs[:4]
    halo_refs, refs = (refs[4:7], refs[7:]) if slabs == 2 else (refs[4:8], refs[8:])
    grad_ref, hidden_ref, keep_ref, send_ref, rt, conv_w, down_w = refs
    channels, voxels = f_ref.shape
    offsets = near_ref.shape[0]
    taps = pick_ref.shape[0]
    conv_columns = offsets * channels
    halo_t = padded_halo(halo_refs)
    lanes = table_lanes(near_ref[:, :LANES], voxels, slabs, core_ref[0])
    for pair in range(0, offsets, 2):
        pair = range(pair, min(pair + 2, offsets))
        away = mm(halo_t, far_one_hots(lanes, halo_t.shape[1], voxels, pair))
        for i, o in enumerate(pair):
            rows = slice(o * channels, (o + 1) * channels)
            first = first_ref[rows, :].astype(F32) + away[:, i * LANES : (i + 1) * LANES]
            rt[rows, :LANES] = first.astype(BF16)
            rt[rows, LANES:] = rest_ref[rows, :]

    out_t = mm(w_ref[...], rt[...])
    sig = 1.0 / (1.0 + jnp.exp(-out_t))
    hidden_t = (f_ref[...].astype(F32) + out_t * sig).astype(BF16)
    grad_t = (hgrad_ref[...] * sig * (1.0 + out_t * (1.0 - sig))).astype(BF16)
    grad_ref[...] = grad_t
    conv_w[:, :conv_columns] = mm(grad_t, rt[...], NT)
    if conv_w.shape[1] > conv_columns:
        slack = conv_w.shape[1] - conv_columns
        conv_w[:, conv_columns:] = jnp.zeros((channels, slack), F32)

    hidden_ref[...] = hidden_t
    cgrad = cgrad_ref[...]
    for t in range(taps):
        picked_t = mm(hidden_t, pick_ref[t], NT).astype(BF16)
        down_w[t * channels : (t + 1) * channels, :] = mm(picked_t, cgrad)

    tiles = half_tiles(channels, conv_columns, taps)
    for ref, half in ((keep_ref, core_ref[0]), (send_ref, 1 - core_ref[0])):
        for i in range(ref.shape[0]):
            if i < len(tiles):
                kind, row, column, _ = tiles[i]
                source = down_w if kind else conv_w
                start = pl.multiple_of(half * (source.shape[0] // 2) + row, TILE)
                value = source[pl.ds(start, TILE), column : column + LANES]
            else:
                value = jnp.zeros((TILE, LANES), F32)
            ref[i] = value.astype(ref.dtype)


def coarse_kernel(pick_ref, hidden_ref, wd_ref, coarse_ref):
    channels = hidden_ref.shape[0]
    coarse = jnp.zeros(coarse_ref.shape, F32)
    for t in range(pick_ref.shape[0]):
        picked = mm(pick_ref[t], hidden_ref[...], NT).astype(BF16)
        coarse += mm(picked, wd_ref[t * channels : (t + 1) * channels, :])
    coarse_ref[...] = coarse.astype(BF16)


def backward_kernel(slabs, core_ref, near_ref, hgrad_ref, grad_ref, w_ref, *refs):
    base_ref, mate_ref, beside_ref, cross_ref, drt, drt_far, hot, far, w_back = refs
    channels, voxels = hgrad_ref.shape
    offsets = near_ref.shape[0]
    lanes = table_lanes(near_ref[...], voxels, slabs, core_ref[0])
    near_iota = lax.broadcasted_iota(jnp.int32, (voxels, voxels), 0)
    w_back[:, :channels] = w_ref[...].astype(F32).T.astype(BF16)
    w_back[:, channels:] = jnp.zeros((offsets * channels, LANES - channels), BF16)
    slack = jnp.zeros((LANES - channels, voxels), BF16)
    grad_pad = jnp.concatenate([grad_ref[...], slack], axis=0)
    for o in range(offsets):
        near = jnp.where(near_iota == lanes[o : o + 1, :], 1.0, 0.0).astype(BF16)
        hot[:, o * voxels : (o + 1) * voxels] = near
        spread = mm(w_back[o * channels : (o + 1) * channels, :], grad_pad).astype(BF16)
        drt[:, o * voxels : (o + 1) * voxels] = spread
        drt_far[:, o * LANES : (o + 1) * LANES] = spread[:, :LANES]
        far[:, o * LANES : (o + 1) * LANES] = far_one_hots(lanes, far.shape[0], voxels, (o,))
    base_ref[...] = hgrad_ref[...] + mm(drt[...], hot[...], NT)
    back_t = mm(drt_far[...], far[...], NT)
    rims = 2 if slabs == 2 else 3
    rim = [back_t[:, i * RIM : (i + 1) * RIM] for i in range(3 * rims - 1)]
    mate, cross, side = rim[:rims], rim[rims : 2 * rims], rim[2 * rims :]
    own, away = (0, (1,)) if slabs == 2 else (1, (0, 2))
    mate_ref[...] = mate[own]
    parts = []
    for place, part in zip(away, side):
        parts += [mate[place], part]
    beside_ref[...] = jnp.concatenate(parts, axis=1)
    cross_ref[...] = jnp.concatenate(cross, axis=1).astype(BF16)


def cross_turn_kernel(own, beside_ref, got_ref, home_ref, *edge_refs):
    got = got_ref[...].astype(F32)
    rim = [got[:, i * RIM : (i + 1) * RIM] for i in range(got.shape[1] // RIM)]
    home_ref[...] = rim.pop(own)
    for i, (ref, part) in enumerate(zip(edge_refs, rim)):
        mine = beside_ref[:, 2 * i * RIM : 2 * (i + 1) * RIM]
        ref[...] = (mine + jnp.concatenate([jnp.zeros_like(part), part], axis=1)).astype(BF16)


def slab_turn_kernel(mate_ref, home_ref, *refs):
    got_refs, (rider_ref, sum_ref) = refs[:-2], refs[-2:]
    got = got_refs[0][...].astype(F32)
    for ref in got_refs[1:]:
        got += ref[...].astype(F32)
    mate = mate_ref[...] + got[:, :RIM]
    sum_ref[...] = home_ref[...] + got[:, RIM:]
    pair = jnp.concatenate([mate, jnp.zeros_like(mate)], axis=1).astype(BF16)
    for i in range(rider_ref.shape[0]):
        rider_ref[i] = pair[i * TILE : (i + 1) * TILE, :]


def step_of(steps, core):
    return jnp.where(core == 0, *steps)


def split_kernel(orders, core_ref, here_ref, own_ref, got_ref, *piece_refs):
    length = piece_refs[0].shape[0]
    for ref, steps in zip(piece_refs, ((0, 0),) + orders):
        rows = pl.ds((here_ref[0] ^ step_of(steps, core_ref[0])) * length, length)
        ref[...] = (own_ref[rows] + got_ref[rows].astype(F32)).astype(ref.dtype)


def join_kernel(orders, core_ref, here_ref, *refs):
    piece_refs, rider_ref, full_ref = refs[:-2], refs[-2], refs[-1]
    length = piece_refs[0].shape[0]
    for ref, steps in zip(piece_refs, ((0, 0),) + orders):
        place = here_ref[0] ^ step_of(steps, core_ref[0])
        full_ref[pl.ds(place * length, length)] = ref[...]
    full_ref[len(piece_refs) * length :] = rider_ref[...]


def write_half(taps, half, tiles_ref, conv_ref, down_ref, conv_half, down_half, sems):
    channels, conv_columns = conv_ref.shape
    tiles = half_tiles(channels, conv_columns, taps)
    copies = []
    for wanted, buffer, whole in ((1, down_half, down_ref), (0, conv_half, conv_ref)):
        for i, (kind, row, column, columns) in enumerate(tiles):
            if kind == wanted:
                value = tiles_ref[i].astype(F32)[:, :columns]
                buffer[row : row + TILE, column : column + columns] = value
        rows = buffer.shape[0]
        start = pl.multiple_of(half * rows, TILE)
        copy = pltpu.make_async_copy(buffer, whole.at[pl.ds(start, rows)], sems.at[wanted])
        copy.start()
        copies.append(copy)
    return copies


def first_half_kernel(taps, core_ref, mine_ref, conv_ref, down_ref, *scratch):
    for copy in write_half(taps, core_ref[0], mine_ref, conv_ref, down_ref, *scratch):
        copy.wait()


def other_half_kernel(taps, size, core_ref, other_ref, base_ref, home_ref, *refs):
    _, _, conv_ref, down_ref, grad_ref, *scratch = refs
    copies = write_half(taps, 1 - core_ref[0], other_ref, conv_ref, down_ref, *scratch)
    grad_ref[:, RIM:] = base_ref[:, RIM:]
    for i in range(base_ref.shape[0] // TILE):
        rows = slice(i * TILE, (i + 1) * TILE)
        total = base_ref[rows, :RIM] + home_ref[rows, :]
        grad_ref[rows, :RIM] = total + other_ref[size + i][:, :RIM].astype(F32)
    for copy in copies:
        copy.wait()


def shifts(count, step):
    return [(i, i + step) for i in range(count) if 0 <= i + step < count]


def chip_pairs(regions):
    mates = [(i, i ^ 1) for i in range(regions)]
    cross = [(i, i + 1) for i in range(1, regions - 1, 2)]
    return mates, cross + [(b, a) for a, b in cross]


def around_orders(nears, slabs):
    count = nears * slabs
    if count == 4:
        return ((3, 3), (2, 1), (1, 2))
    return tuple((i, i) for i in range(count - 1, 0, -1))


def around_pairs(sizes, steps):
    pairs = []
    slabs = sizes["slab"]
    for far in range(sizes["far"]):
        for here in range(sizes["near"] * slabs):
            for core in range(2):
                spots = []
                for spot in (here, here ^ steps[core]):
                    near, slab = divmod(spot, slabs)
                    spots.append(((far * sizes["near"] + near) * 2 + core) * slabs + slab)
                pairs.append(tuple(spots))
    return pairs


def on_device(features, neighbours, down_map, w_conv, w_down, coarse_grad):
    sizes = {axis: lax.axis_size(axis) for axis in SPLIT}
    regions, slabs = sizes["far"] * sizes["near"] * sizes["core"], sizes["slab"]
    voxels, channels = features.shape
    offsets, taps = neighbours.shape[1], down_map.shape[1]
    conv_columns = offsets * channels
    core = lax.axis_index("core").astype(jnp.int32).reshape(1)
    swap = [(0, 1), (1, 0)]
    mates, crossings = chip_pairs(regions)
    here = lax.axis_index(("near", "slab")).astype(jnp.int32).reshape(1)
    orders = around_orders(sizes["near"], slabs)
    routes = [around_pairs(sizes, steps) for steps in orders]
    squares = len(orders) + 1

    smem = pl.BlockSpec(memory_space=pltpu.SMEM)
    vmem = pl.BlockSpec(memory_space=pltpu.VMEM)
    params = pltpu.CompilerParams(vmem_limit_bytes=VMEM_BYTES)
    light = pl.CostEstimate(flops=2 * 10**9, bytes_accessed=10**7, transcendentals=0)
    features_t, neighbours_t, w_conv_t = features.T, neighbours.T, w_conv.T
    rim = features_t[:, :RIM]
    if slabs == 2:
        beside = [swap]
    else:
        beside = [shifts(slabs, 1), shifts(slabs, -1)]
    side = [lax.ppermute(features_t, "slab", pairs) for pairs in beside]
    own = pl.pallas_call(
        functools.partial(gather_kernel, slabs),
        out_shape=(
            jax.ShapeDtypeStruct((conv_columns, LANES), BF16),
            jax.ShapeDtypeStruct((conv_columns, voxels - LANES), BF16),
        ),
        compiler_params=params,
        cost_estimate=light,
        name="gather",
    )(features_t, neighbours_t)
    side, own = lax.optimization_barrier((side, own))
    side = [x[:, :RIM] for x in side]
    row = [rim, side[0]] if slabs == 2 else [side[0], rim, side[1]]
    row = jnp.concatenate(row, axis=1)
    cross = lax.ppermute(row, RING, crossings)
    row, down_t = lax.optimization_barrier((row, down_map.T))
    pick, hgrad = pl.pallas_call(
        taps_kernel,
        out_shape=(
            jax.ShapeDtypeStruct((taps, coarse_grad.shape[0], voxels), BF16),
            jax.ShapeDtypeStruct((channels, voxels), F32),
        ),
        compiler_params=params,
        cost_estimate=light,
        name="taps",
    )(down_t, coarse_grad, w_down)
    mate = lax.ppermute(row, RING, mates)
    halos = [mate, cross, *side]
    far_rows = -(-sum(x.shape[1] for x in halos) // LANES) * LANES

    tiles = len(half_tiles(channels, conv_columns, taps))
    size = -(-tiles // squares) * squares
    grad, hidden, keep, send = pl.pallas_call(
        functools.partial(forward_kernel, slabs),
        out_shape=(
            jax.ShapeDtypeStruct((channels, voxels), BF16),
            jax.ShapeDtypeStruct((channels, voxels), BF16),
            jax.ShapeDtypeStruct((size, TILE, LANES), F32),
            jax.ShapeDtypeStruct((size, TILE, LANES), BF16),
        ),
        in_specs=[smem] + [vmem] * (8 + len(halos)),
        scratch_shapes=[
            pltpu.VMEM((conv_columns, voxels), BF16),
            pltpu.VMEM((channels, -(-conv_columns // LANES) * LANES), F32),
            pltpu.VMEM((taps * channels, LANES), F32),
        ],
        compiler_params=params,
        name="forward",
    )(core, features_t, neighbours_t, coarse_grad, w_conv_t, *own, pick, hgrad, *halos)

    got = lax.ppermute(send, "core", swap)
    piece = size // squares
    keep, *sent = pl.pallas_call(
        functools.partial(split_kernel, orders),
        out_shape=[
            jax.ShapeDtypeStruct((piece, TILE, LANES), BF16 if i else F32) for i in range(squares)
        ],
        in_specs=[smem, smem, vmem, vmem],
        compiler_params=params,
        name="split",
    )(core, here, keep, got)
    sent, grad = lax.optimization_barrier((sent, grad))
    got = [lax.ppermute(x, SPLIT, route) for x, route in zip(sent, routes)]
    base, mate, stay, cross = pl.pallas_call(
        functools.partial(backward_kernel, slabs),
        out_shape=(
            jax.ShapeDtypeStruct((channels, voxels), F32),
            jax.ShapeDtypeStruct((channels, RIM), F32),
            jax.ShapeDtypeStruct((channels, 2 * len(beside) * RIM), F32),
            jax.ShapeDtypeStruct((channels, row.shape[1]), BF16),
        ),
        in_specs=[smem] + [vmem] * 4,
        scratch_shapes=[
            pltpu.VMEM((channels, offsets * voxels), BF16),
            pltpu.VMEM((channels, offsets * LANES), BF16),
            pltpu.VMEM((voxels, offsets * voxels), BF16),
            pltpu.VMEM((far_rows, offsets * LANES), BF16),
            pltpu.VMEM((conv_columns, LANES), BF16),
        ],
        compiler_params=params,
        cost_estimate=light,
        name="backward",
    )(core, neighbours_t, hgrad, grad, w_conv_t)
    got, cross, base = lax.optimization_barrier((got, cross, base))
    coarse = pl.pallas_call(
        coarse_kernel,
        out_shape=jax.ShapeDtypeStruct(coarse_grad.shape, BF16),
        compiler_params=params,
        cost_estimate=light,
        name="coarse",
    )(pick, hidden, w_down)
    total = functools.reduce(lambda x, y: x + y.astype(F32), got, keep).astype(BF16)
    parts = [total]
    for step in range(1, sizes["far"]):
        parts.append(lax.ppermute(total, "far", [(i, i ^ step) for i in range(sizes["far"])]))
    cross = lax.ppermute(cross, RING, crossings)
    parts = [x.astype(F32) for x in parts]
    while len(parts) > 1:
        parts = [x + y for x, y in zip(parts[0::2], parts[1::2])]
    total = parts[0].astype(BF16)
    total, cross = lax.optimization_barrier((total, cross))
    home, *edges = pl.pallas_call(
        functools.partial(cross_turn_kernel, 0 if slabs == 2 else 1),
        out_shape=[jax.ShapeDtypeStruct((channels, RIM), F32)]
        + [jax.ShapeDtypeStruct((channels, 2 * RIM), BF16)] * len(beside),
        compiler_params=params,
        name="cross_turn",
    )(stay, cross)
    back = beside if slabs == 2 else beside[::-1]
    edges = [lax.ppermute(x, "slab", p) for x, p in zip(edges, back)]
    edges, coarse = lax.optimization_barrier((edges, coarse))
    mate, home = pl.pallas_call(
        slab_turn_kernel,
        out_shape=(
            jax.ShapeDtypeStruct((channels // TILE, TILE, LANES), BF16),
            jax.ShapeDtypeStruct((channels, RIM), F32),
        ),
        compiler_params=params,
        name="slab_turn",
    )(mate, home, *edges)
    got = [lax.ppermute(total, SPLIT, route) for route in routes[::-1]]
    mine = pl.pallas_call(
        functools.partial(join_kernel, orders[::-1]),
        out_shape=jax.ShapeDtypeStruct((size + mate.shape[0], TILE, LANES), BF16),
        in_specs=[smem, smem] + [vmem] * (squares + 1),
        compiler_params=params,
        name="join",
    )(core, here, total, *got, mate)
    other = lax.ppermute(mine, "core", swap)
    weights = (
        jax.ShapeDtypeStruct((channels, conv_columns), F32),
        jax.ShapeDtypeStruct((taps * channels, LANES), F32),
    )
    halves = [pltpu.VMEM((x.shape[0] // 2, x.shape[1]), F32) for x in weights]
    scratch = halves + [pltpu.SemaphoreType.DMA((2,))]
    whole = pl.BlockSpec(memory_space=pl.ANY)
    conv_wgrad_t, down_wgrad = pl.pallas_call(
        functools.partial(first_half_kernel, taps),
        out_shape=weights,
        in_specs=[smem, vmem],
        out_specs=(whole, whole),
        scratch_shapes=scratch,
        compiler_params=params,
        name="first_half",
    )(core, mine)
    conv_wgrad_t, down_wgrad, grad_input_t = pl.pallas_call(
        functools.partial(other_half_kernel, taps, size),
        out_shape=(*weights, jax.ShapeDtypeStruct((channels, voxels), F32)),
        in_specs=[smem, vmem, vmem, vmem, whole, whole],
        out_specs=(whole, whole, vmem),
        input_output_aliases={4: 0, 5: 1},
        scratch_shapes=scratch,
        compiler_params=params,
        name="other_half",
    )(core, other, base, home, conv_wgrad_t, down_wgrad)
    return coarse, grad_input_t.T, conv_wgrad_t.T, down_wgrad


def solution(mesh):
    regions, slabs = mesh.shape["region"], mesh.shape["slab"]
    fine = Mesh(mesh.devices.reshape(regions // 4, 2, 2, slabs), SPLIT)
    split = P(SPLIT, None)
    return jax.shard_map(
        on_device,
        mesh=fine,
        in_specs=(split, split, split, P(), P(), split),
        out_specs=(split, split, P(), P()),
        check_vma=False,
    )
```

```python
import functools

import jax
import jax.numpy as jnp
from jax import lax
from jax.experimental import pallas as pl
from jax.experimental.pallas import tpu as pltpu
from jax.sharding import Mesh, PartitionSpec as P

SPLIT = ("far", "near", "core", "slab")
RING = ("far", "near", "core")
RIM = 64
LANES = 128
TILE = 16
F32 = jnp.float32
BF16 = jnp.bfloat16
NN = (((1,), (0,)), ((), ()))
NT = (((1,), (1,)), ((), ()))
VMEM_BYTES = 20 * 2**20


def mm(a, b, dims=NN):
    return lax.dot_general(a, b, dims, preferred_element_type=F32)


def table_lanes(neighbours, voxels, slabs, core):
    code = neighbours // voxels
    slot = neighbours - code * voxels
    row = code // 3
    col = code - row * 3
    if slabs == 2:
        rims = 2
        place = jnp.where(col == 1, 0, 1)
        beside = 0
    else:
        rims = 3
        place = col
        beside = col // 2
    group = jnp.abs(row // 2 + core - 1)
    rim = jnp.where(row == 1, 2 * rims + beside, group * rims + place)
    lane = jnp.where(code == 4, slot, voxels + rim * RIM + slot)
    return jnp.where(code > 8, -1, lane)


def payload_tiles(channels, conv_columns, taps):
    tiles = []
    for column in range(0, conv_columns, LANES):
        for row in range(0, channels, TILE):
            tiles.append((0, row, column, min(LANES, conv_columns - column)))
    for row in range(0, taps * channels, TILE):
        tiles.append((1, row, 0, LANES))
    return tiles


def padded_halo(halo_refs):
    halo = [h[...] for h in halo_refs]
    width = sum(h.shape[1] for h in halo)
    slack = -width % LANES
    if slack:
        halo.append(jnp.zeros((halo[0].shape[0], slack), BF16))
    return jnp.concatenate(halo, axis=1)


def gather_kernel(slabs, f_ref, near_ref, first_ref, rest_ref):
    channels, voxels = f_ref.shape
    table_t = f_ref[...]
    lanes = table_lanes(near_ref[...], voxels, slabs, 0)
    near_iota = lax.broadcasted_iota(jnp.int32, (voxels, voxels), 0)
    for o in range(near_ref.shape[0]):
        near = jnp.where(near_iota == lanes[o : o + 1, :], 1.0, 0.0).astype(BF16)
        own = mm(table_t, near).astype(BF16)
        first_ref[o * channels : (o + 1) * channels, :] = own[:, :LANES]
        rest_ref[o * channels : (o + 1) * channels, :] = own[:, LANES:]


def taps_kernel(down_ref, cgrad_ref, wd_ref, pick_ref, hgrad_ref):
    channels, voxels = hgrad_ref.shape
    taps, coarse_count = down_ref.shape
    cgrad_t = cgrad_ref[...].astype(F32).T.astype(BF16)
    down = down_ref[...].astype(F32).T
    lane_iota = lax.broadcasted_iota(jnp.int32, (coarse_count, voxels), 1).astype(F32)
    hgrad_t = jnp.zeros((channels, voxels), F32)
    for t in range(taps):
        pick = jnp.where(lane_iota == down[:, t : t + 1], 1.0, 0.0).astype(BF16)
        pick_ref[t] = pick
        wd = wd_ref[t * channels : (t + 1) * channels, :]
        hgrad_t += mm(wd, mm(cgrad_t, pick).astype(BF16))
    hgrad_ref[...] = hgrad_t


def far_one_hots(lanes, rows, voxels, offsets):
    iota = lax.broadcasted_iota(jnp.int32, (rows, LANES), 0) + voxels
    hots = [jnp.where(iota == lanes[o : o + 1, :LANES], 1.0, 0.0).astype(BF16) for o in offsets]
    return jnp.concatenate(hots, axis=1)


def forward_kernel(slabs, core_ref, f_ref, near_ref, cgrad_ref, w_ref, *refs):
    first_ref, rest_ref, pick_ref, hgrad_ref = refs[:4]
    halo_refs, refs = (refs[4:7], refs[7:]) if slabs == 2 else (refs[4:8], refs[8:])
    grad_ref, hidden_ref, keep_ref, send_ref, rt, conv_w, down_w = refs
    channels, voxels = f_ref.shape
    offsets = near_ref.shape[0]
    taps = pick_ref.shape[0]
    conv_columns = offsets * channels
    halo_t = padded_halo(halo_refs)
    lanes = table_lanes(near_ref[:, :LANES], voxels, slabs, core_ref[0])
    pack = 2 * LANES // RIM
    iota = lax.broadcasted_iota(jnp.int32, (halo_t.shape[1], 2 * LANES), 0) + voxels
    empty = jnp.zeros((channels, LANES - RIM), F32)
    for start in range(0, offsets, pack):
        group = [lanes[min(o, offsets - 1) : min(o, offsets - 1) + 1, :RIM] for o in range(start, start + pack)]
        hot = jnp.where(iota == jnp.concatenate(group, axis=1), 1.0, 0.0).astype(BF16)
        away = mm(halo_t, hot)
        for i, o in enumerate(range(start, min(start + pack, offsets))):
            rows = slice(o * channels, (o + 1) * channels)
            part = jnp.concatenate([away[:, i * RIM : (i + 1) * RIM], empty], axis=1)
            rt[rows, :LANES] = (first_ref[rows, :].astype(F32) + part).astype(BF16)
            rt[rows, LANES:] = rest_ref[rows, :]

    out_t = mm(w_ref[...], rt[...])
    sig = 1.0 / (1.0 + jnp.exp(-out_t))
    hidden_t = (f_ref[...].astype(F32) + out_t * sig).astype(BF16)
    grad_t = (hgrad_ref[...] * sig * (1.0 + out_t * (1.0 - sig))).astype(BF16)
    grad_ref[...] = grad_t
    conv_w[:, :conv_columns] = mm(grad_t, rt[...], NT)
    if conv_w.shape[1] > conv_columns:
        slack = conv_w.shape[1] - conv_columns
        conv_w[:, conv_columns:] = jnp.zeros((channels, slack), F32)

    hidden_ref[...] = hidden_t
    cgrad = cgrad_ref[...]
    for t in range(taps):
        picked_t = mm(hidden_t, pick_ref[t], NT).astype(BF16)
        down_w[t * channels : (t + 1) * channels, :] = mm(picked_t, cgrad)

    tiles = payload_tiles(channels, conv_columns, taps)
    size = keep_ref.shape[0]
    for core in range(2):

        @pl.when(core_ref[0] == core)
        def _(core=core):
            for i in range(2 * size):
                ref = keep_ref if i // size == core else send_ref
                if i < len(tiles):
                    kind, row, column, _ = tiles[i]
                    source = down_w if kind else conv_w
                    value = source[row : row + TILE, column : column + LANES]
                else:
                    value = jnp.zeros((TILE, LANES), F32)
                ref[i % size] = value.astype(ref.dtype)


def coarse_kernel(pick_ref, hidden_ref, wd_ref, coarse_ref):
    channels = hidden_ref.shape[0]
    coarse = jnp.zeros(coarse_ref.shape, F32)
    for t in range(pick_ref.shape[0]):
        picked = mm(pick_ref[t], hidden_ref[...], NT).astype(BF16)
        coarse += mm(picked, wd_ref[t * channels : (t + 1) * channels, :])
    coarse_ref[...] = coarse.astype(BF16)


def backward_kernel(slabs, core_ref, near_ref, hgrad_ref, grad_ref, w_ref, *refs):
    base_ref, mate_ref, beside_ref, cross_ref, drt, drt_far, hot, far, w_back = refs
    channels, voxels = hgrad_ref.shape
    offsets = near_ref.shape[0]
    lanes = table_lanes(near_ref[...], voxels, slabs, core_ref[0])
    near_iota = lax.broadcasted_iota(jnp.int32, (voxels, voxels), 0)
    w_back[:, :channels] = w_ref[...].astype(F32).T.astype(BF16)
    w_back[:, channels:] = jnp.zeros((offsets * channels, LANES - channels), BF16)
    slack = jnp.zeros((LANES - channels, voxels), BF16)
    grad_pad = jnp.concatenate([grad_ref[...], slack], axis=0)
    for o in range(offsets):
        near = jnp.where(near_iota == lanes[o : o + 1, :], 1.0, 0.0).astype(BF16)
        hot[:, o * voxels : (o + 1) * voxels] = near
        spread = mm(w_back[o * channels : (o + 1) * channels, :], grad_pad).astype(BF16)
        drt[:, o * voxels : (o + 1) * voxels] = spread
        drt_far[:, o * LANES : (o + 1) * LANES] = spread[:, :LANES]
        far[:, o * LANES : (o + 1) * LANES] = far_one_hots(lanes, far.shape[0], voxels, (o,))
    base_ref[...] = hgrad_ref[...] + mm(drt[...], hot[...], NT)
    back_t = mm(drt_far[...], far[...], NT)
    rims = 2 if slabs == 2 else 3
    rim = [back_t[:, i * RIM : (i + 1) * RIM] for i in range(3 * rims - 1)]
    mate, cross, side = rim[:rims], rim[rims : 2 * rims], rim[2 * rims :]
    own, away = (0, (1,)) if slabs == 2 else (1, (0, 2))
    mate_ref[...] = mate[own]
    parts = []
    for place, part in zip(away, side):
        parts += [mate[place], part]
    beside_ref[...] = jnp.concatenate(parts, axis=1)
    cross_ref[...] = jnp.concatenate(cross, axis=1).astype(BF16)


def cross_turn_kernel(own, beside_ref, got_ref, home_ref, *edge_refs):
    got = got_ref[...].astype(F32)
    rim = [got[:, i * RIM : (i + 1) * RIM] for i in range(got.shape[1] // RIM)]
    home_ref[...] = rim.pop(own)
    for i, (ref, part) in enumerate(zip(edge_refs, rim)):
        mine = beside_ref[:, 2 * i * RIM : 2 * (i + 1) * RIM]
        ref[...] = (mine + jnp.concatenate([jnp.zeros_like(part), part], axis=1)).astype(BF16)


def slab_turn_kernel(mate_ref, home_ref, *refs):
    got_refs, (rider_ref, sum_ref) = refs[:-2], refs[-2:]
    got = got_refs[0][...].astype(F32)
    for ref in got_refs[1:]:
        got += ref[...].astype(F32)
    mate = mate_ref[...] + got[:, :RIM]
    sum_ref[...] = home_ref[...] + got[:, RIM:]
    pair = jnp.concatenate([mate, jnp.zeros_like(mate)], axis=1).astype(BF16)
    for i in range(rider_ref.shape[0]):
        rider_ref[i] = pair[i * TILE : (i + 1) * TILE, :]


def step_of(steps, core):
    return jnp.where(core == 0, *steps)


def split_kernel(orders, core_ref, here_ref, own_ref, got_ref, *piece_refs):
    length = piece_refs[0].shape[0]
    for ref, steps in zip(piece_refs, ((0, 0),) + orders):
        rows = pl.ds((here_ref[0] ^ step_of(steps, core_ref[0])) * length, length)
        ref[...] = (own_ref[rows] + got_ref[rows].astype(F32)).astype(ref.dtype)


def join_kernel(orders, core_ref, here_ref, *refs):
    piece_refs, rider_ref, full_ref = refs[:-2], refs[-2], refs[-1]
    length = piece_refs[0].shape[0]
    for ref, steps in zip(piece_refs, ((0, 0),) + orders):
        place = here_ref[0] ^ step_of(steps, core_ref[0])
        full_ref[pl.ds(place * length, length)] = ref[...]
    full_ref[len(piece_refs) * length :] = rider_ref[...]


def final_kernel(taps, size, core_ref, mine_ref, other_ref, *refs):
    base_ref, home_ref, conv_ref, down_ref, grad_ref = refs
    channels, conv_columns = conv_ref.shape
    grad_ref[:, RIM:] = base_ref[:, RIM:]
    for i in range(channels // TILE):
        rows = slice(i * TILE, (i + 1) * TILE)
        total = base_ref[rows, :RIM] + home_ref[rows, :]
        grad_ref[rows, :RIM] = total + other_ref[size + i][:, :RIM].astype(F32)
    for core in range(2):

        @pl.when(core_ref[0] == core)
        def _(core=core):
            for i, tile in enumerate(payload_tiles(channels, conv_columns, taps)):
                kind, row, column, columns = tile
                source = mine_ref if i // size == core else other_ref
                value = source[i % size].astype(F32)
                target = down_ref if kind else conv_ref
                target[row : row + TILE, column : column + columns] = value[:, :columns]


def shifts(count, step):
    return [(i, i + step) for i in range(count) if 0 <= i + step < count]


def chip_pairs(regions):
    mates = [(i, i ^ 1) for i in range(regions)]
    cross = [(i, i + 1) for i in range(1, regions - 1, 2)]
    return mates, cross + [(b, a) for a, b in cross]


def around_orders(nears, slabs):
    count = nears * slabs
    if count == 4:
        return ((3, 3), (2, 1), (1, 2))
    return tuple((i, i) for i in range(count - 1, 0, -1))


def around_pairs(sizes, steps):
    pairs = []
    slabs = sizes["slab"]
    for far in range(sizes["far"]):
        for here in range(sizes["near"] * slabs):
            for core in range(2):
                spots = []
                for spot in (here, here ^ steps[core]):
                    near, slab = divmod(spot, slabs)
                    spots.append(((far * sizes["near"] + near) * 2 + core) * slabs + slab)
                pairs.append(tuple(spots))
    return pairs


def on_device(features, neighbours, down_map, w_conv, w_down, coarse_grad):
    sizes = {axis: lax.axis_size(axis) for axis in SPLIT}
    regions, slabs = sizes["far"] * sizes["near"] * sizes["core"], sizes["slab"]
    voxels, channels = features.shape
    offsets, taps = neighbours.shape[1], down_map.shape[1]
    conv_columns = offsets * channels
    core = lax.axis_index("core").astype(jnp.int32).reshape(1)
    swap = [(0, 1), (1, 0)]
    mates, crossings = chip_pairs(regions)
    here = lax.axis_index(("near", "slab")).astype(jnp.int32).reshape(1)
    orders = around_orders(sizes["near"], slabs)
    routes = [around_pairs(sizes, steps) for steps in orders]
    squares = len(orders) + 1

    smem = pl.BlockSpec(memory_space=pltpu.SMEM)
    vmem = pl.BlockSpec(memory_space=pltpu.VMEM)
    params = pltpu.CompilerParams(vmem_limit_bytes=VMEM_BYTES)
    light = pl.CostEstimate(flops=2 * 10**9, bytes_accessed=10**7, transcendentals=0)
    features_t, neighbours_t, w_conv_t = features.T, neighbours.T, w_conv.T
    rim = features_t[:, :RIM]
    if slabs == 2:
        beside = [swap]
    else:
        beside = [shifts(slabs, 1), shifts(slabs, -1)]
    side = [lax.ppermute(features_t, "slab", pairs) for pairs in beside]
    own = pl.pallas_call(
        functools.partial(gather_kernel, slabs),
        out_shape=(
            jax.ShapeDtypeStruct((conv_columns, LANES), BF16),
            jax.ShapeDtypeStruct((conv_columns, voxels - LANES), BF16),
        ),
        compiler_params=params,
        cost_estimate=light,
        name="gather",
    )(features_t, neighbours_t)
    side, own = lax.optimization_barrier((side, own))
    side = [x[:, :RIM] for x in side]
    row = [rim, side[0]] if slabs == 2 else [side[0], rim, side[1]]
    row = jnp.concatenate(row, axis=1)
    cross = lax.ppermute(row, RING, crossings)
    row, down_t = lax.optimization_barrier((row, down_map.T))
    pick, hgrad = pl.pallas_call(
        taps_kernel,
        out_shape=(
            jax.ShapeDtypeStruct((taps, coarse_grad.shape[0], voxels), BF16),
            jax.ShapeDtypeStruct((channels, voxels), F32),
        ),
        compiler_params=params,
        cost_estimate=light,
        name="taps",
    )(down_t, coarse_grad, w_down)
    row, pick, hgrad = lax.optimization_barrier((row, pick, hgrad))
    mate = lax.ppermute(row, RING, mates)
    halos = [mate, cross, *side]
    far_rows = -(-sum(x.shape[1] for x in halos) // LANES) * LANES

    tiles = len(payload_tiles(channels, conv_columns, taps))
    size = -(-tiles // (2 * squares)) * squares
    grad, hidden, keep, send = pl.pallas_call(
        functools.partial(forward_kernel, slabs),
        out_shape=(
            jax.ShapeDtypeStruct((channels, voxels), BF16),
            jax.ShapeDtypeStruct((channels, voxels), BF16),
            jax.ShapeDtypeStruct((size, TILE, LANES), F32),
            jax.ShapeDtypeStruct((size, TILE, LANES), BF16),
        ),
        in_specs=[smem] + [vmem] * (8 + len(halos)),
        scratch_shapes=[
            pltpu.VMEM((conv_columns, voxels), BF16),
            pltpu.VMEM((channels, -(-conv_columns // LANES) * LANES), F32),
            pltpu.VMEM((taps * channels, LANES), F32),
        ],
        compiler_params=params,
        name="forward",
    )(core, features_t, neighbours_t, coarse_grad, w_conv_t, *own, pick, hgrad, *halos)

    got = lax.ppermute(send, "core", swap)
    piece = size // squares
    keep, *sent = pl.pallas_call(
        functools.partial(split_kernel, orders),
        out_shape=[
            jax.ShapeDtypeStruct((piece, TILE, LANES), BF16 if i else F32) for i in range(squares)
        ],
        in_specs=[smem, smem, vmem, vmem],
        compiler_params=params,
        name="split",
    )(core, here, keep, got)
    sent, grad = lax.optimization_barrier((sent, grad))
    got = [lax.ppermute(x, SPLIT, route) for x, route in zip(sent, routes)]
    base, mate, stay, cross = pl.pallas_call(
        functools.partial(backward_kernel, slabs),
        out_shape=(
            jax.ShapeDtypeStruct((channels, voxels), F32),
            jax.ShapeDtypeStruct((channels, RIM), F32),
            jax.ShapeDtypeStruct((channels, 2 * len(beside) * RIM), F32),
            jax.ShapeDtypeStruct((channels, row.shape[1]), BF16),
        ),
        in_specs=[smem] + [vmem] * 4,
        scratch_shapes=[
            pltpu.VMEM((channels, offsets * voxels), BF16),
            pltpu.VMEM((channels, offsets * LANES), BF16),
            pltpu.VMEM((voxels, offsets * voxels), BF16),
            pltpu.VMEM((far_rows, offsets * LANES), BF16),
            pltpu.VMEM((conv_columns, LANES), BF16),
        ],
        compiler_params=params,
        cost_estimate=light,
        name="backward",
    )(core, neighbours_t, hgrad, grad, w_conv_t)
    got, cross, base = lax.optimization_barrier((got, cross, base))
    coarse = pl.pallas_call(
        coarse_kernel,
        out_shape=jax.ShapeDtypeStruct(coarse_grad.shape, BF16),
        compiler_params=params,
        cost_estimate=light,
        name="coarse",
    )(pick, hidden, w_down)
    total = functools.reduce(lambda x, y: x + y.astype(F32), got, keep).astype(BF16)
    parts = [total]
    for step in range(1, sizes["far"]):
        parts.append(lax.ppermute(total, "far", [(i, i ^ step) for i in range(sizes["far"])]))
    cross = lax.ppermute(cross, RING, crossings)
    parts = [x.astype(F32) for x in parts]
    while len(parts) > 1:
        parts = [x + y for x, y in zip(parts[0::2], parts[1::2])]
    total = parts[0].astype(BF16)
    total, cross = lax.optimization_barrier((total, cross))
    home, *edges = pl.pallas_call(
        functools.partial(cross_turn_kernel, 0 if slabs == 2 else 1),
        out_shape=[jax.ShapeDtypeStruct((channels, RIM), F32)]
        + [jax.ShapeDtypeStruct((channels, 2 * RIM), BF16)] * len(beside),
        compiler_params=params,
        name="cross_turn",
    )(stay, cross)
    back = beside if slabs == 2 else beside[::-1]
    edges = [lax.ppermute(x, "slab", p) for x, p in zip(edges, back)]
    edges, coarse = lax.optimization_barrier((edges, coarse))
    mate, home = pl.pallas_call(
        slab_turn_kernel,
        out_shape=(
            jax.ShapeDtypeStruct((channels // TILE, TILE, LANES), BF16),
            jax.ShapeDtypeStruct((channels, RIM), F32),
        ),
        compiler_params=params,
        name="slab_turn",
    )(mate, home, *edges)
    got = [lax.ppermute(total, SPLIT, route) for route in routes[::-1]]
    mine = pl.pallas_call(
        functools.partial(join_kernel, orders[::-1]),
        out_shape=jax.ShapeDtypeStruct((size + mate.shape[0], TILE, LANES), BF16),
        in_specs=[smem, smem] + [vmem] * (squares + 1),
        compiler_params=params,
        name="join",
    )(core, here, total, *got, mate)
    other = lax.ppermute(mine, "core", swap)
    conv_wgrad_t, down_wgrad, grad_input_t = pl.pallas_call(
        functools.partial(final_kernel, taps, size),
        out_shape=(
            jax.ShapeDtypeStruct((channels, conv_columns), F32),
            jax.ShapeDtypeStruct((taps * channels, LANES), F32),
            jax.ShapeDtypeStruct((channels, voxels), F32),
        ),
        in_specs=[smem] + [vmem] * 4,
        compiler_params=params,
        name="final",
    )(core, mine, other, base, home)
    return coarse, grad_input_t.T, conv_wgrad_t.T, down_wgrad


def solution(mesh):
    regions, slabs = mesh.shape["region"], mesh.shape["slab"]
    fine = Mesh(mesh.devices.reshape(regions // 4, 2, 2, slabs), SPLIT)
    split = P(SPLIT, None)
    return jax.shard_map(
        on_device,
        mesh=fine,
        in_specs=(split, split, split, P(), P(), split),
        out_specs=(split, split, P(), P()),
        check_vma=False,
    )
```

```python
import functools

import jax
import jax.numpy as jnp
from jax import lax
from jax.experimental import pallas as pl
from jax.experimental.pallas import tpu as pltpu
from jax.sharding import Mesh, PartitionSpec as P

SPLIT = ("far", "near", "core", "slab")
RING = ("far", "near", "core")
RIM = 64
LANES = 128
TILE = 16
F32 = jnp.float32
BF16 = jnp.bfloat16
NN = (((1,), (0,)), ((), ()))
NT = (((1,), (1,)), ((), ()))
VMEM_BYTES = 20 * 2**20


def mm(a, b, dims=NN):
    return lax.dot_general(a, b, dims, preferred_element_type=F32)


def table_lanes(neighbours, voxels, slabs, core):
    code = neighbours // voxels
    slot = neighbours - code * voxels
    row = code // 3
    col = code - row * 3
    if slabs == 2:
        rims = 2
        place = jnp.where(col == 1, 0, 1)
        beside = 0
    else:
        rims = 3
        place = col
        beside = col // 2
    group = jnp.abs(row // 2 + core - 1)
    rim = jnp.where(row == 1, 2 * rims + beside, group * rims + place)
    lane = jnp.where(code == 4, slot, voxels + rim * RIM + slot)
    return jnp.where(code > 8, -1, lane)


def payload_tiles(channels, conv_columns, taps):
    tiles = []
    for column in range(0, conv_columns, LANES):
        for row in range(0, channels, TILE):
            tiles.append((0, row, column, min(LANES, conv_columns - column)))
    for row in range(0, taps * channels, TILE):
        tiles.append((1, row, 0, LANES))
    return tiles


def padded_halo(halo_refs):
    halo = [h[...] for h in halo_refs]
    width = sum(h.shape[1] for h in halo)
    slack = -width % LANES
    if slack:
        halo.append(jnp.zeros((halo[0].shape[0], slack), BF16))
    return jnp.concatenate(halo, axis=1)


def gather_kernel(slabs, f_ref, near_ref, first_ref, rest_ref):
    channels, voxels = f_ref.shape
    table_t = f_ref[...]
    lanes = table_lanes(near_ref[...], voxels, slabs, 0)
    near_iota = lax.broadcasted_iota(jnp.int32, (voxels, voxels), 0)
    for o in range(near_ref.shape[0]):
        near = jnp.where(near_iota == lanes[o : o + 1, :], 1.0, 0.0).astype(BF16)
        own = mm(table_t, near).astype(BF16)
        first_ref[o * channels : (o + 1) * channels, :] = own[:, :LANES]
        rest_ref[o * channels : (o + 1) * channels, :] = own[:, LANES:]


def taps_kernel(down_ref, cgrad_ref, wd_ref, pick_ref, hgrad_ref):
    channels, voxels = hgrad_ref.shape
    taps, coarse_count = down_ref.shape
    cgrad_t = cgrad_ref[...].astype(F32).T.astype(BF16)
    down = down_ref[...].astype(F32).T
    lane_iota = lax.broadcasted_iota(jnp.int32, (coarse_count, voxels), 1).astype(F32)
    hgrad_t = jnp.zeros((channels, voxels), F32)
    for t in range(taps):
        pick = jnp.where(lane_iota == down[:, t : t + 1], 1.0, 0.0).astype(BF16)
        pick_ref[t] = pick
        wd = wd_ref[t * channels : (t + 1) * channels, :]
        hgrad_t += mm(wd, mm(cgrad_t, pick).astype(BF16))
    hgrad_ref[...] = hgrad_t


def far_one_hots(lanes, rows, voxels, offsets):
    iota = lax.broadcasted_iota(jnp.int32, (rows, LANES), 0) + voxels
    hots = [jnp.where(iota == lanes[o : o + 1, :LANES], 1.0, 0.0).astype(BF16) for o in offsets]
    return jnp.concatenate(hots, axis=1)


def forward_kernel(slabs, core_ref, f_ref, near_ref, cgrad_ref, w_ref, *refs):
    first_ref, rest_ref, pick_ref, hgrad_ref = refs[:4]
    halo_refs, refs = (refs[4:7], refs[7:]) if slabs == 2 else (refs[4:8], refs[8:])
    grad_ref, hidden_ref, keep_ref, send_ref, rt, conv_w, down_w = refs
    channels, voxels = f_ref.shape
    offsets = near_ref.shape[0]
    taps = pick_ref.shape[0]
    conv_columns = offsets * channels
    halo_t = padded_halo(halo_refs)
    lanes = table_lanes(near_ref[:, :LANES], voxels, slabs, core_ref[0])
    pack = 2 * LANES // RIM
    iota = lax.broadcasted_iota(jnp.int32, (halo_t.shape[1], 2 * LANES), 0) + voxels
    empty = jnp.zeros((channels, LANES - RIM), F32)
    for start in range(0, offsets, pack):
        group = [lanes[min(o, offsets - 1) : min(o, offsets - 1) + 1, :RIM] for o in range(start, start + pack)]
        hot = jnp.where(iota == jnp.concatenate(group, axis=1), 1.0, 0.0).astype(BF16)
        away = mm(halo_t, hot)
        for i, o in enumerate(range(start, min(start + pack, offsets))):
            rows = slice(o * channels, (o + 1) * channels)
            part = jnp.concatenate([away[:, i * RIM : (i + 1) * RIM], empty], axis=1)
            rt[rows, :LANES] = (first_ref[rows, :].astype(F32) + part).astype(BF16)
            rt[rows, LANES:] = rest_ref[rows, :]

    out_t = mm(w_ref[...], rt[...])
    sig = 1.0 / (1.0 + jnp.exp(-out_t))
    hidden_t = (f_ref[...].astype(F32) + out_t * sig).astype(BF16)
    grad_t = (hgrad_ref[...] * sig * (1.0 + out_t * (1.0 - sig))).astype(BF16)
    grad_ref[...] = grad_t
    conv_w[:, :conv_columns] = mm(grad_t, rt[...], NT)
    if conv_w.shape[1] > conv_columns:
        slack = conv_w.shape[1] - conv_columns
        conv_w[:, conv_columns:] = jnp.zeros((channels, slack), F32)

    hidden_ref[...] = hidden_t
    cgrad = cgrad_ref[...]
    for t in range(taps):
        picked_t = mm(hidden_t, pick_ref[t], NT).astype(BF16)
        down_w[t * channels : (t + 1) * channels, :] = mm(picked_t, cgrad)

    tiles = payload_tiles(channels, conv_columns, taps)
    size = keep_ref.shape[0]
    for core in range(2):

        @pl.when(core_ref[0] == core)
        def _(core=core):
            for i in range(2 * size):
                ref = keep_ref if i // size == core else send_ref
                if i < len(tiles):
                    kind, row, column, _ = tiles[i]
                    source = down_w if kind else conv_w
                    value = source[row : row + TILE, column : column + LANES]
                else:
                    value = jnp.zeros((TILE, LANES), F32)
                ref[i % size] = value.astype(ref.dtype)


def coarse_kernel(pick_ref, hidden_ref, wd_ref, coarse_ref):
    channels = hidden_ref.shape[0]
    coarse = jnp.zeros(coarse_ref.shape, F32)
    for t in range(pick_ref.shape[0]):
        picked = mm(pick_ref[t], hidden_ref[...], NT).astype(BF16)
        coarse += mm(picked, wd_ref[t * channels : (t + 1) * channels, :])
    coarse_ref[...] = coarse.astype(BF16)


def backward_kernel(slabs, core_ref, near_ref, hgrad_ref, grad_ref, w_ref, *refs):
    base_ref, mate_ref, beside_ref, cross_ref, drt, drt_far, hot, far, w_back = refs
    channels, voxels = hgrad_ref.shape
    offsets = near_ref.shape[0]
    lanes = table_lanes(near_ref[...], voxels, slabs, core_ref[0])
    near_iota = lax.broadcasted_iota(jnp.int32, (voxels, voxels), 0)
    w_back[:, :channels] = w_ref[...].astype(F32).T.astype(BF16)
    w_back[:, channels:] = jnp.zeros((offsets * channels, LANES - channels), BF16)
    slack = jnp.zeros((LANES - channels, voxels), BF16)
    grad_pad = jnp.concatenate([grad_ref[...], slack], axis=0)
    for o in range(offsets):
        near = jnp.where(near_iota == lanes[o : o + 1, :], 1.0, 0.0).astype(BF16)
        hot[:, o * voxels : (o + 1) * voxels] = near
        spread = mm(w_back[o * channels : (o + 1) * channels, :], grad_pad).astype(BF16)
        drt[:, o * voxels : (o + 1) * voxels] = spread
        drt_far[:, o * LANES : (o + 1) * LANES] = spread[:, :LANES]
        far[:, o * LANES : (o + 1) * LANES] = far_one_hots(lanes, far.shape[0], voxels, (o,))
    base_ref[...] = hgrad_ref[...] + mm(drt[...], hot[...], NT)
    back_t = mm(drt_far[...], far[...], NT)
    rims = 2 if slabs == 2 else 3
    rim = [back_t[:, i * RIM : (i + 1) * RIM] for i in range(3 * rims - 1)]
    mate, cross, side = rim[:rims], rim[rims : 2 * rims], rim[2 * rims :]
    own, away = (0, (1,)) if slabs == 2 else (1, (0, 2))
    mate_ref[...] = mate[own]
    parts = []
    for place, part in zip(away, side):
        parts += [mate[place], part]
    beside_ref[...] = jnp.concatenate(parts, axis=1)
    cross_ref[...] = jnp.concatenate(cross, axis=1).astype(BF16)


def cross_turn_kernel(own, beside_ref, got_ref, home_ref, *edge_refs):
    got = got_ref[...].astype(F32)
    rim = [got[:, i * RIM : (i + 1) * RIM] for i in range(got.shape[1] // RIM)]
    home_ref[...] = rim.pop(own)
    for i, (ref, part) in enumerate(zip(edge_refs, rim)):
        mine = beside_ref[:, 2 * i * RIM : 2 * (i + 1) * RIM]
        ref[...] = (mine + jnp.concatenate([jnp.zeros_like(part), part], axis=1)).astype(BF16)


def slab_turn_kernel(mate_ref, home_ref, *refs):
    got_refs, (rider_ref, sum_ref) = refs[:-2], refs[-2:]
    got = got_refs[0][...].astype(F32)
    for ref in got_refs[1:]:
        got += ref[...].astype(F32)
    mate = mate_ref[...] + got[:, :RIM]
    sum_ref[...] = home_ref[...] + got[:, RIM:]
    pair = jnp.concatenate([mate, jnp.zeros_like(mate)], axis=1).astype(BF16)
    for i in range(rider_ref.shape[0]):
        rider_ref[i] = pair[i * TILE : (i + 1) * TILE, :]


def step_of(steps, core):
    return jnp.where(core == 0, *steps)


def split_kernel(orders, core_ref, here_ref, own_ref, got_ref, *piece_refs):
    length = piece_refs[0].shape[0]
    for ref, steps in zip(piece_refs, ((0, 0),) + orders):
        rows = pl.ds((here_ref[0] ^ step_of(steps, core_ref[0])) * length, length)
        ref[...] = (own_ref[rows] + got_ref[rows].astype(F32)).astype(ref.dtype)


def join_kernel(orders, core_ref, here_ref, *refs):
    piece_refs, rider_ref, full_ref = refs[:-2], refs[-2], refs[-1]
    length = piece_refs[0].shape[0]
    for ref, steps in zip(piece_refs, ((0, 0),) + orders):
        place = here_ref[0] ^ step_of(steps, core_ref[0])
        full_ref[pl.ds(place * length, length)] = ref[...]
    full_ref[len(piece_refs) * length :] = rider_ref[...]


def final_kernel(taps, size, core_ref, mine_ref, other_ref, *refs):
    base_ref, home_ref, conv_ref, down_ref, grad_ref = refs
    channels, conv_columns = conv_ref.shape
    grad_ref[:, RIM:] = base_ref[:, RIM:]
    for i in range(channels // TILE):
        rows = slice(i * TILE, (i + 1) * TILE)
        total = base_ref[rows, :RIM] + home_ref[rows, :]
        grad_ref[rows, :RIM] = total + other_ref[size + i][:, :RIM].astype(F32)
    for core in range(2):

        @pl.when(core_ref[0] == core)
        def _(core=core):
            for i, tile in enumerate(payload_tiles(channels, conv_columns, taps)):
                kind, row, column, columns = tile
                source = mine_ref if i // size == core else other_ref
                value = source[i % size].astype(F32)
                target = down_ref if kind else conv_ref
                target[row : row + TILE, column : column + columns] = value[:, :columns]


def shifts(count, step):
    return [(i, i + step) for i in range(count) if 0 <= i + step < count]


def chip_pairs(regions):
    mates = [(i, i ^ 1) for i in range(regions)]
    cross = [(i, i + 1) for i in range(1, regions - 1, 2)]
    return mates, cross + [(b, a) for a, b in cross]


def around_orders(nears, slabs):
    count = nears * slabs
    if count == 4:
        return ((3, 3), (2, 1), (1, 2))
    return tuple((i, i) for i in range(count - 1, 0, -1))


def around_pairs(sizes, steps):
    pairs = []
    slabs = sizes["slab"]
    for far in range(sizes["far"]):
        for here in range(sizes["near"] * slabs):
            for core in range(2):
                spots = []
                for spot in (here, here ^ steps[core]):
                    near, slab = divmod(spot, slabs)
                    spots.append(((far * sizes["near"] + near) * 2 + core) * slabs + slab)
                pairs.append(tuple(spots))
    return pairs


def on_device(features, neighbours, down_map, w_conv, w_down, coarse_grad):
    sizes = {axis: lax.axis_size(axis) for axis in SPLIT}
    regions, slabs = sizes["far"] * sizes["near"] * sizes["core"], sizes["slab"]
    voxels, channels = features.shape
    offsets, taps = neighbours.shape[1], down_map.shape[1]
    conv_columns = offsets * channels
    core = lax.axis_index("core").astype(jnp.int32).reshape(1)
    swap = [(0, 1), (1, 0)]
    mates, crossings = chip_pairs(regions)
    here = lax.axis_index(("near", "slab")).astype(jnp.int32).reshape(1)
    orders = around_orders(sizes["near"], slabs)
    routes = [around_pairs(sizes, steps) for steps in orders]
    squares = len(orders) + 1

    smem = pl.BlockSpec(memory_space=pltpu.SMEM)
    vmem = pl.BlockSpec(memory_space=pltpu.VMEM)
    params = pltpu.CompilerParams(vmem_limit_bytes=VMEM_BYTES)
    light = pl.CostEstimate(flops=2 * 10**9, bytes_accessed=10**7, transcendentals=0)
    features_t, neighbours_t, w_conv_t = features.T, neighbours.T, w_conv.T
    rim = features_t[:, :RIM]
    if slabs == 2:
        beside = [swap]
    else:
        beside = [shifts(slabs, 1), shifts(slabs, -1)]
    side = [lax.ppermute(features_t, "slab", pairs) for pairs in beside]
    own = pl.pallas_call(
        functools.partial(gather_kernel, slabs),
        out_shape=(
            jax.ShapeDtypeStruct((conv_columns, LANES), BF16),
            jax.ShapeDtypeStruct((conv_columns, voxels - LANES), BF16),
        ),
        compiler_params=params,
        cost_estimate=light,
        name="gather",
    )(features_t, neighbours_t)
    side, own = lax.optimization_barrier((side, own))
    side = [x[:, :RIM] for x in side]
    row = [rim, side[0]] if slabs == 2 else [side[0], rim, side[1]]
    row = jnp.concatenate(row, axis=1)
    cross = lax.ppermute(row, RING, crossings)
    row, down_t = lax.optimization_barrier((row, down_map.T))
    pick, hgrad = pl.pallas_call(
        taps_kernel,
        out_shape=(
            jax.ShapeDtypeStruct((taps, coarse_grad.shape[0], voxels), BF16),
            jax.ShapeDtypeStruct((channels, voxels), F32),
        ),
        compiler_params=params,
        cost_estimate=light,
        name="taps",
    )(down_t, coarse_grad, w_down)
    row, pick, hgrad = lax.optimization_barrier((row, pick, hgrad))
    mate = lax.ppermute(row, RING, mates)
    halos = [mate, cross, *side]
    far_rows = -(-sum(x.shape[1] for x in halos) // LANES) * LANES

    tiles = len(payload_tiles(channels, conv_columns, taps))
    size = -(-tiles // (2 * squares)) * squares
    grad, hidden, keep, send = pl.pallas_call(
        functools.partial(forward_kernel, slabs),
        out_shape=(
            jax.ShapeDtypeStruct((channels, voxels), BF16),
            jax.ShapeDtypeStruct((channels, voxels), BF16),
            jax.ShapeDtypeStruct((size, TILE, LANES), F32),
            jax.ShapeDtypeStruct((size, TILE, LANES), BF16),
        ),
        in_specs=[smem] + [vmem] * (8 + len(halos)),
        scratch_shapes=[
            pltpu.VMEM((conv_columns, voxels), BF16),
            pltpu.VMEM((channels, -(-conv_columns // LANES) * LANES), F32),
            pltpu.VMEM((taps * channels, LANES), F32),
        ],
        compiler_params=params,
        name="forward",
    )(core, features_t, neighbours_t, coarse_grad, w_conv_t, *own, pick, hgrad, *halos)

    got = lax.ppermute(send, "core", swap)
    piece = size // squares
    keep, *sent = pl.pallas_call(
        functools.partial(split_kernel, orders),
        out_shape=[
            jax.ShapeDtypeStruct((piece, TILE, LANES), BF16 if i else F32) for i in range(squares)
        ],
        in_specs=[smem, smem, vmem, vmem],
        compiler_params=params,
        name="split",
    )(core, here, keep, got)
    sent, grad = lax.optimization_barrier((sent, grad))
    got = [lax.ppermute(x, SPLIT, route) for x, route in zip(sent, routes)]
    base, mate, stay, cross = pl.pallas_call(
        functools.partial(backward_kernel, slabs),
        out_shape=(
            jax.ShapeDtypeStruct((channels, voxels), F32),
            jax.ShapeDtypeStruct((channels, RIM), F32),
            jax.ShapeDtypeStruct((channels, 2 * len(beside) * RIM), F32),
            jax.ShapeDtypeStruct((channels, row.shape[1]), BF16),
        ),
        in_specs=[smem] + [vmem] * 4,
        scratch_shapes=[
            pltpu.VMEM((channels, offsets * voxels), BF16),
            pltpu.VMEM((channels, offsets * LANES), BF16),
            pltpu.VMEM((voxels, offsets * voxels), BF16),
            pltpu.VMEM((far_rows, offsets * LANES), BF16),
            pltpu.VMEM((conv_columns, LANES), BF16),
        ],
        compiler_params=params,
        cost_estimate=light,
        name="backward",
    )(core, neighbours_t, hgrad, grad, w_conv_t)
    got, cross, base = lax.optimization_barrier((got, cross, base))
    coarse = pl.pallas_call(
        coarse_kernel,
        out_shape=jax.ShapeDtypeStruct(coarse_grad.shape, BF16),
        compiler_params=params,
        cost_estimate=light,
        name="coarse",
    )(pick, hidden, w_down)
    total = functools.reduce(lambda x, y: x + y.astype(F32), got, keep).astype(BF16)
    parts = [total]
    for step in range(1, sizes["far"]):
        parts.append(lax.ppermute(total, "far", [(i, i ^ step) for i in range(sizes["far"])]))
    cross = lax.ppermute(cross, RING, crossings)
    parts = [x.astype(F32) for x in parts]
    while len(parts) > 1:
        parts = [x + y for x, y in zip(parts[0::2], parts[1::2])]
    total = parts[0].astype(BF16)
    home, *edges = pl.pallas_call(
        functools.partial(cross_turn_kernel, 0 if slabs == 2 else 1),
        out_shape=[jax.ShapeDtypeStruct((channels, RIM), F32)]
        + [jax.ShapeDtypeStruct((channels, 2 * RIM), BF16)] * len(beside),
        compiler_params=params,
        name="cross_turn",
    )(stay, cross)
    back = beside if slabs == 2 else beside[::-1]
    edges = [lax.ppermute(x, "slab", p) for x, p in zip(edges, back)]
    edges, coarse = lax.optimization_barrier((edges, coarse))
    mate, home = pl.pallas_call(
        slab_turn_kernel,
        out_shape=(
            jax.ShapeDtypeStruct((channels // TILE, TILE, LANES), BF16),
            jax.ShapeDtypeStruct((channels, RIM), F32),
        ),
        compiler_params=params,
        name="slab_turn",
    )(mate, home, *edges)
    got = [lax.ppermute(total, SPLIT, route) for route in routes[::-1]]
    mine = pl.pallas_call(
        functools.partial(join_kernel, orders[::-1]),
        out_shape=jax.ShapeDtypeStruct((size + mate.shape[0], TILE, LANES), BF16),
        in_specs=[smem, smem] + [vmem] * (squares + 1),
        compiler_params=params,
        name="join",
    )(core, here, total, *got, mate)
    other = lax.ppermute(mine, "core", swap)
    conv_wgrad_t, down_wgrad, grad_input_t = pl.pallas_call(
        functools.partial(final_kernel, taps, size),
        out_shape=(
            jax.ShapeDtypeStruct((channels, conv_columns), F32),
            jax.ShapeDtypeStruct((taps * channels, LANES), F32),
            jax.ShapeDtypeStruct((channels, voxels), F32),
        ),
        in_specs=[smem] + [vmem] * 4,
        compiler_params=params,
        name="final",
    )(core, mine, other, base, home)
    return coarse, grad_input_t.T, conv_wgrad_t.T, down_wgrad


def solution(mesh):
    regions, slabs = mesh.shape["region"], mesh.shape["slab"]
    fine = Mesh(mesh.devices.reshape(regions // 4, 2, 2, slabs), SPLIT)
    split = P(SPLIT, None)
    return jax.shard_map(
        on_device,
        mesh=fine,
        in_specs=(split, split, split, P(), P(), split),
        out_specs=(split, split, P(), P()),
        check_vma=False,
    )
```

```python
import functools

import jax
import jax.numpy as jnp
from jax import lax
from jax.experimental import pallas as pl
from jax.experimental.pallas import tpu as pltpu
from jax.sharding import Mesh, PartitionSpec as P

SPLIT = ("far", "near", "core", "slab")
RING = ("far", "near", "core")
RIM = 64
LANES = 128
TILE = 16
F32 = jnp.float32
BF16 = jnp.bfloat16
NN = (((1,), (0,)), ((), ()))
NT = (((1,), (1,)), ((), ()))
VMEM_BYTES = 20 * 2**20


def mm(a, b, dims=NN):
    return lax.dot_general(a, b, dims, preferred_element_type=F32)


def table_lanes(neighbours, voxels, slabs, core):
    code = neighbours // voxels
    slot = neighbours - code * voxels
    row = code // 3
    col = code - row * 3
    if slabs == 2:
        rims = 2
        place = jnp.where(col == 1, 0, 1)
        beside = 0
    else:
        rims = 3
        place = col
        beside = col // 2
    group = jnp.abs(row // 2 + core - 1)
    rim = jnp.where(row == 1, 2 * rims + beside, group * rims + place)
    lane = jnp.where(code == 4, slot, voxels + rim * RIM + slot)
    return jnp.where(code > 8, -1, lane)


def payload_tiles(channels, conv_columns, taps):
    tiles = []
    for column in range(0, conv_columns, LANES):
        for row in range(0, channels, TILE):
            tiles.append((0, row, column, min(LANES, conv_columns - column)))
    for row in range(0, taps * channels, TILE):
        tiles.append((1, row, 0, LANES))
    return tiles


def padded_halo(halo_refs):
    halo = [h[...] for h in halo_refs]
    width = sum(h.shape[1] for h in halo)
    slack = -width % LANES
    if slack:
        halo.append(jnp.zeros((halo[0].shape[0], slack), BF16))
    return jnp.concatenate(halo, axis=1)


def gather_kernel(slabs, f_ref, near_ref, first_ref, rest_ref):
    channels, voxels = f_ref.shape
    table_t = f_ref[...]
    lanes = table_lanes(near_ref[...], voxels, slabs, 0)
    near_iota = lax.broadcasted_iota(jnp.int32, (voxels, voxels), 0)
    for o in range(near_ref.shape[0]):
        near = jnp.where(near_iota == lanes[o : o + 1, :], 1.0, 0.0).astype(BF16)
        own = mm(table_t, near).astype(BF16)
        first_ref[o * channels : (o + 1) * channels, :] = own[:, :LANES]
        rest_ref[o * channels : (o + 1) * channels, :] = own[:, LANES:]


def taps_kernel(down_ref, cgrad_ref, wd_ref, pick_ref, hgrad_ref):
    channels, voxels = hgrad_ref.shape
    taps, coarse_count = down_ref.shape
    cgrad_t = cgrad_ref[...].astype(F32).T.astype(BF16)
    down = down_ref[...].astype(F32).T
    lane_iota = lax.broadcasted_iota(jnp.int32, (coarse_count, voxels), 1).astype(F32)
    hgrad_t = jnp.zeros((channels, voxels), F32)
    for t in range(taps):
        pick = jnp.where(lane_iota == down[:, t : t + 1], 1.0, 0.0).astype(BF16)
        pick_ref[t] = pick
        wd = wd_ref[t * channels : (t + 1) * channels, :]
        hgrad_t += mm(wd, mm(cgrad_t, pick).astype(BF16))
    hgrad_ref[...] = hgrad_t


def far_one_hots(lanes, rows, voxels, offsets):
    iota = lax.broadcasted_iota(jnp.int32, (rows, LANES), 0) + voxels
    hots = [jnp.where(iota == lanes[o : o + 1, :LANES], 1.0, 0.0).astype(BF16) for o in offsets]
    return jnp.concatenate(hots, axis=1)


def forward_kernel(slabs, core_ref, f_ref, near_ref, cgrad_ref, w_ref, *refs):
    first_ref, rest_ref, pick_ref, hgrad_ref = refs[:4]
    halo_refs, refs = (refs[4:7], refs[7:]) if slabs == 2 else (refs[4:8], refs[8:])
    grad_ref, hidden_ref, keep_ref, send_ref, rt, conv_w, down_w = refs
    channels, voxels = f_ref.shape
    offsets = near_ref.shape[0]
    taps = pick_ref.shape[0]
    conv_columns = offsets * channels
    halo_t = padded_halo(halo_refs)
    lanes = table_lanes(near_ref[:, :LANES], voxels, slabs, core_ref[0])
    pack = 2 * LANES // RIM
    iota = lax.broadcasted_iota(jnp.int32, (halo_t.shape[1], 2 * LANES), 0) + voxels
    empty = jnp.zeros((channels, LANES - RIM), F32)
    for start in range(0, offsets, pack):
        group = [lanes[min(o, offsets - 1) : min(o, offsets - 1) + 1, :RIM] for o in range(start, start + pack)]
        hot = jnp.where(iota == jnp.concatenate(group, axis=1), 1.0, 0.0).astype(BF16)
        away = mm(halo_t, hot)
        for i, o in enumerate(range(start, min(start + pack, offsets))):
            rows = slice(o * channels, (o + 1) * channels)
            part = jnp.concatenate([away[:, i * RIM : (i + 1) * RIM], empty], axis=1)
            rt[rows, :LANES] = (first_ref[rows, :].astype(F32) + part).astype(BF16)
            rt[rows, LANES:] = rest_ref[rows, :]

    out_t = mm(w_ref[...], rt[...])
    sig = 1.0 / (1.0 + jnp.exp(-out_t))
    hidden_t = (f_ref[...].astype(F32) + out_t * sig).astype(BF16)
    grad_t = (hgrad_ref[...] * sig * (1.0 + out_t * (1.0 - sig))).astype(BF16)
    grad_ref[...] = grad_t
    conv_w[:, :conv_columns] = mm(grad_t, rt[...], NT)
    if conv_w.shape[1] > conv_columns:
        slack = conv_w.shape[1] - conv_columns
        conv_w[:, conv_columns:] = jnp.zeros((channels, slack), F32)

    hidden_ref[...] = hidden_t
    cgrad = cgrad_ref[...]
    for t in range(taps):
        picked_t = mm(hidden_t, pick_ref[t], NT).astype(BF16)
        down_w[t * channels : (t + 1) * channels, :] = mm(picked_t, cgrad)

    tiles = payload_tiles(channels, conv_columns, taps)
    size = keep_ref.shape[0]
    for core in range(2):

        @pl.when(core_ref[0] == core)
        def _(core=core):
            for i in range(2 * size):
                ref = keep_ref if i // size == core else send_ref
                if i < len(tiles):
                    kind, row, column, _ = tiles[i]
                    source = down_w if kind else conv_w
                    value = source[row : row + TILE, column : column + LANES]
                else:
                    value = jnp.zeros((TILE, LANES), F32)
                ref[i % size] = value.astype(ref.dtype)


def coarse_kernel(pick_ref, hidden_ref, wd_ref, coarse_ref):
    channels = hidden_ref.shape[0]
    coarse = jnp.zeros(coarse_ref.shape, F32)
    for t in range(pick_ref.shape[0]):
        picked = mm(pick_ref[t], hidden_ref[...], NT).astype(BF16)
        coarse += mm(picked, wd_ref[t * channels : (t + 1) * channels, :])
    coarse_ref[...] = coarse.astype(BF16)


def backward_kernel(slabs, core_ref, near_ref, hgrad_ref, grad_ref, w_ref, *refs):
    base_ref, mate_ref, beside_ref, cross_ref, drt, drt_far, hot, far, w_back = refs
    channels, voxels = hgrad_ref.shape
    offsets = near_ref.shape[0]
    lanes = table_lanes(near_ref[...], voxels, slabs, core_ref[0])
    near_iota = lax.broadcasted_iota(jnp.int32, (voxels, voxels), 0)
    w_back[:, :channels] = w_ref[...].astype(F32).T.astype(BF16)
    w_back[:, channels:] = jnp.zeros((offsets * channels, LANES - channels), BF16)
    slack = jnp.zeros((LANES - channels, voxels), BF16)
    grad_pad = jnp.concatenate([grad_ref[...], slack], axis=0)
    for o in range(offsets):
        near = jnp.where(near_iota == lanes[o : o + 1, :], 1.0, 0.0).astype(BF16)
        hot[:, o * voxels : (o + 1) * voxels] = near
        spread = mm(w_back[o * channels : (o + 1) * channels, :], grad_pad).astype(BF16)
        drt[:, o * voxels : (o + 1) * voxels] = spread
        drt_far[:, o * LANES : (o + 1) * LANES] = spread[:, :LANES]
        far[:, o * LANES : (o + 1) * LANES] = far_one_hots(lanes, far.shape[0], voxels, (o,))
    base_ref[...] = hgrad_ref[...] + mm(drt[...], hot[...], NT)
    back_t = mm(drt_far[...], far[...], NT)
    rims = 2 if slabs == 2 else 3
    rim = [back_t[:, i * RIM : (i + 1) * RIM] for i in range(3 * rims - 1)]
    mate, cross, side = rim[:rims], rim[rims : 2 * rims], rim[2 * rims :]
    own, away = (0, (1,)) if slabs == 2 else (1, (0, 2))
    mate_ref[...] = mate[own]
    parts = []
    for place, part in zip(away, side):
        parts += [mate[place], part]
    beside_ref[...] = jnp.concatenate(parts, axis=1)
    cross_ref[...] = jnp.concatenate(cross, axis=1).astype(BF16)


def cross_turn_kernel(own, beside_ref, got_ref, home_ref, *edge_refs):
    got = got_ref[...].astype(F32)
    rim = [got[:, i * RIM : (i + 1) * RIM] for i in range(got.shape[1] // RIM)]
    home_ref[...] = rim.pop(own)
    for i, (ref, part) in enumerate(zip(edge_refs, rim)):
        mine = beside_ref[:, 2 * i * RIM : 2 * (i + 1) * RIM]
        ref[...] = (mine + jnp.concatenate([jnp.zeros_like(part), part], axis=1)).astype(BF16)


def slab_turn_kernel(mate_ref, home_ref, *refs):
    got_refs, (rider_ref, sum_ref) = refs[:-2], refs[-2:]
    got = got_refs[0][...].astype(F32)
    for ref in got_refs[1:]:
        got += ref[...].astype(F32)
    mate = mate_ref[...] + got[:, :RIM]
    sum_ref[...] = home_ref[...] + got[:, RIM:]
    pair = jnp.concatenate([mate, jnp.zeros_like(mate)], axis=1).astype(BF16)
    for i in range(rider_ref.shape[0]):
        rider_ref[i] = pair[i * TILE : (i + 1) * TILE, :]


def step_of(steps, core):
    return jnp.where(core == 0, *steps)


def split_kernel(orders, core_ref, here_ref, own_ref, got_ref, *piece_refs):
    length = piece_refs[0].shape[0]
    for ref, steps in zip(piece_refs, ((0, 0),) + orders):
        rows = pl.ds((here_ref[0] ^ step_of(steps, core_ref[0])) * length, length)
        ref[...] = (own_ref[rows] + got_ref[rows].astype(F32)).astype(ref.dtype)


def join_kernel(orders, core_ref, here_ref, *refs):
    piece_refs, rider_ref, full_ref = refs[:-2], refs[-2], refs[-1]
    length = piece_refs[0].shape[0]
    for ref, steps in zip(piece_refs, ((0, 0),) + orders):
        place = here_ref[0] ^ step_of(steps, core_ref[0])
        full_ref[pl.ds(place * length, length)] = ref[...]
    full_ref[len(piece_refs) * length :] = rider_ref[...]


def final_kernel(taps, size, core_ref, mine_ref, other_ref, *refs):
    base_ref, home_ref, conv_ref, down_ref, grad_ref = refs
    channels, conv_columns = conv_ref.shape
    grad_ref[:, RIM:] = base_ref[:, RIM:]
    for i in range(channels // TILE):
        rows = slice(i * TILE, (i + 1) * TILE)
        total = base_ref[rows, :RIM] + home_ref[rows, :]
        grad_ref[rows, :RIM] = total + other_ref[size + i][:, :RIM].astype(F32)
    for core in range(2):

        @pl.when(core_ref[0] == core)
        def _(core=core):
            for i, tile in enumerate(payload_tiles(channels, conv_columns, taps)):
                kind, row, column, columns = tile
                source = mine_ref if i // size == core else other_ref
                value = source[i % size].astype(F32)
                target = down_ref if kind else conv_ref
                target[row : row + TILE, column : column + columns] = value[:, :columns]


def shifts(count, step):
    return [(i, i + step) for i in range(count) if 0 <= i + step < count]


def chip_pairs(regions):
    mates = [(i, i ^ 1) for i in range(regions)]
    cross = [(i, i + 1) for i in range(1, regions - 1, 2)]
    return mates, cross + [(b, a) for a, b in cross]


def around_orders(nears, slabs):
    count = nears * slabs
    if count == 4:
        return ((3, 3), (2, 1), (1, 2))
    return tuple((i, i) for i in range(count - 1, 0, -1))


def around_pairs(sizes, steps):
    pairs = []
    slabs = sizes["slab"]
    for far in range(sizes["far"]):
        for here in range(sizes["near"] * slabs):
            for core in range(2):
                spots = []
                for spot in (here, here ^ steps[core]):
                    near, slab = divmod(spot, slabs)
                    spots.append(((far * sizes["near"] + near) * 2 + core) * slabs + slab)
                pairs.append(tuple(spots))
    return pairs


def on_device(features, neighbours, down_map, w_conv, w_down, coarse_grad):
    sizes = {axis: lax.axis_size(axis) for axis in SPLIT}
    regions, slabs = sizes["far"] * sizes["near"] * sizes["core"], sizes["slab"]
    voxels, channels = features.shape
    offsets, taps = neighbours.shape[1], down_map.shape[1]
    conv_columns = offsets * channels
    core = lax.axis_index("core").astype(jnp.int32).reshape(1)
    swap = [(0, 1), (1, 0)]
    mates, crossings = chip_pairs(regions)
    here = lax.axis_index(("near", "slab")).astype(jnp.int32).reshape(1)
    orders = around_orders(sizes["near"], slabs)
    routes = [around_pairs(sizes, steps) for steps in orders]
    squares = len(orders) + 1

    smem = pl.BlockSpec(memory_space=pltpu.SMEM)
    vmem = pl.BlockSpec(memory_space=pltpu.VMEM)
    params = pltpu.CompilerParams(vmem_limit_bytes=VMEM_BYTES)
    light = pl.CostEstimate(flops=2 * 10**9, bytes_accessed=10**7, transcendentals=0)
    features_t, neighbours_t, w_conv_t = features.T, neighbours.T, w_conv.T
    rim = features_t[:, :RIM]
    if slabs == 2:
        beside = [swap]
    else:
        beside = [shifts(slabs, 1), shifts(slabs, -1)]
    side = [lax.ppermute(features_t, "slab", pairs) for pairs in beside]
    own = pl.pallas_call(
        functools.partial(gather_kernel, slabs),
        out_shape=(
            jax.ShapeDtypeStruct((conv_columns, LANES), BF16),
            jax.ShapeDtypeStruct((conv_columns, voxels - LANES), BF16),
        ),
        compiler_params=params,
        cost_estimate=light,
        name="gather",
    )(features_t, neighbours_t)
    side, own = lax.optimization_barrier((side, own))
    side = [x[:, :RIM] for x in side]
    row = [rim, side[0]] if slabs == 2 else [side[0], rim, side[1]]
    row = jnp.concatenate(row, axis=1)
    cross = lax.ppermute(row, RING, crossings)
    row, down_t = lax.optimization_barrier((row, down_map.T))
    pick, hgrad = pl.pallas_call(
        taps_kernel,
        out_shape=(
            jax.ShapeDtypeStruct((taps, coarse_grad.shape[0], voxels), BF16),
            jax.ShapeDtypeStruct((channels, voxels), F32),
        ),
        compiler_params=params,
        cost_estimate=light,
        name="taps",
    )(down_t, coarse_grad, w_down)
    row, pick, hgrad = lax.optimization_barrier((row, pick, hgrad))
    mate = lax.ppermute(row, RING, mates)
    halos = [mate, cross, *side]
    far_rows = -(-sum(x.shape[1] for x in halos) // LANES) * LANES

    tiles = len(payload_tiles(channels, conv_columns, taps))
    size = -(-tiles // (2 * squares)) * squares
    grad, hidden, keep, send = pl.pallas_call(
        functools.partial(forward_kernel, slabs),
        out_shape=(
            jax.ShapeDtypeStruct((channels, voxels), BF16),
            jax.ShapeDtypeStruct((channels, voxels), BF16),
            jax.ShapeDtypeStruct((size, TILE, LANES), F32),
            jax.ShapeDtypeStruct((size, TILE, LANES), BF16),
        ),
        in_specs=[smem] + [vmem] * (8 + len(halos)),
        scratch_shapes=[
            pltpu.VMEM((conv_columns, voxels), BF16),
            pltpu.VMEM((channels, -(-conv_columns // LANES) * LANES), F32),
            pltpu.VMEM((taps * channels, LANES), F32),
        ],
        compiler_params=params,
        name="forward",
    )(core, features_t, neighbours_t, coarse_grad, w_conv_t, *own, pick, hgrad, *halos)

    got = lax.ppermute(send, "core", swap)
    piece = size // squares
    keep, *sent = pl.pallas_call(
        functools.partial(split_kernel, orders),
        out_shape=[
            jax.ShapeDtypeStruct((piece, TILE, LANES), BF16 if i else F32) for i in range(squares)
        ],
        in_specs=[smem, smem, vmem, vmem],
        compiler_params=params,
        name="split",
    )(core, here, keep, got)
    sent, grad = lax.optimization_barrier((sent, grad))
    got = [lax.ppermute(x, SPLIT, route) for x, route in zip(sent, routes)]
    base, mate, stay, cross = pl.pallas_call(
        functools.partial(backward_kernel, slabs),
        out_shape=(
            jax.ShapeDtypeStruct((channels, voxels), F32),
            jax.ShapeDtypeStruct((channels, RIM), F32),
            jax.ShapeDtypeStruct((channels, 2 * len(beside) * RIM), F32),
            jax.ShapeDtypeStruct((channels, row.shape[1]), BF16),
        ),
        in_specs=[smem] + [vmem] * 4,
        scratch_shapes=[
            pltpu.VMEM((channels, offsets * voxels), BF16),
            pltpu.VMEM((channels, offsets * LANES), BF16),
            pltpu.VMEM((voxels, offsets * voxels), BF16),
            pltpu.VMEM((far_rows, offsets * LANES), BF16),
            pltpu.VMEM((conv_columns, LANES), BF16),
        ],
        compiler_params=params,
        cost_estimate=light,
        name="backward",
    )(core, neighbours_t, hgrad, grad, w_conv_t)
    got, cross, base = lax.optimization_barrier((got, cross, base))
    coarse = pl.pallas_call(
        coarse_kernel,
        out_shape=jax.ShapeDtypeStruct(coarse_grad.shape, BF16),
        compiler_params=params,
        cost_estimate=light,
        name="coarse",
    )(pick, hidden, w_down)
    total = functools.reduce(lambda x, y: x + y.astype(F32), got, keep).astype(BF16)
    late, coarse = lax.optimization_barrier((total, coarse))
    parts = [total]
    for step in range(1, sizes["far"]):
        sent = late if step == 1 else total
        parts.append(lax.ppermute(sent, "far", [(i, i ^ step) for i in range(sizes["far"])]))
    cross = lax.ppermute(cross, RING, crossings)
    parts = [x.astype(F32) for x in parts]
    blocks, start = [], 2
    while start < len(parts):
        block = parts[start : 2 * start]
        while len(block) > 1:
            block = [x + y for x, y in zip(block[0::2], block[1::2])]
        blocks += block
        start *= 2
    blocks, cross = lax.optimization_barrier((blocks, cross))
    total = sum(parts[1:2] + blocks, parts[0]).astype(BF16)
    home, *edges = pl.pallas_call(
        functools.partial(cross_turn_kernel, 0 if slabs == 2 else 1),
        out_shape=[jax.ShapeDtypeStruct((channels, RIM), F32)]
        + [jax.ShapeDtypeStruct((channels, 2 * RIM), BF16)] * len(beside),
        compiler_params=params,
        name="cross_turn",
    )(stay, cross)
    back = beside if slabs == 2 else beside[::-1]
    edges = [lax.ppermute(x, "slab", p) for x, p in zip(edges, back)]
    mate, home = pl.pallas_call(
        slab_turn_kernel,
        out_shape=(
            jax.ShapeDtypeStruct((channels // TILE, TILE, LANES), BF16),
            jax.ShapeDtypeStruct((channels, RIM), F32),
        ),
        compiler_params=params,
        name="slab_turn",
    )(mate, home, *edges)
    got = [lax.ppermute(total, SPLIT, route) for route in routes[::-1]]
    mine = pl.pallas_call(
        functools.partial(join_kernel, orders[::-1]),
        out_shape=jax.ShapeDtypeStruct((size + mate.shape[0], TILE, LANES), BF16),
        in_specs=[smem, smem] + [vmem] * (squares + 1),
        compiler_params=params,
        name="join",
    )(core, here, total, *got, mate)
    other = lax.ppermute(mine, "core", swap)
    conv_wgrad_t, down_wgrad, grad_input_t = pl.pallas_call(
        functools.partial(final_kernel, taps, size),
        out_shape=(
            jax.ShapeDtypeStruct((channels, conv_columns), F32),
            jax.ShapeDtypeStruct((taps * channels, LANES), F32),
            jax.ShapeDtypeStruct((channels, voxels), F32),
        ),
        in_specs=[smem] + [vmem] * 4,
        compiler_params=params,
        name="final",
    )(core, mine, other, base, home)
    return coarse, grad_input_t.T, conv_wgrad_t.T, down_wgrad


def solution(mesh):
    regions, slabs = mesh.shape["region"], mesh.shape["slab"]
    fine = Mesh(mesh.devices.reshape(regions // 4, 2, 2, slabs), SPLIT)
    split = P(SPLIT, None)
    return jax.shard_map(
        on_device,
        mesh=fine,
        in_specs=(split, split, split, P(), P(), split),
        out_specs=(split, split, P(), P()),
        check_vma=False,
    )
```
